32 devices in a mesh: group: 4 (over z), tensor: 8 (over y, x, core).
Axes of the slice: x: 2, y: 2, z: 4, core: 2. Of those that a mesh axis runs over, the one named last changes fastest.
Arguments:
- residual_in: bfloat16 [1024, 2048], P(('group', 'tensor')), parts along dimension 0, may hold values from -22 to 22
- attn_gain: float32 [2048], replicated, may hold values from 0.5 to 1.5
- w_query: bfloat16 [2048, 4096], P(None, 'tensor'), may hold values from -0.125 to 0.125
- w_keyval: bfloat16 [1024, 2048], P('tensor'), may hold values from -0.125 to 0.125
- query_gain: float32 [128], replicated, may hold values from 0.1 to 1.9
- key_gain: float32 [128], replicated, may hold values from 0.1 to 1.9
- w_out: bfloat16 [4096, 2048], P('tensor'), may hold values from -0.09375 to 0.09375
- ffn_gain: float32 [2048], replicated, may hold values from 0.5 to 1.5
- w_gate: bfloat16 [8, 768, 2048], P('tensor'), may hold values from -0.125 to 0.125
- w_up: bfloat16 [8, 768, 2048], P('tensor'), may hold values from -0.125 to 0.125
- w_down: bfloat16 [8, 768, 2048], P('tensor'), may hold values from -0.21875 to 0.21875
- key_cache: bfloat16 [32, 1024, 512], P(('group', 'tensor')), parts along dimension 0, may hold values from -110 to 110
- value_cache: bfloat16 [32, 1024, 512], P(('group', 'tensor')), parts along dimension 0, may hold values from -18 to 18
- prefix_lens: int32 [32], P(('group', 'tensor')), parts along dimension 0, may hold values from 1 to 992
- accepted: int32 [32], P(('group', 'tensor')), parts along dimension 0, may hold values from 1 to 8
- accept_path: int32 [32, 8], P(('group', 'tensor')), parts along dimension 0, may hold values from 0 to 14, as said below
- parents: int32 [32, 32], P(('group', 'tensor')), parts along dimension 0, may hold values from -1 to 30, as said below
- slot_kinds: int32 [32], P(('group', 'tensor')), parts along dimension 0, may hold values from 0 to 1
- expert_ids: int32 [1024, 8], P('group'), parts along dimension 0, may hold values from 0 to 127, as said below
- gate_probs: float32 [1024, 8], P('group'), parts along dimension 0, may hold values from 0.1 to 1
Outputs:
- mixed: bfloat16 [1024, 2048], P(('group', 'tensor')), parts along dimension 0
The draws below stay inside these ranges and needn't reach their ends.
There are 4 independent parts, one for each index of `group`. The reference program is written for one: setup_inputs(seed, part) draws one part's arguments, and reference() takes and returns one part's arrays. A program takes and returns all parts, laid end to end along the dimension named above; an argument that names none is the same for every part. Nothing has to cross between parts.
Inputs may be any that keep to these rules, and one draw needn't show every extreme that they name: `expert_ids`: the tokens of each slot name each of the 128 experts exactly 32 * 8 // 128 times; a token never names one expert twice. `accept_path`: each row starts at 0 and rises by 1 or 2 from one entry to the next. `parents`: node 0 of every slot has parent -1; every other node's parent is an earlier node of the same slot.
All inputs are finite; a program needn't handle non-finite values.
Results may differ from the reference program's by a relative error of at most 0.02.
Values may be sent and summed in bfloat16 or wider, within the bound.
No kernel may reach another device: no remote copies, remote signals or barrier semaphores. Data moves between devices by JAX's collectives and lax.ppermute only.
A program may use at most 128 MiB of HBM per device.

```python
import math
import jax
import jax.numpy as jnp
from jax import lax

D = 2048
HQ = 32
KVH = 4
HD = 128
FF = 768
EXPERTS = 128
TOPK = 8
NEW = 32
CACHE = 1024
ACC = 8
SINK = 4
WIN = 512
SLOTS = 8
TOK = 256
EXP_WIN = 8
PER = 2


def draw_residual_in(key, part):
    key_base, key_rows, key_cols = jax.random.split(jax.random.fold_in(key, 11), 3)
    base_draw = jax.random.truncated_normal(key_base, -6.0, 6.0, (TOK, D), jnp.float32)
    row_scale = jnp.exp(jax.random.uniform(key_rows, (TOK, 1), jnp.float32, math.log(0.3), math.log(3.0)))
    col_scale = jnp.exp(jax.random.uniform(key_cols, (1, D), jnp.float32, math.log(0.5), math.log(2.0)))
    return (0.6 * base_draw * row_scale * col_scale).astype(jnp.bfloat16)


def draw_key_cache(key, part):
    key_base = jax.random.fold_in(jax.random.fold_in(key, 23), 0)
    shape_all = (SLOTS, CACHE, KVH * HD)
    base_draw = jax.random.truncated_normal(key_base, -6.0, 6.0, shape_all, jnp.float32)
    return base_draw.astype(jnp.bfloat16)


def draw_prefix_lens(key, part):
    key_first, key_second, key_pick = jax.random.split(jax.random.fold_in(key, 37), 3)
    span_rows = CACHE - NEW
    first_draw = jax.random.randint(key_first, (SLOTS,), 0, span_rows)
    second_draw = jax.random.randint(key_second, (SLOTS,), 0, span_rows)
    lengths = 1 + first_draw * second_draw // max(span_rows - 1, 1)
    chosen_slot = jax.random.randint(key_pick, (), 0, SLOTS)
    return jnp.where(jnp.arange(SLOTS) == chosen_slot, span_rows, lengths).astype(jnp.int32)


def draw_accepted(key, part):
    counts_drawn = jax.random.randint(jax.random.fold_in(key, 41), (SLOTS,), 1, ACC + 1)
    return counts_drawn.at[SLOTS - 1].set(ACC).astype(jnp.int32)


def draw_accept_path(key, part):
    step_sizes = jax.random.randint(jax.random.fold_in(key, 53), (SLOTS, ACC), 1, 3)
    step_sizes = step_sizes.at[0].set(2)
    step_sizes = step_sizes.at[:, 0].set(0)
    return jnp.cumsum(step_sizes, axis=1).astype(jnp.int32)


def draw_parents(key, part):
    raw_draw = jax.random.randint(jax.random.fold_in(key, 67), (SLOTS, NEW), 0, 1 << 20)
    node_index = jnp.arange(NEW, dtype=jnp.int32)[None, :]
    picked = raw_draw % jnp.maximum(node_index, 1)
    picked = jnp.where(node_index == 0, -1, picked)
    return picked.at[0, NEW - 1].set(NEW - 2).astype(jnp.int32)


def draw_expert_ids(key, part):
    slot_keys = jax.random.split(jax.random.fold_in(key, 79), SLOTS)

    def one_order(slot_key):
        return jax.random.permutation(slot_key, EXPERTS)
    orders = jax.vmap(one_order)(slot_keys)
    tiled = jnp.tile(orders, (1, NEW * TOPK // EXPERTS))
    return tiled.reshape(SLOTS * NEW, TOPK).astype(jnp.int32)


def plant(values, stream_key, smallest, largest):
    longest = values.shape.index(max(values.shape))
    spots = []
    for shift in (0, 1):
        where = [jax.random.randint(jax.random.fold_in(stream_key, axis), (), 0, length) for axis, length in enumerate(values.shape)]
        where[longest] = (where[longest] + shift) % values.shape[longest]
        spots.append(tuple(where))
    return values.at[spots[0]].set(smallest).at[spots[1]].set(largest)


def levels(key, shape, cuts, least, high):
    def one(dim, parts):
        heights = jax.random.uniform(jax.random.fold_in(jax.random.fold_in(key, 6), dim), (parts,), jnp.float32, least / len(cuts), high / len(cuts))
        return jnp.repeat(jnp.exp(heights), shape[dim] // parts).reshape((-1,) + (1,) * (len(shape) - dim - 1))

    gain = one(*cuts[0])
    for cut in cuts[1:]:
        gain = gain * one(*cut)
    return gain


def centred(rng, extent, width, limit, cuts=(), kind=jnp.bfloat16):
    values = width * jax.random.normal(rng, extent, jnp.float32)
    if cuts:
        values = values * levels(rng, extent, cuts, -0.22, 0.18)
    return jnp.clip(values, -limit, limit).astype(kind)


def setup_inputs(seed: int = 0, part: int = 0) -> dict:
    arg_keys = jax.random.split(jax.random.key(seed), 21)
    own_keys = jax.random.split(jax.random.fold_in(arg_keys[20], part), 21)
    return {
        "residual_in": draw_residual_in(jax.random.fold_in(jax.random.fold_in(arg_keys[20], part), 71), part),
        "attn_gain": jnp.clip(1.0 + 0.1 * jax.random.normal(arg_keys[1], (D,), jnp.float32), 0.5, 1.5),
        "w_query": centred(arg_keys[2], (D, HQ * HD), D ** -0.5, 0.125, ((1, 8),)),
        "w_keyval": centred(arg_keys[3], (2 * KVH * HD, D), D ** -0.5, 0.125, ((0, 8),)),
        "query_gain": jnp.clip(1.0 + 0.18 * jax.random.normal(arg_keys[4], (HD,), jnp.float32), 0.1, 1.9),
        "key_gain": jnp.clip(1.0 + 0.18 * jax.random.normal(arg_keys[5], (HD,), jnp.float32), 0.1, 1.9),
        "w_out": centred(arg_keys[6], (HQ * HD, D), (HQ * HD) ** -0.5, 0.09375, ((0, 8),)),
        "ffn_gain": jnp.clip(1.0 + 0.1 * jax.random.normal(arg_keys[7], (D,), jnp.float32), 0.5, 1.5),
        "w_gate": centred(arg_keys[8], (EXP_WIN, FF, D), D ** -0.5, 0.125, ((0, 8),)),
        "w_up": centred(arg_keys[9], (EXP_WIN, FF, D), D ** -0.5, 0.125, ((0, 8),)),
        "w_down": centred(arg_keys[10], (EXP_WIN, FF, D), FF ** -0.5, 0.21875, ((0, 8),)),
        "key_cache": draw_key_cache(jax.random.fold_in(jax.random.fold_in(arg_keys[20], part), 71), part),
        "value_cache": centred(own_keys[12], (SLOTS, CACHE, KVH * HD), 3.0, 18.0, ((0, 8),)),
        "prefix_lens": draw_prefix_lens(jax.random.fold_in(jax.random.fold_in(arg_keys[20], part), 71), part),
        "accepted": draw_accepted(jax.random.fold_in(jax.random.fold_in(arg_keys[20], part), 71), part),
        "accept_path": draw_accept_path(jax.random.fold_in(jax.random.fold_in(arg_keys[20], part), 71), part),
        "parents": draw_parents(jax.random.fold_in(jax.random.fold_in(arg_keys[20], part), 71), part),
        "slot_kinds": plant(jax.random.randint(own_keys[17], (SLOTS,), 0, 2), jax.random.fold_in(own_keys[17], 1), 0, 1).astype(jnp.int32),
        "expert_ids": draw_expert_ids(jax.random.fold_in(jax.random.fold_in(arg_keys[20], part), 71), part),
        "gate_probs": jnp.clip(jax.random.uniform(own_keys[19], (TOK, TOPK), jnp.float32, 0.1, 1.0), 0.1, 1.0),
    }


EPSILON = 1e-06
NEG_FILL = -1e+30
ROPE_BASE = 1000000.0

def rms_rows(values, weight_gain):
    return values * lax.rsqrt(lax.optimization_barrier(jnp.mean(values * values, axis=-1, keepdims=True)) + EPSILON) * weight_gain

def rotate(values, angles):
    half_dim = values.shape[-1] // 2
    cosine = jnp.cos(angles)[:, None, :]
    sine_val = jnp.sin(angles)[:, None, :]
    lower_half = values[..., :half_dim]
    upper_half = values[..., half_dim:]
    return jnp.concatenate([lower_half * cosine - upper_half * sine_val, upper_half * cosine + lower_half * sine_val], axis=-1)

def ancestors(parent_row, count_new):
    parent_link = jax.nn.one_hot(parent_row, count_new, dtype=jnp.float32)
    reach_mat = jnp.eye(count_new, dtype=jnp.float32) + parent_link
    for unused in range((count_new - 1).bit_length()):
        reach_mat = jnp.minimum(jnp.dot(reach_mat, reach_mat, precision=lax.Precision.HIGHEST), 1.0)
    return reach_mat

def attend(query_raw, keyval_raw, key_cache, value_cache, prefix_len, accepted_len, path_row, parent_row, kind_value, query_gain, key_gain):
    count_new = query_raw.shape[0]
    head_dim = query_gain.shape[0]
    kv_heads = key_cache.shape[-1] // head_dim
    q_heads = query_raw.shape[-1] // head_dim
    group_size = q_heads // kv_heads
    cache_len = key_cache.shape[0]
    acc_count = path_row.shape[0]
    total_len = prefix_len + accepted_len
    reach_mat = ancestors(parent_row, count_new)
    index_row = jnp.arange(count_new)
    causal = (index_row[None, :] <= index_row[:, None]).astype(jnp.float32)
    is_tree = kind_value == 1
    allowed = jnp.where(is_tree, reach_mat, causal) > 0.5
    depth_used = jnp.where(is_tree, lax.optimization_barrier(jnp.sum(reach_mat, axis=1)) - 1.0, index_row.astype(jnp.float32))
    position = total_len.astype(jnp.float32) + depth_used
    half_dim = head_dim // 2
    freq_table = jnp.exp(-(2.0 * jnp.arange(half_dim, dtype=jnp.float32) / head_dim) * math.log(ROPE_BASE))
    angles = position[:, None] * freq_table[None, :]
    query_rot = rotate(rms_rows(query_raw.astype(jnp.float32).reshape(count_new, q_heads, head_dim), query_gain), angles).astype(jnp.bfloat16)
    key_width = kv_heads * head_dim
    key_new = rotate(rms_rows(keyval_raw[:, :key_width].astype(jnp.float32).reshape(count_new, kv_heads, head_dim), key_gain), angles).astype(jnp.bfloat16)
    value_new = keyval_raw[:, key_width:].reshape(count_new, kv_heads, head_dim)
    acc_rows = (prefix_len + path_row).astype(jnp.int32)
    key_acc = jnp.take(key_cache, acc_rows, axis=0).reshape(acc_count, kv_heads, head_dim)
    value_acc = jnp.take(value_cache, acc_rows, axis=0).reshape(acc_count, kv_heads, head_dim)
    cache_pos = jnp.arange(cache_len)
    seen_old = (cache_pos < prefix_len) & ((cache_pos < SINK) | (cache_pos >= total_len - WIN))
    acc_index = jnp.arange(acc_count)
    acc_pos = prefix_len + acc_index
    seen_acc = (acc_index < accepted_len) & ((acc_pos < SINK) | (acc_pos >= total_len - WIN))
    keys_all = jnp.concatenate([key_cache.reshape(cache_len, kv_heads, head_dim), key_acc, key_new], axis=0)
    values_all = jnp.concatenate([value_cache.reshape(cache_len, kv_heads, head_dim), value_acc, value_new], axis=0)
    seen_all = jnp.concatenate([jnp.broadcast_to(seen_old[None, :], (count_new, cache_len)), jnp.broadcast_to(seen_acc[None, :], (count_new, acc_count)), allowed], axis=1)
    query_group = query_rot.astype(jnp.float32).reshape(count_new, kv_heads, group_size, head_dim)
    scores = jnp.einsum('nkgd,mkd->kgnm', query_group, keys_all.astype(jnp.float32)) * head_dim ** (-0.5)
    scores = jnp.where(seen_all[None, None], scores, NEG_FILL)
    row_max = lax.optimization_barrier(jnp.max(scores, axis=-1, keepdims=True))
    expo_all = jnp.exp(scores - row_max)
    probs_bf = (expo_all / lax.optimization_barrier(jnp.sum(expo_all, axis=-1, keepdims=True))).astype(jnp.bfloat16)
    result = jnp.einsum('kgnm,mkd->nkgd', probs_bf.astype(jnp.float32), values_all.astype(jnp.float32))
    return result.reshape(count_new, q_heads * head_dim).astype(jnp.bfloat16)

def reference(residual_in, attn_gain, w_query, w_keyval, query_gain, key_gain, w_out, ffn_gain, w_gate, w_up, w_down, key_cache, value_cache, prefix_lens, accepted, accept_path, parents, slot_kinds, expert_ids, gate_probs):
    normed = rms_rows(residual_in.astype(jnp.float32), attn_gain).astype(jnp.bfloat16)
    query_raw = jnp.dot(normed, w_query, preferred_element_type=jnp.float32).astype(jnp.bfloat16)
    keyval_raw = jnp.dot(normed, jnp.transpose(w_keyval), preferred_element_type=jnp.float32).astype(jnp.bfloat16)

    def slot_attend(packed):
        return attend(*packed, query_gain, key_gain)
    attn_out = lax.map(slot_attend, (query_raw.reshape(SLOTS, NEW, -1), keyval_raw.reshape(SLOTS, NEW, -1), key_cache, value_cache, prefix_lens, accepted, accept_path, parents, slot_kinds))
    attn_out = attn_out.reshape(TOK, HQ * HD)
    hidden_mid = residual_in.astype(jnp.float32) + jnp.dot(attn_out, w_out, preferred_element_type=jnp.float32)
    normed_ffn = rms_rows(hidden_mid, ffn_gain).astype(jnp.bfloat16)
    count_rows = SLOTS * PER

    def expert_step(running, expert):
        hit_mask = expert_ids == expert
        weights = lax.optimization_barrier(jnp.sum(jnp.where(hit_mask, gate_probs, 0.0), axis=1))
        named_int = jnp.any(hit_mask, axis=1).astype(jnp.int32)
        chosen = jnp.argsort(1 - named_int, stable=True)[:count_rows].astype(jnp.int32)
        picked = normed_ffn[chosen]
        gate_val = jnp.dot(picked, jnp.transpose(w_gate[expert]), preferred_element_type=jnp.float32)
        up_val = jnp.dot(picked, jnp.transpose(w_up[expert]), preferred_element_type=jnp.float32)
        inner_act = (jax.nn.silu(gate_val) * up_val).astype(jnp.bfloat16)
        result = jnp.dot(inner_act, w_down[expert], preferred_element_type=jnp.float32)
        return (running.at[chosen].add(result * weights[chosen][:, None]), None)
    moe_total, unused = lax.scan(expert_step, jnp.zeros((TOK, D), jnp.float32), jnp.arange(EXP_WIN, dtype=jnp.int32))
    return (hidden_mid + moe_total).astype(jnp.bfloat16)
```

```python
import functools
import math

import jax
import jax.numpy as jnp
import numpy as np
from jax import lax
from jax.experimental import pallas as pl
from jax.experimental.pallas import tpu as pltpu
from jax.sharding import PartitionSpec as P

EXPERTS = 128
SINK = 4
WIN = 512

EPSILON = 1e-06
NEG_FILL = -1e30
ROPE_BASE = 1000000.0
LOG2E = math.log2(math.e)
F32 = jnp.float32
BF16 = jnp.bfloat16
MIB = 1 << 20


def iota(shape, dim):
    return lax.broadcasted_iota(jnp.int32, shape, dim)


def dot_last(left, right):
    return lax.dot_general(left, right, (((1,), (1,)), ((), ())), preferred_element_type=F32)


def norm_rows(values):
    return values * lax.rsqrt(jnp.mean(values * values, axis=-1, keepdims=True) + EPSILON)


def call(kernel, name, outs, args, scratch=(), limit=16, flops=0, moved=0):
    many = isinstance(outs, (list, tuple))
    specs = [pl.BlockSpec(memory_space=pltpu.VMEM) for _ in (outs if many else [outs])]
    return pl.pallas_call(
        kernel,
        out_shape=outs,
        in_specs=[pl.BlockSpec(memory_space=space) for _, space in args],
        out_specs=specs if many else specs[0],
        scratch_shapes=list(scratch),
        compiler_params=pltpu.CompilerParams(vmem_limit_bytes=limit * MIB),
        cost_estimate=pl.CostEstimate(flops=flops, bytes_accessed=moved, transcendentals=0),
        name=name,
    )(*[array for array, _ in args])


def exchange(blocks):
    return lax.all_to_all(blocks, "tensor", split_axis=0, concat_axis=0, tiled=True)


def gather_blocks(block, devices):
    def hop(value, step):
        return lax.ppermute(value, "tensor", [(i, i ^ step) for i in range(devices)])

    got = {0: block}
    for step in range(2, devices, 2):
        got[step] = hop(block, step)
    got[1] = hop(block, 1)
    for step in range(2, devices, 2):
        got[step + 1] = hop(got[step], 1)
    return [got[step] for step in range(devices)]


def window_rows(path_len):
    return -(-(WIN + 2 * (path_len - 1) + 16) // 16) * 16


def prep_kernel(
    per,
    key_cache,
    value_cache,
    prefix_ref,
    accepted_ref,
    path_ref,
    kind_ref,
    parents_ref,
    ids_ref,
    gates_ref,
    freq_ref,
    keys_ref,
    values_ref,
    mask_ref,
    cos_ref,
    sin_ref,
    pick_ref,
    combine_ref,
    weight_ref,
    hit_ref,
    rank_ref,
    own_ref,
    sems,
):
    me = lax.axis_index("tensor")
    new = parents_ref.shape[1]
    cache_len = key_cache.shape[1]
    path_len = path_ref.shape[1]
    wide = window_rows(path_len)
    sink_at, win_at = new, new + 16
    end = win_at + wide
    prefix = prefix_ref[0]
    accepted = accepted_ref[0]
    total = prefix + accepted
    low = jnp.maximum(total - WIN, 0)
    start = pl.multiple_of(jnp.minimum((low // 16) * 16, cache_len - wide), 16)
    copies = []
    for which, (cache, buf) in enumerate(((key_cache, keys_ref), (value_cache, values_ref))):
        copies.append(
            pltpu.make_async_copy(
                cache.at[0, pl.ds(start, wide)], buf.at[pl.ds(win_at, wide)], sems.at[which, 0]
            )
        )
        copies.append(
            pltpu.make_async_copy(
                cache.at[0, pl.ds(0, 16)], buf.at[pl.ds(sink_at, 16)], sems.at[which, 1]
            )
        )
    for copy in copies:
        copy.start()

    span, width = keys_ref.shape
    for buf in (keys_ref, values_ref):
        buf[0:new, :] = jnp.zeros((new, width), BF16)
        buf[end:span, :] = jnp.zeros((span - end, width), BF16)

    column = iota((1, span), 1)
    row = jnp.where(column < win_at, column - sink_at, start + column - win_at)
    taken = jnp.zeros((1, span), jnp.bool_)
    for step in range(path_len):
        taken = taken | ((row == prefix + path_ref[0, step]) & (step < accepted))
    old = (row < prefix) & ((row < SINK) | (row >= total - WIN))
    in_window = (column >= win_at) & (column < end) & (old | taken)
    in_sink = (column >= sink_at) & (column < win_at) & (row < SINK) & (row < prefix) & (start > 0)
    seen = jnp.where(in_window | in_sink, 0.0, NEG_FILL)
    mask_ref[...] = jnp.broadcast_to(seen, mask_ref.shape)

    down, across = iota((new, new), 0), iota((new, new), 1)
    eye = (down == across).astype(F32)
    back = eye + (down == parents_ref[...]).astype(F32)
    for _ in range((new - 1).bit_length()):
        half = back.astype(BF16)
        back = jnp.minimum(jnp.dot(half, half, preferred_element_type=F32), 1.0)
    reach = lax.dot_general(
        back.astype(BF16), eye.astype(BF16), (((0,), (0,)), ((), ())), preferred_element_type=F32
    )
    tree = (kind_ref[0] == 1).astype(F32)
    causal = (across <= down).astype(F32)
    allowed = tree * reach + (1.0 - tree) * causal
    mask_ref[:, 0:new] = jnp.where(allowed > 0.5, 0.0, NEG_FILL)
    depth = tree * (jnp.sum(reach, axis=1, keepdims=True) - 1.0)
    depth = depth + (1.0 - tree) * iota((new, 1), 0).astype(F32)
    angle = (total.astype(F32) + depth) * freq_ref[...]
    lane = iota(angle.shape, 1)
    sine = jnp.sin(angle)
    cos_ref[...] = jnp.cos(angle)
    sin_ref[...] = jnp.where(lane < angle.shape[1] // 2, -sine, sine)

    tokens = ids_ref.shape[1]
    slots = tokens // new
    experts = hit_ref.shape[0]
    ids = ids_ref[...]
    for expert in range(experts):
        hit_ref[expert : expert + 1, :] = jnp.max(
            (ids == expert).astype(F32), axis=0, keepdims=True
        )
    before, after = iota((tokens, tokens), 0), iota((tokens, tokens), 1)
    earlier = (before < after) & (before // new == after // new)
    rank_ref[...] = jnp.dot(
        hit_ref[...].astype(BF16), earlier.astype(BF16), preferred_element_type=F32
    )
    rows = slots * per
    slot_of = iota((rows, tokens), 1) // new
    row_slot = iota((rows, tokens), 0) // per
    row_rank = (iota((rows, tokens), 0) % per).astype(F32)
    same = slot_of == row_slot
    mine = iota((1, tokens), 1) // new == me
    for expert in range(experts):
        hit = hit_ref[expert : expert + 1, :]
        rank = rank_ref[expert : expert + 1, :]
        chosen = same & (hit > 0.5) & (rank == row_rank)
        pick_ref[expert * rows : (expert + 1) * rows, :] = chosen.astype(F32).astype(BF16)
        for place in range(per):
            at = expert * per + place
            own = mine & (hit > 0.5) & (rank == float(place))
            own_ref[at : at + 1, :] = own.astype(F32)
    shift = iota((tokens, new), 0) == me * new + iota((tokens, new), 1)
    combine_ref[...] = lax.dot_general(
        shift.astype(F32).astype(BF16),
        own_ref[...].astype(BF16),
        (((0,), (1,)), ((), ())),
        preferred_element_type=F32,
    )
    weight = jnp.sum(jnp.where(ids == me, gates_ref[...], 0.0), axis=0, keepdims=True)
    hit = jnp.max((ids == me).astype(F32), axis=0, keepdims=True)
    rank = rank_ref[pl.ds(me, 1), :]
    chosen = same & (hit > 0.5) & (rank == row_rank)
    chosen_weight = jnp.sum(jnp.where(chosen, weight, 0.0), axis=1, keepdims=True)
    weight_ref[...] = jnp.broadcast_to(chosen_weight, weight_ref.shape)
    for copy in copies:
        copy.wait()


def project_kernel(devices, *refs):
    blocks = refs[:devices]
    gain_ref, wq_ref, wkv_ref, out_ref, raw_ref, normed = refs[devices:]
    me = lax.axis_index("tensor")
    rows = blocks[0].shape[0]
    gain = gain_ref[...]
    for step in range(devices):
        at = pl.multiple_of((me ^ step) * rows, rows)
        block = blocks[step][...]
        raw_ref[pl.ds(at, rows), :] = block
        normed[pl.ds(at, rows), :] = (norm_rows(block.astype(F32)) * gain).astype(BF16)
    wide = wq_ref.shape[1]
    values = normed[...]
    query = jnp.dot(values, wq_ref[...], preferred_element_type=F32).astype(BF16)
    keyval = dot_last(values, wkv_ref[...]).astype(BF16)
    out_ref[:, :, :wide] = query.reshape(devices, rows, wide)
    out_ref[:, :, wide:] = keyval.reshape(devices, rows, -1)


def attend_kernel(
    q_width,
    head,
    got_ref,
    *refs,
):
    (
        q_gain_ref,
        k_gain_ref,
        keys_in,
        values_in,
        mask_ref,
        cos_ref,
        sin_ref,
        out_ref,
        keys_ref,
        values_ref,
    ) = refs[-10:]
    devices, new, _ = got_ref.shape
    span, kv_width = keys_in.shape
    kv_heads = kv_width // head
    per_device = q_width // head
    group = devices * per_device // kv_heads
    cos, sin = cos_ref[...], sin_ref[...]

    def rope(values):
        return values * cos + pltpu.roll(values, head // 2, 1) * sin

    def fresh(piece):
        if len(refs) > 10:
            return refs[0][:, piece * head : (piece + 1) * head]
        return got_ref[piece, :, q_width : q_width + head]

    keys_ref[...] = keys_in[...]
    values_ref[...] = values_in[...]
    scale = head ** (-0.5) * LOG2E
    for kv in range(kv_heads):
        cols = slice(kv * head, (kv + 1) * head)
        key_new = rope(norm_rows(fresh(kv).astype(F32)) * k_gain_ref[...])
        keys_ref[0:new, cols] = key_new.astype(BF16)
        values_ref[0:new, cols] = fresh(kv_heads + kv)
        queries = []
        for member in range(group):
            device, part = divmod(kv * group + member, per_device)
            raw = got_ref[device, :, part * head : (part + 1) * head].astype(F32)
            queries.append(rope(norm_rows(raw) * q_gain_ref[...]).astype(BF16))
        query = jnp.concatenate(queries, axis=0)
        score = dot_last(query, keys_ref[:, cols]) * scale
        score = score.reshape(group, new, span) + mask_ref[...][None]
        expo = jnp.exp2(score - jnp.max(score, axis=-1, keepdims=True))
        denom = jnp.sum(expo, axis=-1, keepdims=True).reshape(group * new, 1)
        expo = expo.astype(BF16).reshape(group * new, span)
        result = jnp.dot(expo, values_ref[:, cols], preferred_element_type=F32) / denom
        result = result.astype(BF16)
        for member in range(group):
            device, part = divmod(kv * group + member, per_device)
            out_ref[device, :, part * head : (part + 1) * head] = result[
                member * new : (member + 1) * new
            ]


def spread_kernel(got_ref, pick_ref, w_ref, out_ref, rows_ref):
    slots, new, depth = got_ref.shape
    extra = rows_ref.shape[1] - new
    heads = got_ref[...].reshape(slots * new, depth)
    picked = jnp.dot(pick_ref[...], heads, preferred_element_type=F32).astype(BF16)
    rows_ref[:, 0:new, :] = got_ref[...]
    rows_ref[:, new:, :] = picked.reshape(slots, extra, depth)
    left = rows_ref[...].reshape(slots * (new + extra), depth)
    width = w_ref.shape[1]
    tile = min(512, width)
    for at in range(0, width, tile):
        part = jnp.dot(left, w_ref[:, at : at + tile], preferred_element_type=F32)
        out_ref[:, :, at : at + tile] = part.astype(BF16).reshape(slots, new + extra, tile)


def select_kernel(pick_ref, raw_ref, out_ref):
    me = lax.axis_index("tensor")
    rows = out_ref.shape[0]
    pick = pick_ref[pl.ds(pl.multiple_of(me * rows, rows), rows), :]
    out_ref[...] = jnp.dot(pick, raw_ref[...], preferred_element_type=F32)


def expert_kernel(
    got_ref, own_ref, picked_ref, gain_ref, weight_ref, wg_ref, wu_ref, wd_ref, out_ref, hidden_ref
):
    devices, rows, width = got_ref.shape
    new = own_ref.shape[0]
    per = out_ref.shape[1]
    total = got_ref[0].astype(F32)
    for source in range(1, devices):
        total = total + got_ref[source].astype(F32)
    hidden_ref[...] = own_ref[...].astype(F32) + total[:new]
    hidden = picked_ref[...] + total[new:]
    normed = (norm_rows(hidden) * gain_ref[...]).astype(BF16)
    gate = dot_last(normed, wg_ref[0])
    up = dot_last(normed, wu_ref[0])
    inner = (gate / (1.0 + jnp.exp(-gate)) * up).astype(BF16)
    result = jnp.dot(inner, wd_ref[0], preferred_element_type=F32) * weight_ref[:, 0:1]
    for slot in range(out_ref.shape[0]):
        out_ref[slot] = result[slot * per : (slot + 1) * per].astype(BF16)


def combine_kernel(hidden_ref, got_ref, combine_ref, out_ref, rows_ref):
    experts, per, width = got_ref.shape
    for expert in range(experts):
        rows_ref[expert * per : (expert + 1) * per, :] = got_ref[expert].astype(F32)
    moe = jnp.dot(
        combine_ref[...].astype(BF16), rows_ref[...].astype(BF16), preferred_element_type=F32
    )
    out_ref[...] = (hidden_ref[...] + moe).astype(BF16)


def body(
    residual_in,
    attn_gain,
    w_query,
    w_keyval,
    query_gain,
    key_gain,
    w_out,
    ffn_gain,
    w_gate,
    w_up,
    w_down,
    key_cache,
    value_cache,
    prefix_lens,
    accepted,
    accept_path,
    parents,
    slot_kinds,
    expert_ids,
    gate_probs,
):
    devices = lax.axis_size("tensor")
    new, width = residual_in.shape
    head = query_gain.shape[0]
    kv_width = key_cache.shape[2]
    q_width = w_query.shape[1]
    new_width = w_keyval.shape[0]
    tokens, top = expert_ids.shape
    per = new * top // EXPERTS
    held = devices * w_gate.shape[0]
    rows = devices * per
    assert key_cache.shape[0] == 1 and w_gate.shape[0] == 1
    vmem, smem, any_space = pltpu.VMEM, pltpu.SMEM, pl.ANY
    shape = jax.ShapeDtypeStruct

    blocks = gather_blocks(residual_in, devices)

    freq = ROPE_BASE ** (-2.0 * np.arange(head // 2) / head)
    freq = jnp.asarray(np.concatenate([freq, freq])[None, :], F32)
    span = -(-(new + 16 + window_rows(accept_path.shape[1])) // 128) * 128
    keys, values, mask, cos, sin, pick, combine, weight = call(
        functools.partial(prep_kernel, per),
        "prep",
        [
            shape((span, kv_width), BF16),
            shape((span, kv_width), BF16),
            shape((new, span), F32),
            shape((new, head), F32),
            shape((new, head), F32),
            shape((held * rows, tokens), BF16),
            shape((new, held * per), F32),
            shape((rows, 128), F32),
        ],
        [
            (key_cache, any_space),
            (value_cache, any_space),
            (prefix_lens, smem),
            (accepted, smem),
            (accept_path, smem),
            (slot_kinds, smem),
            (parents, vmem),
            (expert_ids.T, vmem),
            (gate_probs.T, vmem),
            (freq, vmem),
        ],
        [
            pltpu.VMEM((held, tokens), F32),
            pltpu.VMEM((held, tokens), F32),
            pltpu.VMEM((held * per, tokens), F32),
            pltpu.SemaphoreType.DMA((2, 2)),
        ],
        limit=24,
        moved=4 * span * kv_width * 2,
    )

    projected, raw = call(
        functools.partial(project_kernel, devices),
        "project",
        [
            shape((devices, new, q_width + new_width), BF16),
            shape((tokens, width), BF16),
        ],
        [(block, vmem) for block in blocks]
        + [(attn_gain[None, :], vmem), (w_query, vmem), (w_keyval, vmem)],
        [pltpu.VMEM((tokens, width), BF16)],
        limit=32,
        flops=2 * tokens * width * (q_width + new_width),
        moved=2 * width * (q_width + new_width),
    )
    got = exchange(projected)
    picked_in = call(
        select_kernel,
        "select",
        shape((rows, width), F32),
        [(pick, vmem), (raw, vmem)],
        flops=2 * rows * width * tokens,
        moved=2 * tokens * width,
    )

    extra = []
    if new_width % head:
        extra = [(got[:, :, q_width:].transpose(1, 0, 2).reshape(new, -1), vmem)]
    attended = call(
        functools.partial(attend_kernel, q_width, head),
        "attend",
        shape((devices, new, q_width), BF16),
        [(got, vmem)]
        + extra
        + [
            (query_gain[None, :], vmem),
            (key_gain[None, :], vmem),
            (keys, vmem),
            (values, vmem),
            (mask, vmem),
            (cos, vmem),
            (sin, vmem),
        ],
        [pltpu.VMEM((span, kv_width), BF16), pltpu.VMEM((span, kv_width), BF16)],
        limit=24,
        flops=4 * new * devices * q_width * span,
        moved=4 * span * kv_width,
    )
    heads = exchange(attended)

    partial = call(
        spread_kernel,
        "spread",
        shape((devices, new + rows, width), BF16),
        [(heads, vmem), (pick, vmem), (w_out, vmem)],
        [pltpu.VMEM((devices, new + rows, q_width), BF16)],
        limit=32,
        flops=2 * devices * (new + rows) * width * q_width,
        moved=2 * q_width * width,
    )
    partials = exchange(partial)

    result, hidden = call(
        expert_kernel,
        "expert",
        [shape((devices, per, width), BF16), shape((new, width), F32)],
        [
            (partials, vmem),
            (residual_in, vmem),
            (picked_in, vmem),
            (ffn_gain[None, :], vmem),
            (weight, vmem),
            (w_gate, vmem),
            (w_up, vmem),
            (w_down, vmem),
        ],
        limit=40,
        flops=6 * rows * width * w_gate.shape[1],
        moved=6 * width * w_gate.shape[1],
    )
    returned = exchange(result)
    return call(
        combine_kernel,
        "combine",
        shape((new, width), BF16),
        [(hidden, vmem), (returned, vmem), (combine, vmem)],
        [pltpu.VMEM((held * per, width), F32)],
        moved=6 * new * width,
    )


def solution(mesh):
    in_specs = (
        P(("group", "tensor"), None),
        P(),
        P(None, "tensor"),
        P("tensor", None),
        P(),
        P(),
        P("tensor", None),
        P(),
        P("tensor", None, None),
        P("tensor", None, None),
        P("tensor", None, None),
        P(("group", "tensor"), None, None),
        P(("group", "tensor"), None, None),
        P(("group", "tensor")),
        P(("group", "tensor")),
        P(("group", "tensor"), None),
        P(("group", "tensor"), None),
        P(("group", "tensor")),
        P("group", None),
        P("group", None),
    )
    out_specs = P(("group", "tensor"), None)
    return jax.shard_map(body, mesh=mesh, in_specs=in_specs, out_specs=out_specs, check_vma=False)
```

```python
import functools
import math

import jax
import jax.numpy as jnp
import numpy as np
from jax import lax
from jax.experimental import pallas as pl
from jax.experimental.pallas import tpu as pltpu
from jax.sharding import PartitionSpec as P

EXPERTS = 128
SINK = 4
WIN = 512

EPSILON = 1e-06
NEG_FILL = -1e30
ROPE_BASE = 1000000.0
LOG2E = math.log2(math.e)
F32 = jnp.float32
BF16 = jnp.bfloat16
MIB = 1 << 20


def iota(shape, dim):
    return lax.broadcasted_iota(jnp.int32, shape, dim)


def dot(left, right):
    return jnp.dot(left, right, preferred_element_type=F32)


def dot_last(left, right):
    return lax.dot_general(left, right, (((1,), (1,)), ((), ())), preferred_element_type=F32)


def dot_first(left, right):
    return lax.dot_general(left, right, (((0,), (0,)), ((), ())), preferred_element_type=F32)


def norm_rows(values):
    return values * lax.rsqrt(jnp.mean(values * values, axis=-1, keepdims=True) + EPSILON)


def in_vmem(shape, dtype):
    return pltpu.VMEM(shape, dtype)


def call(kernel, name, outs, args, scratch=(), limit=16, flops=0, moved=0):
    arrays = []
    specs = []
    for array, space in args:
        if space is pltpu.HBM or space is pltpu.VMEM:
            array = pltpu.with_memory_space_constraint(array, space)
        arrays.append(array)
        specs.append(pl.BlockSpec(memory_space=space))
    return pl.pallas_call(
        kernel,
        out_shape=outs,
        in_specs=specs,
        out_specs=[pl.BlockSpec(memory_space=pltpu.VMEM) for _ in outs],
        scratch_shapes=list(scratch),
        compiler_params=pltpu.CompilerParams(vmem_limit_bytes=limit * MIB),
        cost_estimate=pl.CostEstimate(flops=flops, bytes_accessed=moved, transcendentals=0),
        name=name,
    )(*arrays)


def hop(value, step):
    devices = lax.axis_size("tensor")
    return lax.ppermute(value, "tensor", [(i, i ^ step) for i in range(devices)])


def exchange(blocks):
    return [blocks[0]] + [hop(blocks[j], 2 * j) for j in range(1, len(blocks))]


def after(value, other):
    return lax.optimization_barrier((value, other))[0]


def window_rows(path_len):
    return -(-(WIN + 2 * (path_len - 1) + 16) // 16) * 16


def prep_kernel(path_len, per, n_weights, *refs):
    (
        packed_ref,
        key_cache,
        value_cache,
        packed_in,
        ids_in,
        gates_in,
        freq_in,
        q_gain_in,
        k_gain_in,
    ) = refs[:9]
    sources = refs[9 : 9 + n_weights]
    refs = refs[9 + n_weights :]
    keys_ref, values_ref, mask_ref, rot_ref, pick_ref, combine_ref, weight_ref = refs[:7]
    targets = refs[7 : 7 + n_weights]
    refs = refs[7 + n_weights :]
    packed_vec, ids_ref, gates_ref, freq_ref, q_gain_ref, k_gain_ref = refs[:6]
    hit_ref, rank_ref, own_ref, small_sems, cache_sems, weight_sems = refs[6:]

    me = lax.axis_index("tensor")
    new = mask_ref.shape[0]
    kv_heads, span, head = keys_ref.shape
    cache_len = key_cache.shape[1]
    wide = window_rows(path_len)
    sink_at, win_at = new, new + 16
    end = win_at + wide

    small = []
    pairs = (
        (packed_in, packed_vec),
        (ids_in, ids_ref),
        (gates_in, gates_ref),
        (freq_in, freq_ref),
        (q_gain_in, q_gain_ref),
        (k_gain_in, k_gain_ref),
    )
    for which, (source, target) in enumerate(pairs):
        small.append(pltpu.make_async_copy(source, target, small_sems.at[which]))
        small[-1].start()

    prefix = packed_ref[0, new]
    accepted = packed_ref[0, new + 1]
    total = prefix + accepted
    low = jnp.maximum(total - WIN, 0)
    start = pl.multiple_of(jnp.minimum((low // 16) * 16, cache_len - wide), 16)
    copies = []
    for which, (cache, buf) in enumerate(((key_cache, keys_ref), (value_cache, values_ref))):
        for kv in range(kv_heads):
            cols = pl.ds(kv * head, head)
            copies.append(
                pltpu.make_async_copy(
                    cache.at[0, pl.ds(start, wide), cols],
                    buf.at[kv, pl.ds(win_at, wide)],
                    cache_sems.at[which, kv, 0],
                )
            )
            copies.append(
                pltpu.make_async_copy(
                    cache.at[0, pl.ds(0, 16), cols],
                    buf.at[kv, pl.ds(sink_at, 16)],
                    cache_sems.at[which, kv, 1],
                )
            )
    for which, (source, target) in enumerate(zip(sources, targets)):
        copies.append(pltpu.make_async_copy(source, target, weight_sems.at[which]))
    for copy in copies:
        copy.start()

    for buf in (keys_ref, values_ref):
        buf[:, 0:new, :] = jnp.zeros((kv_heads, new, head), BF16)
        buf[:, end:span, :] = jnp.zeros((kv_heads, span - end, head), BF16)

    column = iota((1, span), 1)
    row = jnp.where(column < win_at, column - sink_at, start + column - win_at)
    taken = jnp.zeros((1, span), jnp.bool_)
    for step in range(path_len):
        at = prefix + packed_ref[0, new + 8 + step]
        taken = taken | ((row == at) & (step < accepted))
    old = (row < prefix) & ((row < SINK) | (row >= total - WIN))
    in_window = (column >= win_at) & (column < end) & (old | taken)
    in_sink = (column >= sink_at) & (column < win_at) & (row < SINK) & (row < prefix) & (start > 0)
    seen = jnp.where(in_window | in_sink, 0.0, NEG_FILL)
    mask_ref[...] = jnp.broadcast_to(seen, mask_ref.shape)

    for copy in small:
        copy.wait()
    down, across = iota((new, new), 0), iota((new, new), 1)
    eye = (down == across).astype(F32)
    back = eye + (down == packed_vec[:, 0:new]).astype(F32)
    for _ in range((new - 1).bit_length()):
        half = back.astype(BF16)
        back = jnp.minimum(dot(half, half), 1.0)
    reach = dot_first(back.astype(BF16), eye.astype(BF16))
    tree = (packed_ref[0, new + 2] == 1).astype(F32)
    causal = (across <= down).astype(F32)
    allowed = tree * reach + (1.0 - tree) * causal
    mask_ref[:, 0:new] = jnp.where(allowed > 0.5, 0.0, NEG_FILL)
    depth = tree * (jnp.sum(reach, axis=1, keepdims=True) - 1.0)
    depth = depth + (1.0 - tree) * iota((new, 1), 0).astype(F32)
    angle = (total.astype(F32) + depth) * freq_ref[...]
    lane = iota(angle.shape, 1)
    cosine, sine = jnp.cos(angle), jnp.sin(angle)
    sine = jnp.where(lane < head // 2, -sine, sine)
    for which, gain_ref in enumerate((q_gain_ref, k_gain_ref)):
        gain = jnp.broadcast_to(gain_ref[...], angle.shape)
        rot_ref[2 * which] = cosine * gain
        rot_ref[2 * which + 1] = sine * pltpu.roll(gain, head // 2, 1)

    all_tokens = ids_ref.shape[1]
    devices = hit_ref.shape[0]
    chips = devices // 2
    tokens = chips * new
    slot = iota((all_tokens, tokens), 1) // new
    source = (me ^ (2 * slot)) * new + iota((all_tokens, tokens), 1) % new
    order = (iota((all_tokens, tokens), 0) == source).astype(F32)
    ids = dot(ids_ref[...].astype(F32).astype(BF16), order.astype(BF16))
    gates = lax.dot_general(
        gates_ref[...],
        order,
        (((1,), (0,)), ((), ())),
        precision=lax.Precision.HIGHEST,
        preferred_element_type=F32,
    )
    for rel in range(devices):
        named = (ids == (me ^ rel).astype(F32)).astype(F32)
        hit_ref[rel : rel + 1, :] = jnp.max(named, axis=0, keepdims=True)
    before, later = iota((tokens, tokens), 0), iota((tokens, tokens), 1)
    earlier = (before < later) & (before // new == later // new)
    rank_ref[...] = dot(hit_ref[...].astype(BF16), earlier.astype(F32).astype(BF16))
    rows = chips * per
    slot_of = iota((rows, tokens), 1) // new
    row_slot = iota((rows, tokens), 0) // per
    row_rank = (iota((rows, tokens), 0) % per).astype(F32)
    in_first = iota((1, tokens), 1) < new
    for rel in range(devices):
        hit = hit_ref[rel : rel + 1, :] > 0.5
        rank = rank_ref[rel : rel + 1, :]
        chosen = (slot_of == (row_slot ^ (rel // 2))) & hit & (rank == row_rank)
        pick_ref[rel * rows : (rel + 1) * rows, :] = chosen.astype(F32)
        if rel < 2:
            named = ids == (me ^ rel).astype(F32)
            weight = jnp.sum(jnp.where(named, gates, 0.0), axis=0, keepdims=True)
            weight = jnp.sum(jnp.where(chosen, weight, 0.0), axis=1, keepdims=True)
            weight_ref[rel * rows : (rel + 1) * rows, :] = jnp.broadcast_to(
                weight, (rows, weight_ref.shape[1])
            )
        for place in range(per):
            at = rel * per + place
            own_ref[at : at + 1, :] = (in_first & hit & (rank == float(place))).astype(F32)
    first = (iota((tokens, new), 0) == iota((tokens, new), 1)).astype(F32)
    combine_ref[...] = lax.dot_general(
        first.astype(BF16),
        own_ref[...].astype(BF16),
        (((0,), (1,)), ((), ())),
        preferred_element_type=F32,
    )
    for copy in copies:
        copy.wait()


def project_kernel(chips, *refs):
    blocks = refs[:chips]
    gain_ref, wq_ref, wkv_ref, wq_sib, wkv_sib, _ = refs[chips : chips + 6]
    outs = refs[chips + 6 : 2 * chips + 6]
    normed, wq_buf, wkv_buf, sems = refs[2 * chips + 6 :]
    copies = [
        pltpu.make_async_copy(wq_sib, wq_buf, sems.at[0]),
        pltpu.make_async_copy(wkv_sib, wkv_buf, sems.at[1]),
    ]
    for copy in copies:
        copy.start()
    rows = blocks[0].shape[0]
    gain = gain_ref[...]
    for j in range(chips):
        values = norm_rows(blocks[j][...].astype(F32)) * gain
        normed[j * rows : (j + 1) * rows, :] = values.astype(BF16)
    values = normed[...]

    def put(result, at):
        result = result.astype(BF16)
        for j in range(chips):
            outs[j][:, at : at + result.shape[1]] = result[j * rows : (j + 1) * rows]

    wide, narrow = wq_ref.shape[1], wkv_ref.shape[0]
    put(dot(values, wq_ref[...]), 0)
    put(dot_last(values, wkv_ref[...]), 2 * wide)
    for copy in copies:
        copy.wait()
    put(dot(values, wq_buf[...]), wide)
    put(dot_last(values, wkv_buf[...]), 2 * wide + narrow)


def attend_kernel(chips, q_width, kv_ready, *refs):
    got = refs[:chips]
    at = chips + 1 if kv_ready else chips
    keys_ref, values_ref, mask_ref, rot_ref = refs[at : at + 4]
    outs = refs[at + 4 : at + 4 + chips]
    fresh_ref = refs[chips] if kv_ready else refs[-1]
    me = lax.axis_index("tensor")
    chip = me // 2
    new = got[0].shape[0]
    kv_heads, span, head = keys_ref.shape
    per_chip = 2 * q_width // head
    group = chips * per_chip // kv_heads

    if not kv_ready:
        for rel in range(2 * chips):
            left = 2 * q_width + (rel % 2) * head
            fresh_ref[rel] = got[rel // 2][:, left : left + head]

    def rope(values, which):
        values = norm_rows(values.astype(F32))
        turned = pltpu.roll(values, head // 2, 1)
        return (values * rot_ref[2 * which] + turned * rot_ref[2 * which + 1]).astype(BF16)

    scale = head ** (-0.5) * LOG2E
    for j in range(chips):
        kv = (chip ^ j) * per_chip // group
        key_at, value_at = kv, kv + kv_heads
        if not kv_ready:
            key_at, value_at = me ^ key_at, me ^ value_at
        keys = jnp.concatenate([rope(fresh_ref[key_at], 1), keys_ref[kv, new:span]], axis=0)
        values = jnp.concatenate([fresh_ref[value_at], values_ref[kv, new:span]], axis=0)
        query = jnp.concatenate(
            [rope(got[j][:, h * head : (h + 1) * head], 0) for h in range(per_chip)], axis=0
        )
        score = dot_last(query, keys) * scale
        score = score.reshape(per_chip, new, span) + mask_ref[...][None]
        expo = jnp.exp2(score - jnp.max(score, axis=-1, keepdims=True))
        denom = jnp.sum(expo, axis=-1, keepdims=True).reshape(per_chip * new, 1)
        expo = expo.astype(BF16).reshape(per_chip * new, span)
        result = (dot(expo, values) / denom).astype(BF16)
        for h in range(per_chip):
            outs[j][:, h * head : (h + 1) * head] = result[h * new : (h + 1) * new]


def spread_kernel(chips, *refs):
    got = refs[:chips]
    pick_ref, w_ref, w_sib = refs[chips : chips + 3]
    outs = refs[chips + 3 : 2 * chips + 3]
    rows_ref, w_buf, sem = refs[2 * chips + 3 :]
    copy = pltpu.make_async_copy(w_sib, w_buf, sem.at[0])
    copy.start()
    new = got[0].shape[0]
    depth, width = w_ref.shape
    each = rows_ref.shape[1]
    heads = jnp.concatenate([got[j][...] for j in range(chips)], axis=0)
    picked = dot(pick_ref[...].astype(BF16), heads).astype(BF16)
    extra = each - new
    for j in range(chips):
        rows_ref[j, 0:new, :] = got[j][...]
        rows_ref[j, new:each, :] = picked[j * extra : (j + 1) * extra]
    left = rows_ref[...].reshape(chips * each, 2 * depth)
    copy.wait()
    tile = min(512, width)
    for at in range(0, width, tile):
        part = dot(left[:, :depth], w_ref[:, at : at + tile])
        part = (part + dot(left[:, depth:], w_buf[:, at : at + tile])).astype(BF16)
        for j in range(chips):
            outs[j][:, at : at + tile] = part[j * each : (j + 1) * each]


def fetch_kernel(chips, *refs):
    blocks = refs[:chips]
    pick_ref, _ = refs[chips : chips + 2]
    sources = refs[chips + 2 : chips + 6]
    picked_ref = refs[chips + 6]
    targets = refs[chips + 7 : chips + 11]
    sems = refs[-1]
    copies = [
        pltpu.make_async_copy(source, target, sems.at[which])
        for which, (source, target) in enumerate(zip(sources, targets))
    ]
    for copy in copies:
        copy.start()
    values = jnp.concatenate([block[...] for block in blocks], axis=0)
    pick = pick_ref[0 : picked_ref.shape[0], :].astype(BF16)
    picked_ref[...] = dot(pick, values)
    for copy in copies:
        copy.wait()


def expert_kernel(chips, per, *refs):
    got = refs[:chips]
    own_ref, picked_ref, weight_ref, gain_ref = refs[chips : chips + 4]
    weights = refs[chips + 4 : chips + 10]
    outs = refs[chips + 10 : 2 * chips + 10]
    hidden_ref = refs[2 * chips + 10]
    new = own_ref.shape[0]
    total = got[0][...].astype(F32)
    for j in range(1, chips):
        total = total + got[j][...].astype(F32)
    hidden_ref[...] = own_ref[...].astype(F32) + total[:new]
    hidden = picked_ref[...] + total[new:]
    normed = norm_rows(hidden) * gain_ref[...]
    rows = chips * per
    for core in range(2):
        gate_ref, up_ref, down_ref = weights[3 * core : 3 * core + 3]
        left = normed[core * rows : (core + 1) * rows].astype(BF16)
        gate = dot_last(left, gate_ref[0])
        up = dot_last(left, up_ref[0])
        inner = (gate / (1.0 + jnp.exp(-gate)) * up).astype(BF16)
        result = dot(inner, down_ref[0]) * weight_ref[core * rows : (core + 1) * rows, 0:1]
        result = result.astype(BF16)
        for j in range(chips):
            outs[j][core * per : (core + 1) * per, :] = result[j * per : (j + 1) * per]


def combine_kernel(chips, *refs):
    hidden_ref, combine_ref = refs[:2]
    got = refs[2 : 2 + chips]
    out_ref = refs[2 + chips]
    rows = jnp.concatenate([block[...].astype(F32) for block in got], axis=0)
    moe = dot(combine_ref[...].astype(BF16), rows.astype(BF16))
    out_ref[...] = (hidden_ref[...] + moe).astype(BF16)


def body(
    residual_in,
    attn_gain,
    w_query,
    w_keyval,
    query_gain,
    key_gain,
    w_out,
    ffn_gain,
    w_gate,
    w_up,
    w_down,
    key_cache,
    value_cache,
    prefix_lens,
    accepted,
    accept_path,
    parents,
    slot_kinds,
    expert_ids,
    gate_probs,
):
    devices = lax.axis_size("tensor")
    chips = devices // 2
    new, width = residual_in.shape
    head = query_gain.shape[0]
    kv_heads = key_cache.shape[2] // head
    q_width = w_query.shape[1]
    new_width = w_keyval.shape[0]
    all_tokens, top = expert_ids.shape
    tokens = chips * new
    per = new * top // EXPERTS
    path_len = accept_path.shape[1]
    rows = 2 * chips * per
    assert key_cache.shape[0] == 1 and w_gate.shape[0] == 1
    assert devices & (devices - 1) == 0
    vmem, smem, hbm, anywhere = pltpu.VMEM, pltpu.SMEM, pltpu.HBM, pl.ANY

    blocks = exchange([residual_in] * chips)
    wq_sib = hop(w_query, 1)
    wkv_sib = hop(w_keyval, 1)

    freq = ROPE_BASE ** (-2.0 * np.arange(head // 2) / head)
    freq = jnp.asarray(np.concatenate([freq, freq])[None, :], F32)
    lens = jnp.stack([prefix_lens[0], accepted[0], slot_kinds[0]])
    packed = jnp.concatenate([parents[0], lens, jnp.zeros(5, jnp.int32), accept_path[0]])
    packed = jnp.pad(packed, (0, 128 - packed.shape[0]))[None, :]
    span = -(-(new + 16 + window_rows(path_len)) // 128) * 128
    weights = [attn_gain[None, :], w_query, w_keyval, w_out]
    prepared = call(
        functools.partial(prep_kernel, path_len, per, len(weights)),
        "prep",
        [
            in_vmem((kv_heads, span, head), BF16),
            in_vmem((kv_heads, span, head), BF16),
            in_vmem((new, span), F32),
            in_vmem((4, new, head), F32),
            in_vmem((chips * rows, tokens), F32),
            in_vmem((new, devices * per), F32),
            in_vmem((rows, 128), F32),
        ]
        + [in_vmem(weight.shape, weight.dtype) for weight in weights],
        [
            (packed, smem),
            (key_cache, hbm),
            (value_cache, hbm),
            (packed, hbm),
            (expert_ids.T, hbm),
            (gate_probs.T, hbm),
            (freq, hbm),
            (query_gain[None, :], hbm),
            (key_gain[None, :], hbm),
        ]
        + [(weight, hbm) for weight in weights],
        [
            pltpu.VMEM((1, 128), jnp.int32),
            pltpu.VMEM((top, all_tokens), jnp.int32),
            pltpu.VMEM((top, all_tokens), F32),
            pltpu.VMEM((1, head), F32),
            pltpu.VMEM((1, head), F32),
            pltpu.VMEM((1, head), F32),
            pltpu.VMEM((devices, tokens), F32),
            pltpu.VMEM((devices, tokens), F32),
            pltpu.VMEM((devices * per, tokens), F32),
            pltpu.SemaphoreType.DMA((6,)),
            pltpu.SemaphoreType.DMA((2, kv_heads, 2)),
            pltpu.SemaphoreType.DMA((len(weights),)),
        ],
        limit=16,
        moved=4 * span * kv_heads * head * 2,
    )
    keys, values, mask, rot, pick, combine, weight, gain, wq, wkv, wo = prepared

    projected = call(
        functools.partial(project_kernel, chips),
        "project",
        [in_vmem((new, 2 * (q_width + new_width)), BF16)] * chips,
        [(block, vmem) for block in blocks]
        + [
            (gain, vmem),
            (wq, vmem),
            (wkv, vmem),
            (wq_sib, anywhere),
            (wkv_sib, anywhere),
            (mask, anywhere),
        ],
        [
            pltpu.VMEM((tokens, width), BF16),
            pltpu.VMEM(w_query.shape, BF16),
            pltpu.VMEM(w_keyval.shape, BF16),
            pltpu.SemaphoreType.DMA((2,)),
        ],
        limit=16,
        flops=4 * tokens * width * (q_width + new_width),
        moved=4 * width * (q_width + new_width),
    )
    wo_sib = hop(after(w_out, blocks[1]), 1)
    experts = [w_gate, w_up, w_down]
    experts_sib = [hop(after(w_gate, projected[0]), 1)]

    got = exchange(projected)
    kv_ready = []
    if new_width != head:
        pieces = [
            got[rel // 2][:, 2 * q_width + (rel % 2) * new_width :][:, :new_width]
            for rel in range(devices)
        ]
        pieces = jnp.stack(pieces)[lax.axis_index("tensor") ^ jnp.arange(devices)]
        pieces = pieces.transpose(1, 0, 2).reshape(new, 2 * kv_heads, head)
        kv_ready = [(pieces.transpose(1, 0, 2), vmem)]
    attended = call(
        functools.partial(attend_kernel, chips, q_width, bool(kv_ready)),
        "attend",
        [in_vmem((new, 2 * q_width), BF16)] * chips,
        [(block, vmem) for block in got]
        + kv_ready
        + [(keys, vmem), (values, vmem), (mask, vmem), (rot, vmem)],
        [] if kv_ready else [pltpu.VMEM((devices, new, head), BF16)],
        limit=16,
        flops=8 * new * chips * q_width * span,
        moved=4 * span * kv_heads * head,
    )
    heads = exchange(attended)
    experts_sib.append(hop(after(w_up, attended[0]), 1))

    partial = call(
        functools.partial(spread_kernel, chips),
        "spread",
        [in_vmem((new + rows, width), BF16)] * chips,
        [(block, vmem) for block in heads] + [(pick, vmem), (wo, vmem), (wo_sib, anywhere)],
        [
            pltpu.VMEM((chips, new + rows, 2 * q_width), BF16),
            pltpu.VMEM(w_out.shape, BF16),
            pltpu.SemaphoreType.DMA((1,)),
        ],
        limit=16,
        flops=4 * chips * (new + rows) * width * q_width,
        moved=4 * q_width * width,
    )
    partials = exchange(partial)
    experts_sib.append(hop(after(w_down, heads[1]), 1))

    fetch = [ffn_gain[None, :]] + experts
    picked, ffn, *held = call(
        functools.partial(fetch_kernel, chips),
        "fetch",
        [in_vmem((rows, width), F32)] + [in_vmem(x.shape, x.dtype) for x in fetch],
        [(block, vmem) for block in blocks]
        + [(pick, vmem), (partial[0], anywhere)]
        + [(x, hbm) for x in fetch],
        [pltpu.SemaphoreType.DMA((len(fetch),))],
        limit=8,
        flops=2 * rows * width * tokens,
        moved=4 * 3 * width * w_gate.shape[1],
    )
    results = call(
        functools.partial(expert_kernel, chips, per),
        "expert",
        [in_vmem((2 * per, width), BF16)] * chips + [in_vmem((new, width), F32)],
        [(block, vmem) for block in partials]
        + [(residual_in, vmem), (picked, vmem), (weight, vmem), (ffn, vmem)]
        + [(w, vmem) for w in held + experts_sib],
        limit=16,
        flops=12 * rows * width * w_gate.shape[1],
        moved=12 * width * w_gate.shape[1],
    )
    hidden = results[chips]
    returned = exchange(results[:chips])
    return call(
        functools.partial(combine_kernel, chips),
        "combine",
        [jax.ShapeDtypeStruct((new, width), BF16)],
        [(hidden, vmem), (combine, vmem)] + [(block, vmem) for block in returned],
        limit=8,
        moved=6 * new * width,
    )[0]


def solution(mesh):
    in_specs = (
        P(("group", "tensor"), None),
        P(),
        P(None, "tensor"),
        P("tensor", None),
        P(),
        P(),
        P("tensor", None),
        P(),
        P("tensor", None, None),
        P("tensor", None, None),
        P("tensor", None, None),
        P(("group", "tensor"), None, None),
        P(("group", "tensor"), None, None),
        P(("group", "tensor")),
        P(("group", "tensor")),
        P(("group", "tensor"), None),
        P(("group", "tensor"), None),
        P(("group", "tensor")),
        P("group", None),
        P("group", None),
    )
    out_specs = P(("group", "tensor"), None)
    return jax.shard_map(body, mesh=mesh, in_specs=in_specs, out_specs=out_specs, check_vma=False)
```

```python
import functools
import math

import jax
import jax.numpy as jnp
import numpy as np
from jax import lax
from jax.experimental import pallas as pl
from jax.experimental.pallas import tpu as pltpu
from jax.sharding import PartitionSpec as P

EXPERTS = 128
SINK = 4
WIN = 512

EPSILON = 1e-06
NEG_FILL = -1e30
ROPE_BASE = 1000000.0
LOG2E = math.log2(math.e)
F32 = jnp.float32
BF16 = jnp.bfloat16
MIB = 1 << 20


def iota(shape, dim):
    return lax.broadcasted_iota(jnp.int32, shape, dim)


def dot(left, right):
    return jnp.dot(left, right, preferred_element_type=F32)


def dot_last(left, right):
    return lax.dot_general(left, right, (((1,), (1,)), ((), ())), preferred_element_type=F32)


def dot_first(left, right):
    return lax.dot_general(left, right, (((0,), (0,)), ((), ())), preferred_element_type=F32)


def norm_rows(values):
    return values * lax.rsqrt(jnp.mean(values * values, axis=-1, keepdims=True) + EPSILON)


def in_vmem(shape, dtype):
    return pltpu.VMEM(shape, dtype)


def call(kernel, name, outs, args, scratch=(), limit=16, flops=0, moved=0, same=None):
    arrays = []
    specs = []
    for array, space in args:
        if space is pltpu.HBM or space is pltpu.VMEM:
            array = pltpu.with_memory_space_constraint(array, space)
        arrays.append(array)
        specs.append(pl.BlockSpec(memory_space=space))
    return pl.pallas_call(
        kernel,
        out_shape=outs,
        in_specs=specs,
        out_specs=[pl.BlockSpec(memory_space=pltpu.VMEM) for _ in outs],
        scratch_shapes=list(scratch),
        input_output_aliases=same or {},
        compiler_params=pltpu.CompilerParams(vmem_limit_bytes=limit * MIB),
        cost_estimate=pl.CostEstimate(flops=flops, bytes_accessed=moved, transcendentals=0),
        name=name,
    )(*arrays)


def hop(value, step):
    devices = lax.axis_size("tensor")
    return lax.ppermute(value, "tensor", [(i, i ^ step) for i in range(devices)])


def exchange(blocks):
    return [blocks[0]] + [hop(blocks[j], 2 * j) for j in range(1, len(blocks))]


def window_rows(path_len):
    return -(-(WIN + 2 * (path_len - 1) + 16) // 16) * 16


def prep_kernel(path_len, per, n_weights, *refs):
    key_cache, value_cache, prefix_ref, accepted_ref, kind_ref = refs[:5]
    small_in = refs[5:12]
    sources = refs[12 : 12 + n_weights]
    refs = refs[12 + n_weights :]
    keys_ref, values_ref, mask_ref, rot_ref, pick_ref, combine_ref, weight_ref = refs[:7]
    targets = refs[7 : 7 + n_weights]
    refs = refs[7 + n_weights :]
    path_ref, parents_ref, ids_ref, gates_ref, freq_ref, q_gain_ref, k_gain_ref = refs[:7]
    hit_ref, rank_ref, own_ref, small_sems, cache_sems, weight_sems = refs[7:]

    me = lax.axis_index("tensor")
    new = mask_ref.shape[0]
    kv_heads, span, head = keys_ref.shape
    cache_len = key_cache.shape[1]
    wide = window_rows(path_len)
    sink_at, win_at = new, new + 16
    end = win_at + wide

    small = [
        pltpu.make_async_copy(source, target, small_sems.at[which])
        for which, (source, target) in enumerate(zip(small_in, refs[:7]))
    ]
    for copy in small:
        copy.start()
    prefix = prefix_ref[0]
    accepted = accepted_ref[0]
    total = prefix + accepted
    low = jnp.maximum(total - WIN, 0)
    start = pl.multiple_of(jnp.minimum((low // 16) * 16, cache_len - wide), 16)
    copies = []
    for which, (cache, buf) in enumerate(((key_cache, keys_ref), (value_cache, values_ref))):
        for kv in range(kv_heads):
            cols = pl.ds(kv * head, head)
            copies.append(
                pltpu.make_async_copy(
                    cache.at[0, pl.ds(start, wide), cols],
                    buf.at[kv, pl.ds(win_at, wide)],
                    cache_sems.at[which, kv, 0],
                )
            )
            copies.append(
                pltpu.make_async_copy(
                    cache.at[0, pl.ds(0, 16), cols],
                    buf.at[kv, pl.ds(sink_at, 16)],
                    cache_sems.at[which, kv, 1],
                )
            )
    for which, (source, target) in enumerate(zip(sources, targets)):
        copies.append(pltpu.make_async_copy(source, target, weight_sems.at[which]))
    for copy in copies:
        copy.start()

    for buf in (keys_ref, values_ref):
        buf[:, 0:new, :] = jnp.zeros((kv_heads, new, head), BF16)
        buf[:, end:span, :] = jnp.zeros((kv_heads, span - end, head), BF16)

    for copy in small:
        copy.wait()
    column = iota((1, span), 1)
    row = jnp.where(column < win_at, column - sink_at, start + column - win_at)
    taken = jnp.zeros((1, span), jnp.bool_)
    for step in range(path_len):
        at = prefix + path_ref[0, step]
        taken = taken | ((row == at) & (step < accepted))
    old = (row < prefix) & ((row < SINK) | (row >= total - WIN))
    in_window = (column >= win_at) & (column < end) & (old | taken)
    in_sink = (column >= sink_at) & (column < win_at) & (row < SINK) & (row < prefix) & (start > 0)
    seen = jnp.where(in_window | in_sink, 0.0, NEG_FILL)
    mask_ref[...] = jnp.broadcast_to(seen, mask_ref.shape)

    down, across = iota((new, new), 0), iota((new, new), 1)
    eye = (down == across).astype(F32)
    back = eye + (down == parents_ref[...]).astype(F32)
    for _ in range((new - 1).bit_length()):
        half = back.astype(BF16)
        back = jnp.minimum(dot(half, half), 1.0)
    reach = dot_first(back.astype(BF16), eye.astype(BF16))
    tree = (kind_ref[0] == 1).astype(F32)
    causal = (across <= down).astype(F32)
    allowed = tree * reach + (1.0 - tree) * causal
    mask_ref[:, 0:new] = jnp.where(allowed > 0.5, 0.0, NEG_FILL)
    depth = tree * (jnp.sum(reach, axis=1, keepdims=True) - 1.0)
    depth = depth + (1.0 - tree) * iota((new, 1), 0).astype(F32)
    angle = (total.astype(F32) + depth) * freq_ref[...]
    lane = iota(angle.shape, 1)
    cosine, sine = jnp.cos(angle), jnp.sin(angle)
    sine = jnp.where(lane < head // 2, -sine, sine)
    for which, gain_ref in enumerate((q_gain_ref, k_gain_ref)):
        gain = jnp.broadcast_to(gain_ref[...], angle.shape)
        rot_ref[2 * which] = cosine * gain
        rot_ref[2 * which + 1] = sine * pltpu.roll(gain, head // 2, 1)

    all_tokens = ids_ref.shape[1]
    devices = hit_ref.shape[0]
    chips = devices // 2
    tokens = chips * new
    slot = iota((all_tokens, tokens), 1) // new
    source = (me ^ (2 * slot)) * new + iota((all_tokens, tokens), 1) % new
    order = (iota((all_tokens, tokens), 0) == source).astype(F32)
    ids = dot(ids_ref[...].astype(F32).astype(BF16), order.astype(BF16))
    gates = lax.dot_general(
        gates_ref[...],
        order,
        (((1,), (0,)), ((), ())),
        precision=lax.Precision.HIGHEST,
        preferred_element_type=F32,
    )
    for rel in range(devices):
        named = (ids == (me ^ rel).astype(F32)).astype(F32)
        hit_ref[rel : rel + 1, :] = jnp.max(named, axis=0, keepdims=True)
    before, later = iota((tokens, tokens), 0), iota((tokens, tokens), 1)
    earlier = (before < later) & (before // new == later // new)
    rank_ref[...] = dot(hit_ref[...].astype(BF16), earlier.astype(F32).astype(BF16))
    rows = chips * per
    slot_of = iota((rows, tokens), 1) // new
    row_slot = iota((rows, tokens), 0) // per
    row_rank = (iota((rows, tokens), 0) % per).astype(F32)
    in_first = iota((1, tokens), 1) < new
    for rel in range(devices):
        hit = hit_ref[rel : rel + 1, :] > 0.5
        rank = rank_ref[rel : rel + 1, :]
        chosen = (slot_of == (row_slot ^ (rel // 2))) & hit & (rank == row_rank)
        pick_ref[rel * rows : (rel + 1) * rows, :] = chosen.astype(F32)
        if rel < 2:
            named = ids == (me ^ rel).astype(F32)
            weight = jnp.sum(jnp.where(named, gates, 0.0), axis=0, keepdims=True)
            weight = jnp.sum(jnp.where(chosen, weight, 0.0), axis=1, keepdims=True)
            weight_ref[rel * rows : (rel + 1) * rows, :] = jnp.broadcast_to(
                weight, (rows, weight_ref.shape[1])
            )
        for place in range(per):
            at = rel * per + place
            own_ref[at : at + 1, :] = (in_first & hit & (rank == float(place))).astype(F32)
    first = (iota((tokens, new), 0) == iota((tokens, new), 1)).astype(F32)
    combine_ref[...] = lax.dot_general(
        first.astype(BF16),
        own_ref[...].astype(BF16),
        (((0,), (1,)), ((), ())),
        preferred_element_type=F32,
    )
    for copy in copies:
        copy.wait()


def project_kernel(chips, *refs):
    blocks = refs[:chips]
    gain_ref, wq_ref, wkv_ref, wq_sib, wkv_sib = refs[chips : chips + 5]
    outs = refs[chips + 7 : 2 * chips + 7]
    normed, wq_buf, wkv_buf, sems = refs[2 * chips + 9 :]
    copies = [
        pltpu.make_async_copy(wq_sib, wq_buf, sems.at[0]),
        pltpu.make_async_copy(wkv_sib, wkv_buf, sems.at[1]),
    ]
    for copy in copies:
        copy.start()
    rows = blocks[0].shape[0]
    gain = gain_ref[...]
    for j in range(chips):
        values = norm_rows(blocks[j][...].astype(F32)) * gain
        normed[j * rows : (j + 1) * rows, :] = values.astype(BF16)
    values = normed[...]

    def put(result, at):
        result = result.astype(BF16)
        for j in range(chips):
            outs[j][:, at : at + result.shape[1]] = result[j * rows : (j + 1) * rows]

    wide, narrow = wq_ref.shape[1], wkv_ref.shape[0]
    put(dot(values, wq_ref[...]), 0)
    put(dot_last(values, wkv_ref[...]), 2 * wide)
    for copy in copies:
        copy.wait()
    put(dot(values, wq_buf[...]), wide)
    put(dot_last(values, wkv_buf[...]), 2 * wide + narrow)


def attend_kernel(chips, q_width, kv_ready, *refs):
    got = refs[:chips]
    at = chips + 1 if kv_ready else chips
    keys_ref, values_ref, mask_ref, rot_ref = refs[at : at + 4]
    outs = refs[at + 8 : at + 8 + chips]
    fresh_ref = refs[chips] if kv_ready else refs[-1]
    me = lax.axis_index("tensor")
    chip = me // 2
    new = got[0].shape[0]
    kv_heads, span, head = keys_ref.shape
    per_chip = 2 * q_width // head
    group = chips * per_chip // kv_heads

    if not kv_ready:
        for rel in range(2 * chips):
            left = 2 * q_width + (rel % 2) * head
            fresh_ref[rel] = got[rel // 2][:, left : left + head]

    def rope(values, which):
        values = norm_rows(values.astype(F32))
        turned = pltpu.roll(values, head // 2, 1)
        return (values * rot_ref[2 * which] + turned * rot_ref[2 * which + 1]).astype(BF16)

    scale = head ** (-0.5) * LOG2E
    for j in range(chips):
        kv = (chip ^ j) * per_chip // group
        key_at, value_at = kv, kv + kv_heads
        if not kv_ready:
            key_at, value_at = me ^ key_at, me ^ value_at
        keys = jnp.concatenate([rope(fresh_ref[key_at], 1), keys_ref[kv, new:span]], axis=0)
        values = jnp.concatenate([fresh_ref[value_at], values_ref[kv, new:span]], axis=0)
        query = jnp.concatenate(
            [rope(got[j][:, h * head : (h + 1) * head], 0) for h in range(per_chip)], axis=0
        )
        score = dot_last(query, keys) * scale
        score = score.reshape(per_chip, new, span) + mask_ref[...][None]
        expo = jnp.exp2(score - jnp.max(score, axis=-1, keepdims=True))
        denom = jnp.sum(expo, axis=-1, keepdims=True).reshape(per_chip * new, 1)
        expo = expo.astype(BF16).reshape(per_chip * new, span)
        result = (dot(expo, values) / denom).astype(BF16)
        for h in range(per_chip):
            outs[j][:, h * head : (h + 1) * head] = result[h * new : (h + 1) * new]


def spread_kernel(chips, *refs):
    got = refs[:chips]
    pick_ref, w_ref, w_sib = refs[chips : chips + 3]
    outs = refs[chips + 3 : 2 * chips + 3]
    rows_ref, w_buf, sem = refs[2 * chips + 3 :]
    copy = pltpu.make_async_copy(w_sib, w_buf, sem.at[0])
    copy.start()
    new = got[0].shape[0]
    depth, width = w_ref.shape
    each = rows_ref.shape[1]
    heads = jnp.concatenate([got[j][...] for j in range(chips)], axis=0)
    picked = dot(pick_ref[...].astype(BF16), heads).astype(BF16)
    extra = each - new
    for j in range(chips):
        rows_ref[j, 0:new, :] = got[j][...]
        rows_ref[j, new:each, :] = picked[j * extra : (j + 1) * extra]
    left = rows_ref[...].reshape(chips * each, 2 * depth)
    copy.wait()
    tile = min(512, width)
    for at in range(0, width, tile):
        part = dot(left[:, :depth], w_ref[:, at : at + tile])
        part = (part + dot(left[:, depth:], w_buf[:, at : at + tile])).astype(BF16)
        for j in range(chips):
            outs[j][:, at : at + tile] = part[j * each : (j + 1) * each]


def fetch_kernel(chips, *refs):
    blocks = refs[:chips]
    pick_ref, _ = refs[chips : chips + 2]
    sources = refs[chips + 2 : chips + 4]
    picked_ref = refs[chips + 4]
    targets = refs[chips + 5 : chips + 7]
    sems = refs[-1]
    copies = [
        pltpu.make_async_copy(source, target, sems.at[which])
        for which, (source, target) in enumerate(zip(sources, targets))
    ]
    for copy in copies:
        copy.start()
    values = jnp.concatenate([block[...] for block in blocks], axis=0)
    pick = pick_ref[0 : picked_ref.shape[0], :].astype(BF16)
    picked_ref[...] = dot(pick, values)
    for copy in copies:
        copy.wait()


def expert_kernel(chips, per, *refs):
    got = refs[:chips]
    own_ref, picked_ref, weight_ref, gain_ref = refs[chips : chips + 4]
    weights = refs[chips + 4 : chips + 10]
    outs = refs[chips + 10 : 2 * chips + 10]
    hidden_ref = refs[2 * chips + 10]
    new = own_ref.shape[0]
    total = got[0][...].astype(F32)
    for j in range(1, chips):
        total = total + got[j][...].astype(F32)
    hidden_ref[...] = own_ref[...].astype(F32) + total[:new]
    hidden = picked_ref[...] + total[new:]
    normed = norm_rows(hidden) * gain_ref[...]
    rows = chips * per
    for core in range(2):
        gate_ref, up_ref, down_ref = weights[3 * core : 3 * core + 3]
        left = normed[core * rows : (core + 1) * rows].astype(BF16)
        gate = dot_last(left, gate_ref[0])
        up = dot_last(left, up_ref[0])
        inner = (gate / (1.0 + jnp.exp(-gate)) * up).astype(BF16)
        result = dot(inner, down_ref[0]) * weight_ref[core * rows : (core + 1) * rows, 0:1]
        result = result.astype(BF16)
        for j in range(chips):
            outs[j][core * per : (core + 1) * per, :] = result[j * per : (j + 1) * per]


def combine_kernel(chips, *refs):
    hidden_ref, combine_ref = refs[:2]
    got = refs[2 : 2 + chips]
    out_ref = refs[2 + chips]
    rows = jnp.concatenate([block[...].astype(F32) for block in got], axis=0)
    moe = dot(combine_ref[...].astype(BF16), rows.astype(BF16))
    out_ref[...] = (hidden_ref[...] + moe).astype(BF16)


def body(
    residual_in,
    attn_gain,
    w_query,
    w_keyval,
    query_gain,
    key_gain,
    w_out,
    ffn_gain,
    w_gate,
    w_up,
    w_down,
    key_cache,
    value_cache,
    prefix_lens,
    accepted,
    accept_path,
    parents,
    slot_kinds,
    expert_ids,
    gate_probs,
):
    devices = lax.axis_size("tensor")
    chips = devices // 2
    new, width = residual_in.shape
    head = query_gain.shape[0]
    kv_heads = key_cache.shape[2] // head
    q_width = w_query.shape[1]
    new_width = w_keyval.shape[0]
    all_tokens, top = expert_ids.shape
    tokens = chips * new
    per = new * top // EXPERTS
    path_len = accept_path.shape[1]
    rows = 2 * chips * per
    assert key_cache.shape[0] == 1 and w_gate.shape[0] == 1
    assert devices & (devices - 1) == 0
    vmem, smem, hbm, anywhere = pltpu.VMEM, pltpu.SMEM, pltpu.HBM, pl.ANY

    blocks = exchange([residual_in] * chips)
    wq_sib = hop(w_query, 1)
    wkv_sib = hop(w_keyval, 1)

    freq = ROPE_BASE ** (-2.0 * np.arange(head // 2) / head)
    freq = jnp.asarray(np.concatenate([freq, freq])[None, :], F32)
    span = -(-(new + 16 + window_rows(path_len)) // 128) * 128
    weights = [attn_gain[None, :], ffn_gain[None, :], w_query, w_keyval, w_out, w_gate]
    prepared = call(
        functools.partial(prep_kernel, path_len, per, len(weights)),
        "prep",
        [
            in_vmem((kv_heads, span, head), BF16),
            in_vmem((kv_heads, span, head), BF16),
            in_vmem((new, span), F32),
            in_vmem((4, new, head), F32),
            in_vmem((chips * rows, tokens), F32),
            in_vmem((new, devices * per), F32),
            in_vmem((rows, 128), F32),
        ]
        + [in_vmem(weight.shape, weight.dtype) for weight in weights],
        [
            (key_cache, hbm),
            (value_cache, hbm),
            (prefix_lens, smem),
            (accepted, smem),
            (slot_kinds, smem),
            (accept_path, hbm),
            (parents, hbm),
            (expert_ids.T, hbm),
            (gate_probs.T, hbm),
            (freq, hbm),
            (query_gain[None, :], hbm),
            (key_gain[None, :], hbm),
        ]
        + [(weight, hbm) for weight in weights],
        [
            pltpu.SMEM((1, path_len), jnp.int32),
            pltpu.VMEM((1, new), jnp.int32),
            pltpu.VMEM((top, all_tokens), jnp.int32),
            pltpu.VMEM((top, all_tokens), F32),
            pltpu.VMEM((1, head), F32),
            pltpu.VMEM((1, head), F32),
            pltpu.VMEM((1, head), F32),
            pltpu.VMEM((devices, tokens), F32),
            pltpu.VMEM((devices, tokens), F32),
            pltpu.VMEM((devices * per, tokens), F32),
            pltpu.SemaphoreType.DMA((7,)),
            pltpu.SemaphoreType.DMA((2, kv_heads, 2)),
            pltpu.SemaphoreType.DMA((len(weights),)),
        ],
        limit=16,
        moved=4 * span * kv_heads * head * 2,
    )
    keys, values, mask, rot, pick, combine, weight, gain, ffn, wq, wkv, wo, wg = prepared

    *projected, wo, wg = call(
        functools.partial(project_kernel, chips),
        "project",
        [in_vmem((new, 2 * (q_width + new_width)), BF16)] * chips
        + [in_vmem(w.shape, w.dtype) for w in (wo, wg)],
        [(block, vmem) for block in blocks]
        + [
            (gain, vmem),
            (wq, vmem),
            (wkv, vmem),
            (wq_sib, anywhere),
            (wkv_sib, anywhere),
            (wo, vmem),
            (wg, vmem),
        ],
        [
            pltpu.VMEM((tokens, width), BF16),
            pltpu.VMEM(w_query.shape, BF16),
            pltpu.VMEM(w_keyval.shape, BF16),
            pltpu.SemaphoreType.DMA((2,)),
        ],
        limit=16,
        same={chips + 5: chips, chips + 6: chips + 1},
        flops=4 * tokens * width * (q_width + new_width),
        moved=4 * width * (q_width + new_width),
    )
    wo_sib, wg_sib = hop(wo, 1), hop(wg, 1)

    got = exchange(projected)
    picked, wu, wd = call(
        functools.partial(fetch_kernel, chips),
        "fetch",
        [in_vmem((rows, width), F32)] + [in_vmem(w.shape, w.dtype) for w in (w_up, w_down)],
        [(block, vmem) for block in blocks]
        + [(pick, vmem), (projected[0], anywhere), (w_up, hbm), (w_down, hbm)],
        [pltpu.SemaphoreType.DMA((2,))],
        limit=8,
        flops=2 * rows * width * tokens,
        moved=8 * width * w_gate.shape[1],
    )
    kv_ready = []
    if new_width != head:
        pieces = [
            got[rel // 2][:, 2 * q_width + (rel % 2) * new_width :][:, :new_width]
            for rel in range(devices)
        ]
        pieces = jnp.stack(pieces)[lax.axis_index("tensor") ^ jnp.arange(devices)]
        pieces = pieces.transpose(1, 0, 2).reshape(new, 2 * kv_heads, head)
        kv_ready = [(pieces.transpose(1, 0, 2), vmem)]
    at = chips + len(kv_ready) + 6
    *attended, wu, wd = call(
        functools.partial(attend_kernel, chips, q_width, bool(kv_ready)),
        "attend",
        [in_vmem((new, 2 * q_width), BF16)] * chips
        + [in_vmem(w.shape, w.dtype) for w in (wu, wd)],
        [(block, vmem) for block in got]
        + kv_ready
        + [(keys, vmem), (values, vmem), (mask, vmem), (rot, vmem)]
        + [(wo_sib, anywhere), (wg_sib, anywhere), (wu, vmem), (wd, vmem)],
        [] if kv_ready else [pltpu.VMEM((devices, new, head), BF16)],
        limit=16,
        same={at: chips, at + 1: chips + 1},
        flops=8 * new * chips * q_width * span,
        moved=4 * span * kv_heads * head,
    )
    wu_sib, wd_sib = hop(wu, 1), hop(wd, 1)
    heads = exchange(attended)

    partial = call(
        functools.partial(spread_kernel, chips),
        "spread",
        [in_vmem((new + rows, width), BF16)] * chips,
        [(block, vmem) for block in heads] + [(pick, vmem), (wo, vmem), (wo_sib, anywhere)],
        [
            pltpu.VMEM((chips, new + rows, 2 * q_width), BF16),
            pltpu.VMEM(w_out.shape, BF16),
            pltpu.SemaphoreType.DMA((1,)),
        ],
        limit=16,
        flops=4 * chips * (new + rows) * width * q_width,
        moved=4 * q_width * width,
    )
    partials = exchange(partial)
    results = call(
        functools.partial(expert_kernel, chips, per),
        "expert",
        [in_vmem((2 * per, width), BF16)] * chips + [in_vmem((new, width), F32)],
        [(block, vmem) for block in partials]
        + [(residual_in, vmem), (picked, vmem), (weight, vmem), (ffn, vmem)]
        + [(w, vmem) for w in (wg, wu, wd, wg_sib, wu_sib, wd_sib)],
        limit=16,
        flops=12 * rows * width * w_gate.shape[1],
        moved=12 * width * w_gate.shape[1],
    )
    hidden = results[chips]
    returned = exchange(results[:chips])
    return call(
        functools.partial(combine_kernel, chips),
        "combine",
        [jax.ShapeDtypeStruct((new, width), BF16)],
        [(hidden, vmem), (combine, vmem)] + [(block, vmem) for block in returned],
        limit=8,
        moved=6 * new * width,
    )[0]


def solution(mesh):
    in_specs = (
        P(("group", "tensor"), None),
        P(),
        P(None, "tensor"),
        P("tensor", None),
        P(),
        P(),
        P("tensor", None),
        P(),
        P("tensor", None, None),
        P("tensor", None, None),
        P("tensor", None, None),
        P(("group", "tensor"), None, None),
        P(("group", "tensor"), None, None),
        P(("group", "tensor")),
        P(("group", "tensor")),
        P(("group", "tensor"), None),
        P(("group", "tensor"), None),
        P(("group", "tensor")),
        P("group", None),
        P("group", None),
    )
    out_specs = P(("group", "tensor"), None)
    return jax.shard_map(body, mesh=mesh, in_specs=in_specs, out_specs=out_specs, check_vma=False)
```

```python
import functools
import math

import jax
import jax.numpy as jnp
import numpy as np
from jax import lax
from jax.experimental import pallas as pl
from jax.experimental.pallas import tpu as pltpu
from jax.sharding import PartitionSpec as P

EXPERTS = 128
SINK = 4
WIN = 512

EPSILON = 1e-06
NEG_FILL = -1e30
ROPE_BASE = 1000000.0
LOG2E = math.log2(math.e)
F32 = jnp.float32
BF16 = jnp.bfloat16
MIB = 1 << 20


def iota(shape, dim):
    return lax.broadcasted_iota(jnp.int32, shape, dim)


def dot(left, right):
    return jnp.dot(left, right, preferred_element_type=F32)


def dot_last(left, right):
    return lax.dot_general(left, right, (((1,), (1,)), ((), ())), preferred_element_type=F32)


def dot_first(left, right):
    return lax.dot_general(left, right, (((0,), (0,)), ((), ())), preferred_element_type=F32)


def norm_rows(values):
    return values * lax.rsqrt(jnp.mean(values * values, axis=-1, keepdims=True) + EPSILON)


def in_vmem(shape, dtype):
    return pltpu.VMEM(shape, dtype)


def call(kernel, name, outs, args, scratch=(), limit=16, flops=0, moved=0, same=None):
    arrays = []
    specs = []
    for array, space in args:
        if space is pltpu.HBM or space is pltpu.VMEM:
            array = pltpu.with_memory_space_constraint(array, space)
        arrays.append(array)
        specs.append(pl.BlockSpec(memory_space=space))
    return pl.pallas_call(
        kernel,
        out_shape=outs,
        in_specs=specs,
        out_specs=[pl.BlockSpec(memory_space=pltpu.VMEM) for _ in outs],
        scratch_shapes=list(scratch),
        input_output_aliases=same or {},
        compiler_params=pltpu.CompilerParams(vmem_limit_bytes=limit * MIB),
        cost_estimate=pl.CostEstimate(flops=flops, bytes_accessed=moved, transcendentals=0),
        name=name,
    )(*arrays)


def hop(value, step):
    devices = lax.axis_size("tensor")
    return lax.ppermute(value, "tensor", [(i, i ^ step) for i in range(devices)])


def exchange(blocks):
    return [blocks[0]] + [hop(blocks[j], 2 * j) for j in range(1, len(blocks))]


def window_rows(path_len):
    return -(-(WIN + 2 * (path_len - 1) + 16) // 16) * 16


def prep_kernel(path_len, per, n_weights, *refs):
    key_cache, value_cache, prefix_ref, accepted_ref, kind_ref = refs[:5]
    small_in = refs[5:12]
    sources = refs[12 : 12 + n_weights]
    refs = refs[12 + n_weights :]
    keys_ref, values_ref, mask_ref, rot_ref, pick_ref, combine_ref, weight_ref = refs[:7]
    targets = refs[7 : 7 + n_weights]
    refs = refs[7 + n_weights :]
    path_ref, parents_ref, ids_ref, gates_ref, freq_ref, q_gain_ref, k_gain_ref = refs[:7]
    hit_ref, rank_ref, own_ref, small_sems, cache_sems, weight_sems = refs[7:]

    me = lax.axis_index("tensor")
    new = mask_ref.shape[0]
    kv_heads, span, head = keys_ref.shape
    cache_len = key_cache.shape[1]
    wide = window_rows(path_len)
    sink_at, win_at = new, new + 16
    end = win_at + wide

    small = [
        pltpu.make_async_copy(source, target, small_sems.at[which])
        for which, (source, target) in enumerate(zip(small_in, refs[:7]))
    ]
    for copy in small:
        copy.start()
    prefix = prefix_ref[0]
    accepted = accepted_ref[0]
    total = prefix + accepted
    low = jnp.maximum(total - WIN, 0)
    start = pl.multiple_of(jnp.minimum((low // 16) * 16, cache_len - wide), 16)
    copies = []
    for which, (cache, buf) in enumerate(((key_cache, keys_ref), (value_cache, values_ref))):
        for kv in range(kv_heads):
            cols = pl.ds(kv * head, head)
            copies.append(
                pltpu.make_async_copy(
                    cache.at[0, pl.ds(start, wide), cols],
                    buf.at[kv, pl.ds(win_at, wide)],
                    cache_sems.at[which, kv, 0],
                )
            )
            copies.append(
                pltpu.make_async_copy(
                    cache.at[0, pl.ds(0, 16), cols],
                    buf.at[kv, pl.ds(sink_at, 16)],
                    cache_sems.at[which, kv, 1],
                )
            )
    for which, (source, target) in enumerate(zip(sources, targets)):
        copies.append(pltpu.make_async_copy(source, target, weight_sems.at[which]))
    for copy in copies:
        copy.start()

    for buf in (keys_ref, values_ref):
        buf[:, 0:new, :] = jnp.zeros((kv_heads, new, head), BF16)
        buf[:, end:span, :] = jnp.zeros((kv_heads, span - end, head), BF16)

    for copy in small:
        copy.wait()
    column = iota((1, span), 1)
    row = jnp.where(column < win_at, column - sink_at, start + column - win_at)
    taken = jnp.zeros((1, span), jnp.bool_)
    for step in range(path_len):
        at = prefix + path_ref[0, step]
        taken = taken | ((row == at) & (step < accepted))
    old = (row < prefix) & ((row < SINK) | (row >= total - WIN))
    in_window = (column >= win_at) & (column < end) & (old | taken)
    in_sink = (column >= sink_at) & (column < win_at) & (row < SINK) & (row < prefix) & (start > 0)
    seen = jnp.where(in_window | in_sink, 0.0, NEG_FILL)
    mask_ref[...] = jnp.broadcast_to(seen, mask_ref.shape)

    down, across = iota((new, new), 0), iota((new, new), 1)
    eye = (down == across).astype(F32)
    back = eye + (down == parents_ref[...]).astype(F32)
    for _ in range((new - 1).bit_length()):
        half = back.astype(BF16)
        back = jnp.minimum(dot(half, half), 1.0)
    reach = dot_first(back.astype(BF16), eye.astype(BF16))
    tree = (kind_ref[0] == 1).astype(F32)
    causal = (across <= down).astype(F32)
    allowed = tree * reach + (1.0 - tree) * causal
    mask_ref[:, 0:new] = jnp.where(allowed > 0.5, 0.0, NEG_FILL)
    depth = tree * (jnp.sum(reach, axis=1, keepdims=True) - 1.0)
    depth = depth + (1.0 - tree) * iota((new, 1), 0).astype(F32)
    angle = (total.astype(F32) + depth) * freq_ref[...]
    lane = iota(angle.shape, 1)
    cosine, sine = jnp.cos(angle), jnp.sin(angle)
    sine = jnp.where(lane < head // 2, -sine, sine)
    for which, gain_ref in enumerate((q_gain_ref, k_gain_ref)):
        gain = jnp.broadcast_to(gain_ref[...], angle.shape)
        rot_ref[2 * which] = cosine * gain
        rot_ref[2 * which + 1] = sine * pltpu.roll(gain, head // 2, 1)

    all_tokens = ids_ref.shape[1]
    devices = hit_ref.shape[0]
    chips = devices // 2
    tokens = chips * new
    slot = iota((all_tokens, tokens), 1) // new
    source = (me ^ (2 * slot)) * new + iota((all_tokens, tokens), 1) % new
    order = (iota((all_tokens, tokens), 0) == source).astype(F32)
    ids = dot(ids_ref[...].astype(F32).astype(BF16), order.astype(BF16))
    gates = lax.dot_general(
        gates_ref[...],
        order,
        (((1,), (0,)), ((), ())),
        precision=lax.Precision.HIGHEST,
        preferred_element_type=F32,
    )
    for rel in range(devices):
        named = (ids == (me ^ rel).astype(F32)).astype(F32)
        hit_ref[rel : rel + 1, :] = jnp.max(named, axis=0, keepdims=True)
    before, later = iota((tokens, tokens), 0), iota((tokens, tokens), 1)
    earlier = (before < later) & (before // new == later // new)
    rank_ref[...] = dot(hit_ref[...].astype(BF16), earlier.astype(F32).astype(BF16))
    rows = chips * per
    slot_of = iota((rows, tokens), 1) // new
    row_slot = iota((rows, tokens), 0) // per
    row_rank = (iota((rows, tokens), 0) % per).astype(F32)
    in_first = iota((1, tokens), 1) < new
    for rel in range(devices):
        hit = hit_ref[rel : rel + 1, :] > 0.5
        rank = rank_ref[rel : rel + 1, :]
        chosen = (slot_of == (row_slot ^ (rel // 2))) & hit & (rank == row_rank)
        pick_ref[rel * rows : (rel + 1) * rows, :] = chosen.astype(F32)
        if rel < 2:
            named = ids == (me ^ rel).astype(F32)
            weight = jnp.sum(jnp.where(named, gates, 0.0), axis=0, keepdims=True)
            weight = jnp.sum(jnp.where(chosen, weight, 0.0), axis=1, keepdims=True)
            weight_ref[rel * rows : (rel + 1) * rows, :] = jnp.broadcast_to(
                weight, (rows, weight_ref.shape[1])
            )
        for place in range(per):
            at = rel * per + place
            own_ref[at : at + 1, :] = (in_first & hit & (rank == float(place))).astype(F32)
    first = (iota((tokens, new), 0) == iota((tokens, new), 1)).astype(F32)
    combine_ref[...] = lax.dot_general(
        first.astype(BF16),
        own_ref[...].astype(BF16),
        (((0,), (1,)), ((), ())),
        preferred_element_type=F32,
    )
    for copy in copies:
        copy.wait()


def project_kernel(chips, *refs):
    blocks = refs[:chips]
    gain_ref, wq_ref, wkv_ref, wq_sib, wkv_sib, _ = refs[chips : chips + 6]
    outs = refs[chips + 6 : 2 * chips + 6]
    normed = refs[-1]
    rows = blocks[0].shape[0]
    gain = gain_ref[...]
    for j in range(chips):
        values = norm_rows(blocks[j][...].astype(F32)) * gain
        normed[j * rows : (j + 1) * rows, :] = values.astype(BF16)
    values = normed[...]

    def put(result, at):
        result = result.astype(BF16)
        for j in range(chips):
            outs[j][:, at : at + result.shape[1]] = result[j * rows : (j + 1) * rows]

    wide, narrow = wq_ref.shape[1], wkv_ref.shape[0]
    put(dot(values, wq_ref[...]), 0)
    put(dot(values, wq_sib[...]), wide)
    put(dot_last(values, wkv_ref[...]), 2 * wide)
    put(dot_last(values, wkv_sib[...]), 2 * wide + narrow)


def attend_kernel(chips, q_width, kv_ready, *refs):
    got = refs[:chips]
    at = chips + 1 if kv_ready else chips
    keys_ref, values_ref, mask_ref, rot_ref = refs[at : at + 4]
    outs = refs[at + 6 : at + 6 + chips]
    fresh_ref = refs[chips] if kv_ready else refs[-1]
    me = lax.axis_index("tensor")
    chip = me // 2
    new = got[0].shape[0]
    kv_heads, span, head = keys_ref.shape
    per_chip = 2 * q_width // head
    group = chips * per_chip // kv_heads

    if not kv_ready:
        for rel in range(2 * chips):
            left = 2 * q_width + (rel % 2) * head
            fresh_ref[rel] = got[rel // 2][:, left : left + head]

    def rope(values, which):
        values = norm_rows(values.astype(F32))
        turned = pltpu.roll(values, head // 2, 1)
        return (values * rot_ref[2 * which] + turned * rot_ref[2 * which + 1]).astype(BF16)

    scale = head ** (-0.5) * LOG2E
    for j in range(chips):
        kv = (chip ^ j) * per_chip // group
        key_at, value_at = kv, kv + kv_heads
        if not kv_ready:
            key_at, value_at = me ^ key_at, me ^ value_at
        keys = jnp.concatenate([rope(fresh_ref[key_at], 1), keys_ref[kv, new:span]], axis=0)
        values = jnp.concatenate([fresh_ref[value_at], values_ref[kv, new:span]], axis=0)
        query = jnp.concatenate(
            [rope(got[j][:, h * head : (h + 1) * head], 0) for h in range(per_chip)], axis=0
        )
        score = dot_last(query, keys) * scale
        score = score.reshape(per_chip, new, span) + mask_ref[...][None]
        expo = jnp.exp2(score - jnp.max(score, axis=-1, keepdims=True))
        denom = jnp.sum(expo, axis=-1, keepdims=True).reshape(per_chip * new, 1)
        expo = expo.astype(BF16).reshape(per_chip * new, span)
        result = (dot(expo, values) / denom).astype(BF16)
        for h in range(per_chip):
            outs[j][:, h * head : (h + 1) * head] = result[h * new : (h + 1) * new]


def spread_kernel(chips, *refs):
    got = refs[:chips]
    pick_ref, w_ref, w_sib = refs[chips : chips + 3]
    outs = refs[chips + 6 : 2 * chips + 6]
    rows_ref = refs[-1]
    new = got[0].shape[0]
    depth, width = w_ref.shape
    each = rows_ref.shape[1]
    heads = jnp.concatenate([got[j][...] for j in range(chips)], axis=0)
    picked = dot(pick_ref[...].astype(BF16), heads).astype(BF16)
    extra = each - new
    for j in range(chips):
        rows_ref[j, 0:new, :] = got[j][...]
        rows_ref[j, new:each, :] = picked[j * extra : (j + 1) * extra]
    left = rows_ref[...].reshape(chips * each, 2 * depth)
    tile = min(512, width)
    for at in range(0, width, tile):
        part = dot(left[:, :depth], w_ref[:, at : at + tile])
        part = (part + dot(left[:, depth:], w_sib[:, at : at + tile])).astype(BF16)
        for j in range(chips):
            outs[j][:, at : at + tile] = part[j * each : (j + 1) * each]


def fetch_kernel(_, up_in, down_in, up_out, down_out, sems):
    copies = [
        pltpu.make_async_copy(up_in, up_out, sems.at[0]),
        pltpu.make_async_copy(down_in, down_out, sems.at[1]),
    ]
    for copy in copies:
        copy.start()
    for copy in copies:
        copy.wait()


def select_kernel(chips, *refs):
    blocks = refs[:chips]
    pick_ref, _ = refs[chips : chips + 2]
    sources = refs[chips + 2 : chips + 3]
    picked_ref = refs[chips + 3]
    targets = refs[chips + 4 : chips + 5]
    sems = refs[-1]
    copies = [
        pltpu.make_async_copy(source, target, sems.at[which])
        for which, (source, target) in enumerate(zip(sources, targets))
    ]
    for copy in copies:
        copy.start()
    values = jnp.concatenate([block[...] for block in blocks], axis=0)
    pick = pick_ref[0 : picked_ref.shape[0], :].astype(BF16)
    picked_ref[...] = dot(pick, values)
    for copy in copies:
        copy.wait()


def hidden_kernel(chips, *refs):
    got = refs[:chips]
    own_ref, out_ref = refs[chips:]
    new = own_ref.shape[0]
    total = own_ref[...].astype(F32)
    for j in range(chips):
        total = total + got[j][0:new, :].astype(F32)
    out_ref[...] = total


def expert_kernel(chips, per, *refs):
    got = refs[:chips]
    picked_ref, weight_ref, gain_ref = refs[chips : chips + 3]
    weights = refs[chips + 3 : chips + 9]
    outs = refs[chips + 9 :]
    rows = chips * per
    hidden = picked_ref[...]
    new = got[0].shape[0] - 2 * rows
    for j in range(chips):
        hidden = hidden + got[j][new:, :].astype(F32)
    normed = norm_rows(hidden) * gain_ref[...]
    for core in range(2):
        gate_ref, up_ref, down_ref = weights[3 * core : 3 * core + 3]
        right = normed[core * rows : (core + 1) * rows].astype(BF16)
        gate = dot_last(gate_ref[0], right)
        up = dot_last(up_ref[0], right)
        inner = (gate / (1.0 + jnp.exp(-gate)) * up).astype(BF16)
        result = dot_first(inner, down_ref[0])
        result = (result * weight_ref[core * rows : (core + 1) * rows, 0:1]).astype(BF16)
        for j in range(chips):
            outs[j][core * per : (core + 1) * per, :] = result[j * per : (j + 1) * per]


def combine_kernel(chips, *refs):
    hidden_ref, combine_ref = refs[:2]
    got = refs[2 : 2 + chips]
    out_ref = refs[2 + chips]
    rows = jnp.concatenate([block[...].astype(F32) for block in got], axis=0)
    moe = dot(combine_ref[...].astype(BF16), rows.astype(BF16))
    out_ref[...] = (hidden_ref[...] + moe).astype(BF16)


def body(
    residual_in,
    attn_gain,
    w_query,
    w_keyval,
    query_gain,
    key_gain,
    w_out,
    ffn_gain,
    w_gate,
    w_up,
    w_down,
    key_cache,
    value_cache,
    prefix_lens,
    accepted,
    accept_path,
    parents,
    slot_kinds,
    expert_ids,
    gate_probs,
):
    devices = lax.axis_size("tensor")
    chips = devices // 2
    new, width = residual_in.shape
    head = query_gain.shape[0]
    kv_heads = key_cache.shape[2] // head
    q_width = w_query.shape[1]
    new_width = w_keyval.shape[0]
    all_tokens, top = expert_ids.shape
    tokens = chips * new
    per = new * top // EXPERTS
    path_len = accept_path.shape[1]
    rows = 2 * chips * per
    assert key_cache.shape[0] == 1 and w_gate.shape[0] == 1
    assert devices & (devices - 1) == 0
    vmem, smem, hbm, anywhere = pltpu.VMEM, pltpu.SMEM, pltpu.HBM, pl.ANY

    blocks = exchange([residual_in] * chips)
    wq_sib = hop(w_query, 1)
    wkv_sib = hop(w_keyval, 1)

    freq = ROPE_BASE ** (-2.0 * np.arange(head // 2) / head)
    freq = jnp.asarray(np.concatenate([freq, freq])[None, :], F32)
    span = -(-(new + 16 + window_rows(path_len)) // 128) * 128
    weights = [attn_gain[None, :], ffn_gain[None, :], w_query, w_keyval, w_out]
    prepared = call(
        functools.partial(prep_kernel, path_len, per, len(weights)),
        "prep",
        [
            in_vmem((kv_heads, span, head), BF16),
            in_vmem((kv_heads, span, head), BF16),
            in_vmem((new, span), F32),
            in_vmem((4, new, head), F32),
            in_vmem((chips * rows, tokens), F32),
            in_vmem((new, devices * per), F32),
            in_vmem((rows, 128), F32),
        ]
        + [in_vmem(weight.shape, weight.dtype) for weight in weights],
        [
            (key_cache, hbm),
            (value_cache, hbm),
            (prefix_lens, smem),
            (accepted, smem),
            (slot_kinds, smem),
            (accept_path, hbm),
            (parents, hbm),
            (expert_ids.T, hbm),
            (gate_probs.T, hbm),
            (freq, hbm),
            (query_gain[None, :], hbm),
            (key_gain[None, :], hbm),
        ]
        + [(weight, hbm) for weight in weights],
        [
            pltpu.SMEM((1, path_len), jnp.int32),
            pltpu.VMEM((1, new), jnp.int32),
            pltpu.VMEM((top, all_tokens), jnp.int32),
            pltpu.VMEM((top, all_tokens), F32),
            pltpu.VMEM((1, head), F32),
            pltpu.VMEM((1, head), F32),
            pltpu.VMEM((1, head), F32),
            pltpu.VMEM((devices, tokens), F32),
            pltpu.VMEM((devices, tokens), F32),
            pltpu.VMEM((devices * per, tokens), F32),
            pltpu.SemaphoreType.DMA((7,)),
            pltpu.SemaphoreType.DMA((2, kv_heads, 2)),
            pltpu.SemaphoreType.DMA((len(weights),)),
        ],
        limit=16,
        moved=4 * span * kv_heads * head * 2,
    )
    keys, values, mask, rot, pick, combine, weight, gain, ffn, wq, wkv, wo = prepared

    *projected, wo = call(
        functools.partial(project_kernel, chips),
        "project",
        [in_vmem((new, 2 * (q_width + new_width)), BF16)] * chips
        + [in_vmem(wo.shape, wo.dtype)],
        [(block, vmem) for block in blocks]
        + [
            (gain, vmem),
            (wq, vmem),
            (wkv, vmem),
            (wq_sib, vmem),
            (wkv_sib, vmem),
            (wo, vmem),
        ],
        [pltpu.VMEM((tokens, width), BF16)],
        limit=16,
        same={chips + 5: chips},
        flops=4 * tokens * width * (q_width + new_width),
        moved=4 * width * (q_width + new_width),
    )
    wo_sib = hop(wo, 1)

    got = exchange(projected)
    picked, wg = call(
        functools.partial(select_kernel, chips),
        "select",
        [in_vmem((rows, width), F32)] + [in_vmem(w.shape, w.dtype) for w in (w_gate,)],
        [(block, vmem) for block in blocks]
        + [(pick, vmem), (projected[0], anywhere), (w_gate, hbm)],
        [pltpu.SemaphoreType.DMA((2,))],
        limit=8,
        flops=2 * rows * width * tokens,
        moved=8 * width * w_gate.shape[1],
    )
    kv_ready = []
    if new_width != head:
        pieces = [
            got[rel // 2][:, 2 * q_width + (rel % 2) * new_width :][:, :new_width]
            for rel in range(devices)
        ]
        pieces = jnp.stack(pieces)[lax.axis_index("tensor") ^ jnp.arange(devices)]
        pieces = pieces.transpose(1, 0, 2).reshape(new, 2 * kv_heads, head)
        kv_ready = [(pieces.transpose(1, 0, 2), vmem)]
    at = chips + len(kv_ready) + 5
    *attended, wg = call(
        functools.partial(attend_kernel, chips, q_width, bool(kv_ready)),
        "attend",
        [in_vmem((new, 2 * q_width), BF16)] * chips
        + [in_vmem(w.shape, w.dtype) for w in (wg,)],
        [(block, vmem) for block in got]
        + kv_ready
        + [(keys, vmem), (values, vmem), (mask, vmem), (rot, vmem)]
        + [(wo_sib, anywhere), (wg, vmem)],
        [] if kv_ready else [pltpu.VMEM((devices, new, head), BF16)],
        limit=16,
        same={at: chips},
        flops=8 * new * chips * q_width * span,
        moved=4 * span * kv_heads * head,
    )
    wg_sib = hop(wg, 1)
    heads = exchange(attended)
    wu, wd = call(
        fetch_kernel,
        "fetch",
        [in_vmem(w.shape, w.dtype) for w in (w_up, w_down)],
        [(attended[0], anywhere), (w_up, hbm), (w_down, hbm)],
        [pltpu.SemaphoreType.DMA((2,))],
        limit=8,
        moved=8 * width * w_gate.shape[1],
    )

    *partial, wu, wd = call(
        functools.partial(spread_kernel, chips),
        "spread",
        [in_vmem((new + rows, width), BF16)] * chips
        + [in_vmem(w.shape, w.dtype) for w in (wu, wd)],
        [(block, vmem) for block in heads]
        + [(pick, vmem), (wo, vmem), (wo_sib, vmem), (wg_sib, anywhere), (wu, vmem), (wd, vmem)],
        [pltpu.VMEM((chips, new + rows, 2 * q_width), BF16)],
        same={chips + 4: chips, chips + 5: chips + 1},
        limit=16,
        flops=4 * chips * (new + rows) * width * q_width,
        moved=4 * q_width * width,
    )
    wu_sib, wd_sib = hop(wu, 1), hop(wd, 1)
    partials = exchange(partial)
    results = call(
        functools.partial(expert_kernel, chips, per),
        "expert",
        [in_vmem((2 * per, width), BF16)] * chips,
        [(block, vmem) for block in partials]
        + [(picked, vmem), (weight, vmem), (ffn, vmem)]
        + [(w, vmem) for w in (wg, wu, wd, wg_sib, wu_sib, wd_sib)],
        limit=16,
        flops=12 * rows * width * w_gate.shape[1],
        moved=12 * width * w_gate.shape[1],
    )
    returned = exchange(results)
    hidden = call(
        functools.partial(hidden_kernel, chips),
        "hidden",
        [in_vmem((new, width), F32)],
        [(block, vmem) for block in partials] + [(residual_in, vmem)],
        limit=8,
        moved=2 * chips * new * width,
    )[0]
    return call(
        functools.partial(combine_kernel, chips),
        "combine",
        [jax.ShapeDtypeStruct((new, width), BF16)],
        [(hidden, vmem), (combine, vmem)] + [(block, vmem) for block in returned],
        limit=8,
        moved=6 * new * width,
    )[0]


def solution(mesh):
    in_specs = (
        P(("group", "tensor"), None),
        P(),
        P(None, "tensor"),
        P("tensor", None),
        P(),
        P(),
        P("tensor", None),
        P(),
        P("tensor", None, None),
        P("tensor", None, None),
        P("tensor", None, None),
        P(("group", "tensor"), None, None),
        P(("group", "tensor"), None, None),
        P(("group", "tensor")),
        P(("group", "tensor")),
        P(("group", "tensor"), None),
        P(("group", "tensor"), None),
        P(("group", "tensor")),
        P("group", None),
        P("group", None),
    )
    out_specs = P(("group", "tensor"), None)
    return jax.shard_map(body, mesh=mesh, in_specs=in_specs, out_specs=out_specs, check_vma=False)
```

```python
import functools
import math

import jax
import jax.numpy as jnp
import numpy as np
from jax import lax
from jax.experimental import pallas as pl
from jax.experimental.pallas import tpu as pltpu
from jax.sharding import PartitionSpec as P

EXPERTS = 128
SINK = 4
WIN = 512

EPSILON = 1e-06
NEG_FILL = -1e30
ROPE_BASE = 1000000.0
LOG2E = math.log2(math.e)
F32 = jnp.float32
BF16 = jnp.bfloat16
MIB = 1 << 20


def iota(shape, dim):
    return lax.broadcasted_iota(jnp.int32, shape, dim)


def dot(left, right):
    return jnp.dot(left, right, preferred_element_type=F32)


def dot_last(left, right):
    return lax.dot_general(left, right, (((1,), (1,)), ((), ())), preferred_element_type=F32)


def dot_first(left, right):
    return lax.dot_general(left, right, (((0,), (0,)), ((), ())), preferred_element_type=F32)


def norm_rows(values):
    return values * lax.rsqrt(jnp.mean(values * values, axis=-1, keepdims=True) + EPSILON)


def in_vmem(shape, dtype):
    return pltpu.VMEM(shape, dtype)


def call(kernel, name, outs, args, scratch=(), limit=16, flops=0, moved=0, same=None):
    arrays = []
    specs = []
    for array, space in args:
        if space is pltpu.HBM or space is pltpu.VMEM:
            array = pltpu.with_memory_space_constraint(array, space)
        arrays.append(array)
        specs.append(pl.BlockSpec(memory_space=space))
    return pl.pallas_call(
        kernel,
        out_shape=outs,
        in_specs=specs,
        out_specs=[pl.BlockSpec(memory_space=pltpu.VMEM) for _ in outs],
        scratch_shapes=list(scratch),
        input_output_aliases=same or {},
        compiler_params=pltpu.CompilerParams(vmem_limit_bytes=limit * MIB),
        cost_estimate=pl.CostEstimate(flops=flops, bytes_accessed=moved, transcendentals=0),
        name=name,
    )(*arrays)


def hop(value, step):
    devices = lax.axis_size("tensor")
    return lax.ppermute(value, "tensor", [(i, i ^ step) for i in range(devices)])


def exchange(blocks):
    return [blocks[0]] + [hop(blocks[j], 2 * j) for j in range(1, len(blocks))]


def window_rows(path_len):
    return -(-(WIN + 2 * (path_len - 1) + 16) // 16) * 16


def prep_kernel(path_len, per, n_weights, *refs):
    key_cache, value_cache, prefix_ref, accepted_ref, kind_ref = refs[:5]
    small_in = refs[5:12]
    sources = refs[12 : 12 + n_weights]
    refs = refs[12 + n_weights :]
    keys_ref, values_ref, mask_ref, rot_ref, pick_ref, combine_ref, weight_ref = refs[:7]
    targets = refs[7 : 7 + n_weights]
    refs = refs[7 + n_weights :]
    path_ref, parents_ref, ids_ref, gates_ref, freq_ref, q_gain_ref, k_gain_ref = refs[:7]
    hit_ref, rank_ref, own_ref, small_sems, cache_sems, weight_sems = refs[7:]

    me = lax.axis_index("tensor")
    new = mask_ref.shape[0]
    kv_heads, span, head = keys_ref.shape
    cache_len = key_cache.shape[1]
    wide = window_rows(path_len)
    sink_at, win_at = new, new + 16
    end = win_at + wide

    small = [
        pltpu.make_async_copy(source, target, small_sems.at[which])
        for which, (source, target) in enumerate(zip(small_in, refs[:7]))
    ]
    for copy in small:
        copy.start()
    prefix = prefix_ref[0]
    accepted = accepted_ref[0]
    total = prefix + accepted
    low = jnp.maximum(total - WIN, 0)
    start = pl.multiple_of(jnp.minimum((low // 16) * 16, cache_len - wide), 16)
    copies = []
    for which, (cache, buf) in enumerate(((key_cache, keys_ref), (value_cache, values_ref))):
        for kv in range(kv_heads):
            cols = pl.ds(kv * head, head)
            copies.append(
                pltpu.make_async_copy(
                    cache.at[0, pl.ds(start, wide), cols],
                    buf.at[kv, pl.ds(win_at, wide)],
                    cache_sems.at[which, kv, 0],
                )
            )
            copies.append(
                pltpu.make_async_copy(
                    cache.at[0, pl.ds(0, 16), cols],
                    buf.at[kv, pl.ds(sink_at, 16)],
                    cache_sems.at[which, kv, 1],
                )
            )
    for which, (source, target) in enumerate(zip(sources, targets)):
        copies.append(pltpu.make_async_copy(source, target, weight_sems.at[which]))
    for copy in copies:
        copy.start()

    for buf in (keys_ref, values_ref):
        buf[:, 0:new, :] = jnp.zeros((kv_heads, new, head), BF16)
        buf[:, end:span, :] = jnp.zeros((kv_heads, span - end, head), BF16)

    for copy in small:
        copy.wait()
    column = iota((1, span), 1)
    row = jnp.where(column < win_at, column - sink_at, start + column - win_at)
    taken = jnp.zeros((1, span), jnp.bool_)
    for step in range(path_len):
        at = prefix + path_ref[0, step]
        taken = taken | ((row == at) & (step < accepted))
    old = (row < prefix) & ((row < SINK) | (row >= total - WIN))
    in_window = (column >= win_at) & (column < end) & (old | taken)
    in_sink = (column >= sink_at) & (column < win_at) & (row < SINK) & (row < prefix) & (start > 0)
    seen = jnp.where(in_window | in_sink, 0.0, NEG_FILL)
    mask_ref[...] = jnp.broadcast_to(seen, mask_ref.shape)

    down, across = iota((new, new), 0), iota((new, new), 1)
    eye = (down == across).astype(F32)
    back = eye + (down == parents_ref[...]).astype(F32)
    for _ in range((new - 1).bit_length()):
        half = back.astype(BF16)
        back = jnp.minimum(dot(half, half), 1.0)
    reach = dot_first(back.astype(BF16), eye.astype(BF16))
    tree = (kind_ref[0] == 1).astype(F32)
    causal = (across <= down).astype(F32)
    allowed = tree * reach + (1.0 - tree) * causal
    mask_ref[:, 0:new] = jnp.where(allowed > 0.5, 0.0, NEG_FILL)
    depth = tree * (jnp.sum(reach, axis=1, keepdims=True) - 1.0)
    depth = depth + (1.0 - tree) * iota((new, 1), 0).astype(F32)
    angle = (total.astype(F32) + depth) * freq_ref[...]
    lane = iota(angle.shape, 1)
    cosine, sine = jnp.cos(angle), jnp.sin(angle)
    sine = jnp.where(lane < head // 2, -sine, sine)
    for which, gain_ref in enumerate((q_gain_ref, k_gain_ref)):
        gain = jnp.broadcast_to(gain_ref[...], angle.shape)
        rot_ref[2 * which] = cosine * gain
        rot_ref[2 * which + 1] = sine * pltpu.roll(gain, head // 2, 1)

    all_tokens = ids_ref.shape[1]
    devices = hit_ref.shape[0]
    chips = devices // 2
    tokens = chips * new
    slot = iota((all_tokens, tokens), 1) // new
    source = (me ^ (2 * slot)) * new + iota((all_tokens, tokens), 1) % new
    order = (iota((all_tokens, tokens), 0) == source).astype(F32)
    ids = dot(ids_ref[...].astype(F32).astype(BF16), order.astype(BF16))
    gates = lax.dot_general(
        gates_ref[...],
        order,
        (((1,), (0,)), ((), ())),
        precision=lax.Precision.HIGHEST,
        preferred_element_type=F32,
    )
    for rel in range(devices):
        named = (ids == (me ^ rel).astype(F32)).astype(F32)
        hit_ref[rel : rel + 1, :] = jnp.max(named, axis=0, keepdims=True)
    before, later = iota((tokens, tokens), 0), iota((tokens, tokens), 1)
    earlier = (before < later) & (before // new == later // new)
    rank_ref[...] = dot(hit_ref[...].astype(BF16), earlier.astype(F32).astype(BF16))
    rows = chips * per
    slot_of = iota((rows, tokens), 1) // new
    row_slot = iota((rows, tokens), 0) // per
    row_rank = (iota((rows, tokens), 0) % per).astype(F32)
    in_first = iota((1, tokens), 1) < new
    for rel in range(devices):
        hit = hit_ref[rel : rel + 1, :] > 0.5
        rank = rank_ref[rel : rel + 1, :]
        chosen = (slot_of == (row_slot ^ (rel // 2))) & hit & (rank == row_rank)
        pick_ref[rel * rows : (rel + 1) * rows, :] = chosen.astype(F32)
        named = ids == (me ^ rel).astype(F32)
        weight = jnp.sum(jnp.where(named, gates, 0.0), axis=0, keepdims=True)
        for place in range(per):
            at = rel * per + place
            own = in_first & hit & (rank == float(place))
            own_ref[at : at + 1, :] = own.astype(F32)
            one = jnp.sum(jnp.where(own, weight, 0.0), axis=1, keepdims=True)
            weight_ref[at : at + 1, :] = jnp.broadcast_to(one, (1, weight_ref.shape[1]))
    first = (iota((tokens, new), 0) == iota((tokens, new), 1)).astype(F32)
    combine_ref[...] = lax.dot_general(
        first.astype(BF16),
        own_ref[...].astype(BF16),
        (((0,), (1,)), ((), ())),
        preferred_element_type=F32,
    )
    for copy in copies:
        copy.wait()


def project_kernel(chips, *refs):
    blocks = refs[:chips]
    gain_ref, wq_ref, wkv_ref, wq_sib, wkv_sib, _ = refs[chips : chips + 6]
    outs = refs[chips + 6 : 2 * chips + 6]
    normed = refs[-1]
    rows = blocks[0].shape[0]
    gain = gain_ref[...]
    for j in range(chips):
        values = norm_rows(blocks[j][...].astype(F32)) * gain
        normed[j * rows : (j + 1) * rows, :] = values.astype(BF16)
    values = normed[...]

    def put(result, at):
        result = result.astype(BF16)
        for j in range(chips):
            outs[j][:, at : at + result.shape[1]] = result[j * rows : (j + 1) * rows]

    wide, narrow = wq_ref.shape[1], wkv_ref.shape[0]
    put(dot(values, wq_ref[...]), 0)
    put(dot(values, wq_sib[...]), wide)
    put(dot_last(values, wkv_ref[...]), 2 * wide)
    put(dot_last(values, wkv_sib[...]), 2 * wide + narrow)


def attend_kernel(chips, q_width, kv_ready, *refs):
    got = refs[:chips]
    at = chips + 1 if kv_ready else chips
    keys_ref, values_ref, mask_ref, rot_ref = refs[at : at + 4]
    outs = refs[at + 6 : at + 6 + chips]
    fresh_ref = refs[chips] if kv_ready else refs[-1]
    me = lax.axis_index("tensor")
    chip = me // 2
    new = got[0].shape[0]
    kv_heads, span, head = keys_ref.shape
    per_chip = 2 * q_width // head
    group = chips * per_chip // kv_heads

    if not kv_ready:
        for rel in range(2 * chips):
            left = 2 * q_width + (rel % 2) * head
            fresh_ref[rel] = got[rel // 2][:, left : left + head]

    def rope(values, which):
        values = norm_rows(values.astype(F32))
        turned = pltpu.roll(values, head // 2, 1)
        return (values * rot_ref[2 * which] + turned * rot_ref[2 * which + 1]).astype(BF16)

    scale = head ** (-0.5) * LOG2E
    for j in range(chips):
        kv = (chip ^ j) * per_chip // group
        key_at, value_at = kv, kv + kv_heads
        if not kv_ready:
            key_at, value_at = me ^ key_at, me ^ value_at
        keys = jnp.concatenate([rope(fresh_ref[key_at], 1), keys_ref[kv, new:span]], axis=0)
        values = jnp.concatenate([fresh_ref[value_at], values_ref[kv, new:span]], axis=0)
        query = jnp.concatenate(
            [rope(got[j][:, h * head : (h + 1) * head], 0) for h in range(per_chip)], axis=0
        )
        score = dot_last(query, keys) * scale
        score = score.reshape(per_chip, new, span) + mask_ref[...][None]
        expo = jnp.exp2(score - jnp.max(score, axis=-1, keepdims=True))
        denom = jnp.sum(expo, axis=-1, keepdims=True).reshape(per_chip * new, 1)
        expo = expo.astype(BF16).reshape(per_chip * new, span)
        result = (dot(expo, values) / denom).astype(BF16)
        for h in range(per_chip):
            outs[j][:, h * head : (h + 1) * head] = result[h * new : (h + 1) * new]


def spread_kernel(chips, *refs):
    got = refs[:chips]
    pick_ref, w_ref, w_sib = refs[chips : chips + 3]
    for_experts = refs[chips + 4 : 2 * chips + 4]
    for_slots = refs[2 * chips + 4 : 3 * chips + 4]
    rows_ref = refs[-1]
    new = got[0].shape[0]
    depth, width = w_ref.shape
    each = rows_ref.shape[1]
    heads = jnp.concatenate([got[j][...] for j in range(chips)], axis=0)
    picked = dot(pick_ref[...].astype(BF16), heads).astype(BF16)
    extra = each - new
    for j in range(chips):
        rows_ref[j, 0:new, :] = got[j][...]
        rows_ref[j, new:each, :] = picked[j * extra : (j + 1) * extra]
    left = rows_ref[...].reshape(chips * each, 2 * depth)
    tile = min(512, width)
    for at in range(0, width, tile):
        part = dot(left[:, :depth], w_ref[:, at : at + tile])
        part = (part + dot(left[:, depth:], w_sib[:, at : at + tile])).astype(BF16)
        for j in range(chips):
            block = part[j * each : (j + 1) * each]
            for_slots[j][:, at : at + tile] = block[:new]
            for_experts[j][:, at : at + tile] = block[new:]


def fetch_kernel(_, source, target, sem):
    copy = pltpu.make_async_copy(source, target, sem.at[0])
    copy.start()
    copy.wait()


def select_kernel(chips, *refs):
    blocks = refs[:chips]
    pick_ref, _ = refs[chips : chips + 2]
    sources = refs[chips + 2 : chips + 4]
    picked_ref = refs[chips + 4]
    targets = refs[chips + 5 : chips + 7]
    sems = refs[-1]
    copies = [
        pltpu.make_async_copy(source, target, sems.at[which])
        for which, (source, target) in enumerate(zip(sources, targets))
    ]
    for copy in copies:
        copy.start()
    values = jnp.concatenate([block[...] for block in blocks], axis=0)
    pick = pick_ref[0 : picked_ref.shape[0], :].astype(BF16)
    picked_ref[...] = dot(pick, values)
    for copy in copies:
        copy.wait()


def hidden_kernel(chips, *refs):
    got = refs[:chips]
    own_ref, out_ref = refs[chips:]
    total = own_ref[...].astype(F32)
    for j in range(chips):
        total = total + got[j][...].astype(F32)
    out_ref[...] = total


def rows_kernel(chips, *refs):
    got = refs[:chips]
    picked_ref, gain_ref, own_ref, other_ref = refs[chips:]
    hidden = picked_ref[...]
    for j in range(chips):
        hidden = hidden + got[j][...].astype(F32)
    normed = (norm_rows(hidden) * gain_ref[...]).astype(BF16)
    half = own_ref.shape[0]
    own_ref[...] = normed[:half]
    other_ref[...] = normed[half:]


def expert_kernel(own_ref, other_ref, gate_ref, up_ref, down_ref, own_out, other_out):
    left = jnp.concatenate([own_ref[...].astype(F32), other_ref[...].astype(F32)], axis=0)
    left = left.astype(BF16)
    gate = dot_last(left, gate_ref[0])
    up = dot_last(left, up_ref[0])
    inner = (gate / (1.0 + jnp.exp(-gate)) * up).astype(BF16)
    result = dot(inner, down_ref[0])
    half = own_ref.shape[0]
    own_out[...] = result[:half].astype(BF16)
    other_out[...] = result[half:].astype(BF16)


def pack_kernel(chips, per, own_ref, other_ref, *outs):
    own, other = own_ref[...].astype(F32), other_ref[...].astype(F32)
    for j in range(chips):
        at = slice(j * per, (j + 1) * per)
        outs[j][...] = jnp.concatenate([own[at], other[at]], axis=0).astype(BF16)


def combine_kernel(chips, *refs):
    hidden_ref, combine_ref, weight_ref = refs[:3]
    got = refs[3 : 3 + chips]
    out_ref = refs[3 + chips]
    rows = jnp.concatenate([block[...].astype(F32) for block in got], axis=0)
    moe = lax.dot_general(
        combine_ref[...],
        rows * weight_ref[:, 0:1],
        (((1,), (0,)), ((), ())),
        precision=lax.Precision.HIGHEST,
        preferred_element_type=F32,
    )
    out_ref[...] = (hidden_ref[...] + moe).astype(BF16)


def body(
    residual_in,
    attn_gain,
    w_query,
    w_keyval,
    query_gain,
    key_gain,
    w_out,
    ffn_gain,
    w_gate,
    w_up,
    w_down,
    key_cache,
    value_cache,
    prefix_lens,
    accepted,
    accept_path,
    parents,
    slot_kinds,
    expert_ids,
    gate_probs,
):
    devices = lax.axis_size("tensor")
    chips = devices // 2
    new, width = residual_in.shape
    head = query_gain.shape[0]
    kv_heads = key_cache.shape[2] // head
    q_width = w_query.shape[1]
    new_width = w_keyval.shape[0]
    all_tokens, top = expert_ids.shape
    tokens = chips * new
    per = new * top // EXPERTS
    path_len = accept_path.shape[1]
    rows = 2 * chips * per
    assert key_cache.shape[0] == 1 and w_gate.shape[0] == 1
    assert devices & (devices - 1) == 0
    vmem, smem, hbm, anywhere = pltpu.VMEM, pltpu.SMEM, pltpu.HBM, pl.ANY

    blocks = exchange([residual_in] * chips)
    wq_sib = hop(w_query, 1)
    wkv_sib = hop(w_keyval, 1)

    freq = ROPE_BASE ** (-2.0 * np.arange(head // 2) / head)
    freq = jnp.asarray(np.concatenate([freq, freq])[None, :], F32)
    span = -(-(new + 16 + window_rows(path_len)) // 128) * 128
    weights = [attn_gain[None, :], ffn_gain[None, :], w_query, w_keyval, w_out]
    prepared = call(
        functools.partial(prep_kernel, path_len, per, len(weights)),
        "prep",
        [
            in_vmem((kv_heads, span, head), BF16),
            in_vmem((kv_heads, span, head), BF16),
            in_vmem((new, span), F32),
            in_vmem((4, new, head), F32),
            in_vmem((chips * rows, tokens), F32),
            in_vmem((new, devices * per), F32),
            in_vmem((devices * per, 128), F32),
        ]
        + [in_vmem(weight.shape, weight.dtype) for weight in weights],
        [
            (key_cache, hbm),
            (value_cache, hbm),
            (prefix_lens, smem),
            (accepted, smem),
            (slot_kinds, smem),
            (accept_path, hbm),
            (parents, hbm),
            (expert_ids.T, hbm),
            (gate_probs.T, hbm),
            (freq, hbm),
            (query_gain[None, :], hbm),
            (key_gain[None, :], hbm),
        ]
        + [(weight, hbm) for weight in weights],
        [
            pltpu.SMEM((1, path_len), jnp.int32),
            pltpu.VMEM((1, new), jnp.int32),
            pltpu.VMEM((top, all_tokens), jnp.int32),
            pltpu.VMEM((top, all_tokens), F32),
            pltpu.VMEM((1, head), F32),
            pltpu.VMEM((1, head), F32),
            pltpu.VMEM((1, head), F32),
            pltpu.VMEM((devices, tokens), F32),
            pltpu.VMEM((devices, tokens), F32),
            pltpu.VMEM((devices * per, tokens), F32),
            pltpu.SemaphoreType.DMA((7,)),
            pltpu.SemaphoreType.DMA((2, kv_heads, 2)),
            pltpu.SemaphoreType.DMA((len(weights),)),
        ],
        limit=16,
        moved=4 * span * kv_heads * head * 2,
    )
    keys, values, mask, rot, pick, combine, weight, gain, ffn, wq, wkv, wo = prepared

    *projected, wo = call(
        functools.partial(project_kernel, chips),
        "project",
        [in_vmem((new, 2 * (q_width + new_width)), BF16)] * chips
        + [in_vmem(wo.shape, wo.dtype)],
        [(block, vmem) for block in blocks]
        + [
            (gain, vmem),
            (wq, vmem),
            (wkv, vmem),
            (wq_sib, vmem),
            (wkv_sib, vmem),
            (wo, vmem),
        ],
        [pltpu.VMEM((tokens, width), BF16)],
        limit=16,
        same={chips + 5: chips},
        flops=4 * tokens * width * (q_width + new_width),
        moved=4 * width * (q_width + new_width),
    )
    wo_sib = hop(wo, 1)

    got = exchange(projected)
    picked, wg, wu = call(
        functools.partial(select_kernel, chips),
        "select",
        [in_vmem((rows, width), F32)] + [in_vmem(w.shape, w.dtype) for w in (w_gate, w_up)],
        [(block, vmem) for block in blocks]
        + [(pick, vmem), (projected[0], anywhere), (w_gate, hbm), (w_up, hbm)],
        [pltpu.SemaphoreType.DMA((2,))],
        limit=8,
        flops=2 * rows * width * tokens,
        moved=8 * width * w_gate.shape[1],
    )
    kv_ready = []
    if new_width != head:
        pieces = [
            got[rel // 2][:, 2 * q_width + (rel % 2) * new_width :][:, :new_width]
            for rel in range(devices)
        ]
        pieces = jnp.stack(pieces)[lax.axis_index("tensor") ^ jnp.arange(devices)]
        pieces = pieces.transpose(1, 0, 2).reshape(new, 2 * kv_heads, head)
        kv_ready = [(pieces.transpose(1, 0, 2), vmem)]
    attended = call(
        functools.partial(attend_kernel, chips, q_width, bool(kv_ready)),
        "attend",
        [in_vmem((new, 2 * q_width), BF16)] * chips,
        [(block, vmem) for block in got]
        + kv_ready
        + [(keys, vmem), (values, vmem), (mask, vmem), (rot, vmem)]
        + [(wo_sib, anywhere), (wg, anywhere)],
        [] if kv_ready else [pltpu.VMEM((devices, new, head), BF16)],
        limit=16,
        flops=8 * new * chips * q_width * span,
        moved=4 * span * kv_heads * head,
    )
    heads = exchange(attended)
    wd = call(
        fetch_kernel,
        "fetch",
        [in_vmem(w_down.shape, w_down.dtype)],
        [(attended[0], anywhere), (w_down, hbm)],
        [pltpu.SemaphoreType.DMA((1,))],
        limit=8,
        moved=4 * width * w_gate.shape[1],
    )[0]

    partial = call(
        functools.partial(spread_kernel, chips),
        "spread",
        [in_vmem((rows, width), BF16)] * chips + [in_vmem((new, width), BF16)] * chips,
        [(block, vmem) for block in heads] + [(pick, vmem), (wo, vmem), (wo_sib, vmem), (wd, anywhere)],
        [pltpu.VMEM((chips, new + rows, 2 * q_width), BF16)],
        limit=16,
        flops=4 * chips * (new + rows) * width * q_width,
        moved=4 * q_width * width,
    )
    for_experts = exchange(partial[:chips])
    for_slots = exchange(partial[chips:])

    own, other = call(
        functools.partial(rows_kernel, chips),
        "rows",
        [in_vmem((rows // 2, width), BF16)] * 2,
        [(block, vmem) for block in for_experts] + [(picked, vmem), (ffn, vmem)],
        limit=8,
        moved=2 * chips * rows * width,
    )
    own_out, other_out = call(
        expert_kernel,
        "expert",
        [in_vmem((rows // 2, width), BF16)] * 2,
        [(own, vmem), (hop(other, 1), vmem), (wg, vmem), (wu, vmem), (wd, vmem)],
        limit=16,
        flops=6 * rows * width * w_gate.shape[1],
        moved=6 * width * w_gate.shape[1],
    )
    results = call(
        functools.partial(pack_kernel, chips, per),
        "pack",
        [in_vmem((2 * per, width), BF16)] * chips,
        [(own_out, vmem), (hop(other_out, 1), vmem)],
        limit=8,
        moved=4 * rows * width,
    )
    returned = exchange(results)
    hidden = call(
        functools.partial(hidden_kernel, chips),
        "hidden",
        [in_vmem((new, width), F32)],
        [(block, vmem) for block in for_slots] + [(residual_in, vmem)],
        limit=8,
        moved=2 * chips * new * width,
    )[0]
    return call(
        functools.partial(combine_kernel, chips),
        "combine",
        [jax.ShapeDtypeStruct((new, width), BF16)],
        [(hidden, vmem), (combine, vmem), (weight, vmem)]
        + [(block, vmem) for block in returned],
        limit=8,
        moved=6 * new * width,
    )[0]


def solution(mesh):
    in_specs = (
        P(("group", "tensor"), None),
        P(),
        P(None, "tensor"),
        P("tensor", None),
        P(),
        P(),
        P("tensor", None),
        P(),
        P("tensor", None, None),
        P("tensor", None, None),
        P("tensor", None, None),
        P(("group", "tensor"), None, None),
        P(("group", "tensor"), None, None),
        P(("group", "tensor")),
        P(("group", "tensor")),
        P(("group", "tensor"), None),
        P(("group", "tensor"), None),
        P(("group", "tensor")),
        P("group", None),
        P("group", None),
    )
    out_specs = P(("group", "tensor"), None)
    return jax.shard_map(body, mesh=mesh, in_specs=in_specs, out_specs=out_specs, check_vma=False)
```

```python
import functools
import math

import jax
import jax.numpy as jnp
import numpy as np
from jax import lax
from jax.experimental import pallas as pl
from jax.experimental.pallas import tpu as pltpu
from jax.sharding import PartitionSpec as P

EXPERTS = 128
SINK = 4
WIN = 512

EPSILON = 1e-06
NEG_FILL = -1e30
ROPE_BASE = 1000000.0
LOG2E = math.log2(math.e)
F32 = jnp.float32
BF16 = jnp.bfloat16
MIB = 1 << 20


def iota(shape, dim):
    return lax.broadcasted_iota(jnp.int32, shape, dim)


def dot(left, right):
    return jnp.dot(left, right, preferred_element_type=F32)


def dot_last(left, right):
    return lax.dot_general(left, right, (((1,), (1,)), ((), ())), preferred_element_type=F32)


def dot_first(left, right):
    return lax.dot_general(left, right, (((0,), (0,)), ((), ())), preferred_element_type=F32)


def norm_rows(values):
    return values * lax.rsqrt(jnp.mean(values * values, axis=-1, keepdims=True) + EPSILON)


def in_vmem(shape, dtype):
    return pltpu.VMEM(shape, dtype)


def call(kernel, name, outs, args, scratch=(), limit=16, flops=0, moved=0, same=None):
    arrays = []
    specs = []
    for array, space in args:
        if space is pltpu.HBM or space is pltpu.VMEM:
            array = pltpu.with_memory_space_constraint(array, space)
        arrays.append(array)
        specs.append(pl.BlockSpec(memory_space=space))
    return pl.pallas_call(
        kernel,
        out_shape=outs,
        in_specs=specs,
        out_specs=[pl.BlockSpec(memory_space=pltpu.VMEM) for _ in outs],
        scratch_shapes=list(scratch),
        input_output_aliases=same or {},
        compiler_params=pltpu.CompilerParams(vmem_limit_bytes=limit * MIB),
        cost_estimate=pl.CostEstimate(flops=flops, bytes_accessed=moved, transcendentals=0),
        name=name,
    )(*arrays)


def hop(value, step):
    devices = lax.axis_size("tensor")
    return lax.ppermute(value, "tensor", [(i, i ^ step) for i in range(devices)])


def exchange(blocks):
    got = [hop(blocks[j], 2 * j) for j in reversed(range(1, len(blocks)))]
    return [blocks[0]] + got[::-1]


def window_rows(path_len):
    return -(-(WIN + 2 * (path_len - 1) + 16) // 16) * 16


def prep_kernel(path_len, n_weights, *refs):
    key_cache, value_cache, prefix_ref, accepted_ref, kind_ref = refs[:5]
    small_in = refs[5:10]
    sources = refs[10 : 10 + n_weights]
    refs = refs[10 + n_weights :]
    keys_ref, values_ref, mask_ref, rot_ref = refs[:4]
    targets = refs[4 : 4 + n_weights]
    refs = refs[4 + n_weights :]
    path_ref, parents_ref, freq_ref, q_gain_ref, k_gain_ref = refs[:5]
    small_sems, cache_sems, weight_sems = refs[5:]

    new = mask_ref.shape[0]
    kv_heads, span, head = keys_ref.shape
    cache_len = key_cache.shape[1]
    wide = window_rows(path_len)
    sink_at, win_at = new, new + 16
    end = win_at + wide

    small = [
        pltpu.make_async_copy(source, target, small_sems.at[which])
        for which, (source, target) in enumerate(zip(small_in, refs[:5]))
    ]
    for copy in small:
        copy.start()
    copies = [
        pltpu.make_async_copy(source, target, weight_sems.at[which])
        for which, (source, target) in enumerate(zip(sources, targets))
    ]
    prefix = prefix_ref[0]
    accepted = accepted_ref[0]
    total = prefix + accepted
    low = jnp.maximum(total - WIN, 0)
    start = pl.multiple_of(jnp.minimum((low // 16) * 16, cache_len - wide), 16)
    for which, (cache, buf) in enumerate(((key_cache, keys_ref), (value_cache, values_ref))):
        for kv in range(kv_heads):
            cols = pl.ds(kv * head, head)
            copies.append(
                pltpu.make_async_copy(
                    cache.at[0, pl.ds(start, wide), cols],
                    buf.at[kv, pl.ds(win_at, wide)],
                    cache_sems.at[which, kv, 0],
                )
            )
            copies.append(
                pltpu.make_async_copy(
                    cache.at[0, pl.ds(0, 16), cols],
                    buf.at[kv, pl.ds(sink_at, 16)],
                    cache_sems.at[which, kv, 1],
                )
            )
    for copy in copies:
        copy.start()

    for buf in (keys_ref, values_ref):
        buf[:, 0:new, :] = jnp.zeros((kv_heads, new, head), BF16)
        buf[:, end:span, :] = jnp.zeros((kv_heads, span - end, head), BF16)

    for copy in small:
        copy.wait()
    column = iota((1, span), 1)
    row = jnp.where(column < win_at, column - sink_at, start + column - win_at)
    taken = jnp.zeros((1, span), jnp.bool_)
    for step in range(path_len):
        at = prefix + path_ref[0, step]
        taken = taken | ((row == at) & (step < accepted))
    old = (row < prefix) & ((row < SINK) | (row >= total - WIN))
    in_window = (column >= win_at) & (column < end) & (old | taken)
    in_sink = (column >= sink_at) & (column < win_at) & (row < SINK) & (row < prefix) & (start > 0)
    seen = jnp.where(in_window | in_sink, 0.0, NEG_FILL)
    mask_ref[...] = jnp.broadcast_to(seen, mask_ref.shape)

    down, across = iota((new, new), 0), iota((new, new), 1)
    eye = (down == across).astype(F32)
    back = eye + (down == parents_ref[...]).astype(F32)
    for _ in range((new - 1).bit_length()):
        half = back.astype(BF16)
        back = jnp.minimum(dot(half, half), 1.0)
    reach = dot_first(back.astype(BF16), eye.astype(BF16))
    tree = (kind_ref[0] == 1).astype(F32)
    causal = (across <= down).astype(F32)
    allowed = tree * reach + (1.0 - tree) * causal
    mask_ref[:, 0:new] = jnp.where(allowed > 0.5, 0.0, NEG_FILL)
    depth = tree * (jnp.sum(reach, axis=1, keepdims=True) - 1.0)
    depth = depth + (1.0 - tree) * iota((new, 1), 0).astype(F32)
    angle = (total.astype(F32) + depth) * freq_ref[...]
    lane = iota(angle.shape, 1)
    cosine, sine = jnp.cos(angle), jnp.sin(angle)
    sine = jnp.where(lane < head // 2, -sine, sine)
    for which, gain_ref in enumerate((q_gain_ref, k_gain_ref)):
        gain = jnp.broadcast_to(gain_ref[...], angle.shape)
        rot_ref[2 * which] = cosine * gain
        rot_ref[2 * which + 1] = sine * pltpu.roll(gain, head // 2, 1)
    for copy in copies:
        copy.wait()


def route_kernel(per, new, n_weights, *refs):
    small_in = refs[1:3]
    sources = refs[3 : 3 + n_weights]
    refs = refs[3 + n_weights :]
    pick_ref, combine_ref, weight_ref = refs[:3]
    targets = refs[3 : 3 + n_weights]
    ids_ref, gates_ref, hit_ref, rank_ref, own_ref, sems = refs[3 + n_weights :]
    sources, targets = (*small_in, *sources), (ids_ref, gates_ref, *targets)
    copies = [
        pltpu.make_async_copy(source, target, sems.at[which])
        for which, (source, target) in enumerate(zip(sources, targets))
    ]
    for copy in copies:
        copy.start()
    for copy in copies[:2]:
        copy.wait()

    me = lax.axis_index("tensor")
    all_tokens = ids_ref.shape[1]
    devices = hit_ref.shape[0]
    chips = devices // 2
    tokens = chips * new
    slot = iota((all_tokens, tokens), 1) // new
    source = (me ^ (2 * slot)) * new + iota((all_tokens, tokens), 1) % new
    order = (iota((all_tokens, tokens), 0) == source).astype(F32)
    ids = dot(ids_ref[...].astype(F32).astype(BF16), order.astype(BF16))
    gates = lax.dot_general(
        gates_ref[...],
        order,
        (((1,), (0,)), ((), ())),
        precision=lax.Precision.HIGHEST,
        preferred_element_type=F32,
    )
    for rel in range(devices):
        named = (ids == (me ^ rel).astype(F32)).astype(F32)
        hit_ref[rel : rel + 1, :] = jnp.max(named, axis=0, keepdims=True)
    before, later = iota((tokens, tokens), 0), iota((tokens, tokens), 1)
    earlier = (before < later) & (before // new == later // new)
    rank_ref[...] = dot(hit_ref[...].astype(BF16), earlier.astype(F32).astype(BF16))
    rows = chips * per
    slot_of = iota((rows, tokens), 1) // new
    row_slot = iota((rows, tokens), 0) // per
    row_rank = (iota((rows, tokens), 0) % per).astype(F32)
    in_first = iota((1, tokens), 1) < new
    for rel in range(devices):
        hit = hit_ref[rel : rel + 1, :] > 0.5
        rank = rank_ref[rel : rel + 1, :]
        chosen = (slot_of == (row_slot ^ (rel // 2))) & hit & (rank == row_rank)
        pick_ref[rel * rows : (rel + 1) * rows, :] = chosen.astype(F32)
        named = ids == (me ^ rel).astype(F32)
        weight = jnp.sum(jnp.where(named, gates, 0.0), axis=0, keepdims=True)
        for place in range(per):
            at = rel * per + place
            own = in_first & hit & (rank == float(place))
            own_ref[at : at + 1, :] = own.astype(F32)
            one = jnp.sum(jnp.where(own, weight, 0.0), axis=1, keepdims=True)
            weight_ref[at : at + 1, :] = jnp.broadcast_to(one, (1, weight_ref.shape[1]))
    first = (iota((tokens, new), 0) == iota((tokens, new), 1)).astype(F32)
    combine_ref[...] = lax.dot_general(
        first.astype(BF16),
        own_ref[...].astype(BF16),
        (((0,), (1,)), ((), ())),
        preferred_element_type=F32,
    )
    for copy in copies[2:]:
        copy.wait()


def project_kernel(count, *refs):
    blocks = refs[:count]
    gain_ref, wq_ref, wkv_ref, wq_sib, wkv_sib = refs[count : count + 5]
    outs = refs[count + 5 :]
    rows = blocks[0].shape[0]
    gain = gain_ref[...]
    values = [(norm_rows(block[...].astype(F32)) * gain).astype(BF16) for block in blocks]
    values = jnp.concatenate(values, axis=0)

    def put(result, at):
        result = result.astype(BF16)
        for j in range(count):
            outs[j][:, at : at + result.shape[1]] = result[j * rows : (j + 1) * rows]

    wide, narrow = wq_ref.shape[1], wkv_ref.shape[0]
    put(dot(values, wq_ref[...]), 0)
    put(dot(values, wq_sib[...]), wide)
    put(dot_last(values, wkv_ref[...]), 2 * wide)
    put(dot_last(values, wkv_sib[...]), 2 * wide + narrow)


def attend_kernel(chips, q_width, kv_ready, *refs):
    got = refs[:chips]
    at = chips + 1 if kv_ready else chips
    keys_ref, values_ref, mask_ref, rot_ref = refs[at : at + 4]
    outs = refs[at + 5 : at + 5 + chips]
    fresh_ref = refs[chips] if kv_ready else refs[-1]
    me = lax.axis_index("tensor")
    chip = me // 2
    new = got[0].shape[0]
    kv_heads, span, head = keys_ref.shape
    per_chip = 2 * q_width // head
    group = chips * per_chip // kv_heads

    if not kv_ready:
        for rel in range(2 * chips):
            left = 2 * q_width + (rel % 2) * head
            fresh_ref[rel] = got[rel // 2][:, left : left + head]

    def rope(values, which):
        values = norm_rows(values.astype(F32))
        turned = pltpu.roll(values, head // 2, 1)
        return (values * rot_ref[2 * which] + turned * rot_ref[2 * which + 1]).astype(BF16)

    scale = head ** (-0.5) * LOG2E
    for j in range(chips):
        kv = (chip ^ j) * per_chip // group
        key_at, value_at = kv, kv + kv_heads
        if not kv_ready:
            key_at, value_at = me ^ key_at, me ^ value_at
        keys = jnp.concatenate([rope(fresh_ref[key_at], 1), keys_ref[kv, new:span]], axis=0)
        values = jnp.concatenate([fresh_ref[value_at], values_ref[kv, new:span]], axis=0)
        query = jnp.concatenate(
            [rope(got[j][:, h * head : (h + 1) * head], 0) for h in range(per_chip)], axis=0
        )
        score = dot_last(query, keys) * scale
        score = score.reshape(per_chip, new, span) + mask_ref[...][None]
        expo = jnp.exp2(score - jnp.max(score, axis=-1, keepdims=True))
        denom = jnp.sum(expo, axis=-1, keepdims=True).reshape(per_chip * new, 1)
        expo = expo.astype(BF16).reshape(per_chip * new, span)
        result = (dot(expo, values) / denom).astype(BF16)
        for h in range(per_chip):
            outs[j][:, h * head : (h + 1) * head] = result[h * new : (h + 1) * new]


def spread_kernel(chips, picks, *refs):
    got = refs[:chips]
    w_ref, w_sib = refs[chips : chips + 2]
    outs = refs[-chips:]
    depth, width = w_ref.shape
    left = jnp.concatenate([got[j][...] for j in range(chips)], axis=0)
    if picks:
        left = dot(refs[chips + 2][...].astype(BF16), left).astype(BF16)
    each = left.shape[0] // chips
    tile = min(512, width)
    for at in range(0, width, tile):
        part = dot(left[:, :depth], w_ref[:, at : at + tile])
        part = (part + dot(left[:, depth:], w_sib[:, at : at + tile])).astype(BF16)
        for j in range(chips):
            outs[j][:, at : at + tile] = part[j * each : (j + 1) * each]


def select_kernel(chips, *refs):
    blocks = refs[:chips]
    pick_ref, _ = refs[chips : chips + 2]
    sources = refs[chips + 2 : chips + 4]
    picked_ref = refs[chips + 4]
    targets = refs[chips + 5 : chips + 7]
    sems = refs[-1]
    copies = [
        pltpu.make_async_copy(source, target, sems.at[which])
        for which, (source, target) in enumerate(zip(sources, targets))
    ]
    for copy in copies:
        copy.start()
    values = jnp.concatenate([block[...] for block in blocks], axis=0)
    pick = pick_ref[0 : picked_ref.shape[0], :].astype(BF16)
    picked_ref[...] = dot(pick, values)
    for copy in copies:
        copy.wait()


def hidden_kernel(chips, *refs):
    got = refs[:chips]
    own_ref, out_ref = refs[chips:]
    total = own_ref[...].astype(F32)
    for j in range(chips):
        total = total + got[j][...].astype(F32)
    out_ref[...] = total


def rows_kernel(chips, *refs):
    got = refs[:chips]
    picked_ref, gain_ref, _, own_ref, other_ref = refs[chips:]
    hidden = picked_ref[...]
    for j in range(chips):
        hidden = hidden + got[j][...].astype(F32)
    normed = (norm_rows(hidden) * gain_ref[...]).astype(BF16)
    half = own_ref.shape[0]
    own_ref[...] = normed[:half]
    other_ref[...] = normed[half:]


def expert_kernel(own_ref, other_ref, gate_ref, up_ref, down_ref, own_out, other_out):
    left = jnp.concatenate([own_ref[...].astype(F32), other_ref[...].astype(F32)], axis=0)
    left = left.astype(BF16)
    gate = dot_last(left, gate_ref[0])
    up = dot_last(left, up_ref[0])
    inner = (gate / (1.0 + jnp.exp(-gate)) * up).astype(BF16)
    result = dot(inner, down_ref[0])
    half = own_ref.shape[0]
    own_out[...] = result[:half].astype(BF16)
    other_out[...] = result[half:].astype(BF16)


def pack_kernel(chips, per, own_ref, other_ref, *outs):
    own, other = own_ref[...].astype(F32), other_ref[...].astype(F32)
    for j in range(chips):
        at = slice(j * per, (j + 1) * per)
        outs[j][...] = jnp.concatenate([own[at], other[at]], axis=0).astype(BF16)


def combine_kernel(chips, *refs):
    hidden_ref, combine_ref, weight_ref = refs[:3]
    got = refs[3 : 3 + chips]
    out_ref = refs[3 + chips]
    rows = jnp.concatenate([block[...].astype(F32) for block in got], axis=0)
    moe = lax.dot_general(
        combine_ref[...],
        rows * weight_ref[:, 0:1],
        (((1,), (0,)), ((), ())),
        precision=lax.Precision.HIGHEST,
        preferred_element_type=F32,
    )
    out_ref[...] = (hidden_ref[...] + moe).astype(BF16)


def body(
    residual_in,
    attn_gain,
    w_query,
    w_keyval,
    query_gain,
    key_gain,
    w_out,
    ffn_gain,
    w_gate,
    w_up,
    w_down,
    key_cache,
    value_cache,
    prefix_lens,
    accepted,
    accept_path,
    parents,
    slot_kinds,
    expert_ids,
    gate_probs,
):
    devices = lax.axis_size("tensor")
    chips = devices // 2
    new, width = residual_in.shape
    head = query_gain.shape[0]
    kv_heads = key_cache.shape[2] // head
    q_width = w_query.shape[1]
    new_width = w_keyval.shape[0]
    all_tokens, top = expert_ids.shape
    tokens = chips * new
    per = new * top // EXPERTS
    path_len = accept_path.shape[1]
    rows = 2 * chips * per
    assert key_cache.shape[0] == 1 and w_gate.shape[0] == 1
    assert devices & (devices - 1) == 0
    vmem, smem, hbm, anywhere = pltpu.VMEM, pltpu.SMEM, pltpu.HBM, pl.ANY

    blocks = exchange([residual_in] * chips)
    wq_sib = hop(w_query, 1)
    wkv_sib = hop(w_keyval, 1)

    freq = ROPE_BASE ** (-2.0 * np.arange(head // 2) / head)
    freq = jnp.asarray(np.concatenate([freq, freq])[None, :], F32)
    span = -(-(new + 16 + window_rows(path_len)) // 128) * 128
    weights = [attn_gain[None, :], w_query, w_keyval]
    keys, values, mask, rot, gain, wq, wkv = call(
        functools.partial(prep_kernel, path_len, len(weights)),
        "prep",
        [
            in_vmem((kv_heads, span, head), BF16),
            in_vmem((kv_heads, span, head), BF16),
            in_vmem((new, span), F32),
            in_vmem((4, new, head), F32),
        ]
        + [in_vmem(w.shape, w.dtype) for w in weights],
        [
            (key_cache, hbm),
            (value_cache, hbm),
            (prefix_lens, smem),
            (accepted, smem),
            (slot_kinds, smem),
            (accept_path, hbm),
            (parents, hbm),
            (freq, hbm),
            (query_gain[None, :], hbm),
            (key_gain[None, :], hbm),
        ]
        + [(w, hbm) for w in weights],
        [
            pltpu.SMEM((1, path_len), jnp.int32),
            pltpu.VMEM((1, new), jnp.int32),
            pltpu.VMEM((1, head), F32),
            pltpu.VMEM((1, head), F32),
            pltpu.VMEM((1, head), F32),
            pltpu.SemaphoreType.DMA((5,)),
            pltpu.SemaphoreType.DMA((2, kv_heads, 2)),
            pltpu.SemaphoreType.DMA((len(weights),)),
        ],
        limit=16,
        moved=4 * span * kv_heads * head * 2,
    )

    def project(some):
        return call(
            functools.partial(project_kernel, len(some)),
            "project",
            [in_vmem((new, 2 * (q_width + new_width)), BF16)] * len(some),
            [(block, vmem) for block in some]
            + [(w, vmem) for w in (gain, wq, wkv, wq_sib, wkv_sib)],
            limit=16,
            flops=4 * len(some) * new * width * (q_width + new_width),
            moved=4 * width * (q_width + new_width),
        )

    projected = project(blocks[:-1])
    got = [projected[0]] + [hop(projected[j], 2 * j) for j in range(1, chips - 1)]
    got.append(hop(project(blocks[-1:])[0], 2 * (chips - 1)))

    weights = [ffn_gain[None, :], w_out, w_down]
    pick, combine, weight, ffn, wo, wd = call(
        functools.partial(route_kernel, per, new, len(weights)),
        "route",
        [
            in_vmem((chips * rows, tokens), F32),
            in_vmem((new, devices * per), F32),
            in_vmem((devices * per, 128), F32),
        ]
        + [in_vmem(w.shape, w.dtype) for w in weights],
        [(projected[0], anywhere), (expert_ids.T, hbm), (gate_probs.T, hbm)]
        + [(w, hbm) for w in weights],
        [
            pltpu.VMEM((top, all_tokens), jnp.int32),
            pltpu.VMEM((top, all_tokens), F32),
            pltpu.VMEM((devices, tokens), F32),
            pltpu.VMEM((devices, tokens), F32),
            pltpu.VMEM((devices * per, tokens), F32),
            pltpu.SemaphoreType.DMA((2 + len(weights),)),
        ],
        limit=16,
        moved=4 * width * (q_width + w_down.shape[1]),
    )
    kv_ready = []
    if new_width != head:
        pieces = [
            got[rel // 2][:, 2 * q_width + (rel % 2) * new_width :][:, :new_width]
            for rel in range(devices)
        ]
        pieces = jnp.stack(pieces)[lax.axis_index("tensor") ^ jnp.arange(devices)]
        pieces = pieces.transpose(1, 0, 2).reshape(new, 2 * kv_heads, head)
        kv_ready = [(pieces.transpose(1, 0, 2), vmem)]
    *attended, wo = call(
        functools.partial(attend_kernel, chips, q_width, bool(kv_ready)),
        "attend",
        [in_vmem((new, 2 * q_width), BF16)] * chips + [in_vmem(wo.shape, wo.dtype)],
        [(block, vmem) for block in got]
        + kv_ready
        + [(keys, vmem), (values, vmem), (mask, vmem), (rot, vmem)]
        + [(wo, vmem)],
        [] if kv_ready else [pltpu.VMEM((devices, new, head), BF16)],
        limit=16,
        same={chips + len(kv_ready) + 4: chips},
        flops=8 * new * chips * q_width * span,
        moved=4 * span * kv_heads * head,
    )
    wo_sib = hop(wo, 1)
    heads = exchange(attended)
    picked, wg, wu = call(
        functools.partial(select_kernel, chips),
        "select",
        [in_vmem((rows, width), F32)] + [in_vmem(w.shape, w.dtype) for w in (w_gate, w_up)],
        [(block, vmem) for block in blocks]
        + [(pick, vmem), (attended[0], anywhere), (w_gate, hbm), (w_up, hbm)],
        [pltpu.SemaphoreType.DMA((2,))],
        limit=8,
        flops=2 * rows * width * tokens,
        moved=8 * width * w_gate.shape[1],
    )

    def spread(name, each, more):
        return call(
            functools.partial(spread_kernel, chips, name == "experts"),
            name,
            [in_vmem((each, width), BF16)] * chips,
            [(block, vmem) for block in heads] + [(wo, vmem), (wo_sib, vmem)] + more,
            limit=16,
            flops=4 * chips * each * width * q_width,
            moved=4 * q_width * width,
        )

    partial = spread("experts", rows, [(pick, vmem), (wg, anywhere)])
    for_experts = exchange(partial)
    partial = spread("slots", new, [(partial[0], anywhere)])
    for_slots = exchange(partial)

    own, other = call(
        functools.partial(rows_kernel, chips),
        "rows",
        [in_vmem((rows // 2, width), BF16)] * 2,
        [(block, vmem) for block in for_experts]
        + [(picked, vmem), (ffn, vmem), (partial[0], anywhere)],
        limit=8,
        moved=2 * chips * rows * width,
    )
    own_out, other_out = call(
        expert_kernel,
        "expert",
        [in_vmem((rows // 2, width), BF16)] * 2,
        [(own, vmem), (hop(other, 1), vmem), (wg, vmem), (wu, vmem), (wd, vmem)],
        limit=16,
        flops=6 * rows * width * w_gate.shape[1],
        moved=6 * width * w_gate.shape[1],
    )
    results = call(
        functools.partial(pack_kernel, chips, per),
        "pack",
        [in_vmem((2 * per, width), BF16)] * chips,
        [(own_out, vmem), (hop(other_out, 1), vmem)],
        limit=8,
        moved=4 * rows * width,
    )
    returned = exchange(results)
    hidden = call(
        functools.partial(hidden_kernel, chips),
        "hidden",
        [in_vmem((new, width), F32)],
        [(block, vmem) for block in for_slots] + [(residual_in, vmem)],
        limit=8,
        moved=2 * chips * new * width,
    )[0]
    return call(
        functools.partial(combine_kernel, chips),
        "combine",
        [jax.ShapeDtypeStruct((new, width), BF16)],
        [(hidden, vmem), (combine, vmem), (weight, vmem)]
        + [(block, vmem) for block in returned],
        limit=8,
        moved=6 * new * width,
    )[0]


def solution(mesh):
    in_specs = (
        P(("group", "tensor"), None),
        P(),
        P(None, "tensor"),
        P("tensor", None),
        P(),
        P(),
        P("tensor", None),
        P(),
        P("tensor", None, None),
        P("tensor", None, None),
        P("tensor", None, None),
        P(("group", "tensor"), None, None),
        P(("group", "tensor"), None, None),
        P(("group", "tensor")),
        P(("group", "tensor")),
        P(("group", "tensor"), None),
        P(("group", "tensor"), None),
        P(("group", "tensor")),
        P("group", None),
        P("group", None),
    )
    out_specs = P(("group", "tensor"), None)
    return jax.shard_map(body, mesh=mesh, in_specs=in_specs, out_specs=out_specs, check_vma=False)
```

```python
import functools
import math

import jax
import jax.numpy as jnp
import numpy as np
from jax import lax
from jax.experimental import pallas as pl
from jax.experimental.pallas import tpu as pltpu
from jax.sharding import PartitionSpec as P

EXPERTS = 128
SINK = 4
WIN = 512

EPSILON = 1e-06
NEG_FILL = -1e30
ROPE_BASE = 1000000.0
LOG2E = math.log2(math.e)
F32 = jnp.float32
BF16 = jnp.bfloat16
MIB = 1 << 20


def step(j):
    return 2 * j + bin(j).count("1") % 2


def iota(shape, dim):
    return lax.broadcasted_iota(jnp.int32, shape, dim)


def dot(left, right):
    return jnp.dot(left, right, preferred_element_type=F32)


def dot_last(left, right):
    return lax.dot_general(left, right, (((1,), (1,)), ((), ())), preferred_element_type=F32)


def dot_first(left, right):
    return lax.dot_general(left, right, (((0,), (0,)), ((), ())), preferred_element_type=F32)


def norm_rows(values):
    return values * lax.rsqrt(jnp.mean(values * values, axis=-1, keepdims=True) + EPSILON)


def in_vmem(shape, dtype):
    return pltpu.VMEM(shape, dtype)


def call(kernel, name, outs, args, scratch=(), limit=16, flops=0, moved=0, same=None):
    arrays = []
    specs = []
    for array, space in args:
        if space is pltpu.HBM or space is pltpu.VMEM:
            array = pltpu.with_memory_space_constraint(array, space)
        arrays.append(array)
        specs.append(pl.BlockSpec(memory_space=space))
    return pl.pallas_call(
        kernel,
        out_shape=outs,
        in_specs=specs,
        out_specs=[pl.BlockSpec(memory_space=pltpu.VMEM) for _ in outs],
        scratch_shapes=list(scratch),
        input_output_aliases=same or {},
        compiler_params=pltpu.CompilerParams(vmem_limit_bytes=limit * MIB),
        cost_estimate=pl.CostEstimate(flops=flops, bytes_accessed=moved, transcendentals=0),
        name=name,
    )(*arrays)


def hop(value, step):
    devices = lax.axis_size("tensor")
    return lax.ppermute(value, "tensor", [(i, i ^ step) for i in range(devices)])


def exchange(blocks):
    return [blocks[0]] + [hop(blocks[j], step(j)) for j in range(1, len(blocks))]


def window_rows(path_len):
    return -(-(WIN + 2 * (path_len - 1) + 16) // 16) * 16


def prep_kernel(path_len, n_weights, *refs):
    key_cache, value_cache, prefix_ref, accepted_ref, kind_ref = refs[:5]
    small_in = refs[5:10]
    sources = refs[10 : 10 + n_weights]
    refs = refs[10 + n_weights :]
    keys_ref, values_ref, mask_ref, rot_ref = refs[:4]
    targets = refs[4 : 4 + n_weights]
    refs = refs[4 + n_weights :]
    path_ref, parents_ref, freq_ref, q_gain_ref, k_gain_ref = refs[:5]
    small_sems, cache_sems, weight_sems = refs[5:]

    new = mask_ref.shape[0]
    kv_heads, span, head = keys_ref.shape
    cache_len = key_cache.shape[1]
    wide = window_rows(path_len)
    sink_at, win_at = new, new + 16
    end = win_at + wide

    small = [
        pltpu.make_async_copy(source, target, small_sems.at[which])
        for which, (source, target) in enumerate(zip(small_in, refs[:5]))
    ]
    for copy in small:
        copy.start()
    copies = [
        pltpu.make_async_copy(source, target, weight_sems.at[which])
        for which, (source, target) in enumerate(zip(sources, targets))
    ]
    prefix = prefix_ref[0]
    accepted = accepted_ref[0]
    total = prefix + accepted
    low = jnp.maximum(total - WIN, 0)
    start = pl.multiple_of(jnp.minimum((low // 16) * 16, cache_len - wide), 16)
    for which, (cache, buf) in enumerate(((key_cache, keys_ref), (value_cache, values_ref))):
        for kv in range(kv_heads):
            cols = pl.ds(kv * head, head)
            copies.append(
                pltpu.make_async_copy(
                    cache.at[0, pl.ds(start, wide), cols],
                    buf.at[kv, pl.ds(win_at, wide)],
                    cache_sems.at[which, kv, 0],
                )
            )
            copies.append(
                pltpu.make_async_copy(
                    cache.at[0, pl.ds(0, 16), cols],
                    buf.at[kv, pl.ds(sink_at, 16)],
                    cache_sems.at[which, kv, 1],
                )
            )
    for copy in copies:
        copy.start()

    for buf in (keys_ref, values_ref):
        buf[:, 0:new, :] = jnp.zeros((kv_heads, new, head), BF16)
        buf[:, end:span, :] = jnp.zeros((kv_heads, span - end, head), BF16)

    for copy in small:
        copy.wait()
    column = iota((1, span), 1)
    row = jnp.where(column < win_at, column - sink_at, start + column - win_at)
    taken = jnp.zeros((1, span), jnp.bool_)
    for step in range(path_len):
        at = prefix + path_ref[0, step]
        taken = taken | ((row == at) & (step < accepted))
    old = (row < prefix) & ((row < SINK) | (row >= total - WIN))
    in_window = (column >= win_at) & (column < end) & (old | taken)
    in_sink = (column >= sink_at) & (column < win_at) & (row < SINK) & (row < prefix) & (start > 0)
    seen = jnp.where(in_window | in_sink, 0.0, NEG_FILL)
    mask_ref[...] = jnp.broadcast_to(seen, mask_ref.shape)

    down, across = iota((new, new), 0), iota((new, new), 1)
    eye = (down == across).astype(F32)
    back = eye + (down == parents_ref[...]).astype(F32)
    for _ in range((new - 1).bit_length()):
        half = back.astype(BF16)
        back = jnp.minimum(dot(half, half), 1.0)
    reach = dot_first(back.astype(BF16), eye.astype(BF16))
    tree = (kind_ref[0] == 1).astype(F32)
    causal = (across <= down).astype(F32)
    allowed = tree * reach + (1.0 - tree) * causal
    mask_ref[:, 0:new] = jnp.where(allowed > 0.5, 0.0, NEG_FILL)
    depth = tree * (jnp.sum(reach, axis=1, keepdims=True) - 1.0)
    depth = depth + (1.0 - tree) * iota((new, 1), 0).astype(F32)
    angle = (total.astype(F32) + depth) * freq_ref[...]
    lane = iota(angle.shape, 1)
    cosine, sine = jnp.cos(angle), jnp.sin(angle)
    sine = jnp.where(lane < head // 2, -sine, sine)
    for which, gain_ref in enumerate((q_gain_ref, k_gain_ref)):
        gain = jnp.broadcast_to(gain_ref[...], angle.shape)
        rot_ref[2 * which] = cosine * gain
        rot_ref[2 * which + 1] = sine * pltpu.roll(gain, head // 2, 1)
    for copy in copies:
        copy.wait()


def route_kernel(per, new, n_weights, *refs):
    small_in = refs[1:3]
    sources = refs[3 : 3 + n_weights]
    refs = refs[3 + n_weights :]
    pick_ref, combine_ref, weight_ref = refs[:3]
    targets = refs[3 : 3 + n_weights]
    ids_ref, gates_ref, hit_ref, rank_ref, own_ref, sems = refs[3 + n_weights :]
    sources, targets = (*small_in, *sources), (ids_ref, gates_ref, *targets)
    copies = [
        pltpu.make_async_copy(source, target, sems.at[which])
        for which, (source, target) in enumerate(zip(sources, targets))
    ]
    for copy in copies:
        copy.start()
    for copy in copies[:2]:
        copy.wait()

    me = lax.axis_index("tensor")
    all_tokens = ids_ref.shape[1]
    devices = hit_ref.shape[0]
    chips = devices // 2
    tokens = chips * new
    slot = iota((all_tokens, tokens), 1) // new
    odd = slot
    for shift in (4, 2, 1):
        odd = odd ^ (odd >> shift)
    source = (me ^ (2 * slot + (odd & 1))) * new + iota((all_tokens, tokens), 1) % new
    order = (iota((all_tokens, tokens), 0) == source).astype(F32)
    ids = dot(ids_ref[...].astype(F32).astype(BF16), order.astype(BF16))
    gates = lax.dot_general(
        gates_ref[...],
        order,
        (((1,), (0,)), ((), ())),
        precision=lax.Precision.HIGHEST,
        preferred_element_type=F32,
    )
    for rel in range(devices):
        expert = (me ^ step(rel // 2) ^ (rel % 2)).astype(F32)
        named = (ids == expert).astype(F32)
        hit_ref[rel : rel + 1, :] = jnp.max(named, axis=0, keepdims=True)
    before, later = iota((tokens, tokens), 0), iota((tokens, tokens), 1)
    earlier = (before < later) & (before // new == later // new)
    rank_ref[...] = dot(hit_ref[...].astype(BF16), earlier.astype(F32).astype(BF16))
    rows = chips * per
    slot_of = iota((rows, tokens), 1) // new
    row_slot = iota((rows, tokens), 0) // per
    row_rank = (iota((rows, tokens), 0) % per).astype(F32)
    in_first = iota((1, tokens), 1) < new
    for rel in range(devices):
        hit = hit_ref[rel : rel + 1, :] > 0.5
        rank = rank_ref[rel : rel + 1, :]
        chosen = (slot_of == (row_slot ^ (rel // 2))) & hit & (rank == row_rank)
        pick_ref[rel * rows : (rel + 1) * rows, :] = chosen.astype(F32)
        if rel < 2:
            named = ids == (me ^ rel).astype(F32)
            weight = jnp.sum(jnp.where(named, gates, 0.0), axis=0, keepdims=True)
            weight = jnp.sum(jnp.where(chosen, weight, 0.0), axis=1, keepdims=True)
            weight_ref[rel * rows : (rel + 1) * rows, :] = jnp.broadcast_to(
                weight, (rows, weight_ref.shape[1])
            )
        for place in range(per):
            at = rel * per + place
            own_ref[at : at + 1, :] = (in_first & hit & (rank == float(place))).astype(F32)
    first = (iota((tokens, new), 0) == iota((tokens, new), 1)).astype(F32)
    combine_ref[...] = lax.dot_general(
        first.astype(BF16),
        own_ref[...].astype(BF16),
        (((0,), (1,)), ((), ())),
        preferred_element_type=F32,
    )
    for copy in copies[2:]:
        copy.wait()


def project_kernel(count, *refs):
    blocks = refs[:count]
    gain_ref, wq_ref, wkv_ref, wq_sib, wkv_sib = refs[count : count + 5]
    outs = refs[count + 5 :]
    rows = blocks[0].shape[0]
    gain = gain_ref[...]
    values = [(norm_rows(block[...].astype(F32)) * gain).astype(BF16) for block in blocks]
    values = jnp.concatenate(values, axis=0)

    def put(result, at):
        result = result.astype(BF16)
        for j in range(count):
            outs[j][:, at : at + result.shape[1]] = result[j * rows : (j + 1) * rows]

    wide, narrow = wq_ref.shape[1], wkv_ref.shape[0]
    put(dot(values, wq_ref[...]), 0)
    put(dot(values, wq_sib[...]), wide)
    put(dot_last(values, wkv_ref[...]), 2 * wide)
    put(dot_last(values, wkv_sib[...]), 2 * wide + narrow)


def attend_kernel(chips, q_width, kv_ready, *refs):
    got = refs[:chips]
    at = chips + 1 if kv_ready else chips
    keys_ref, values_ref, mask_ref, rot_ref = refs[at : at + 4]
    outs = refs[at + 5 : at + 5 + chips]
    fresh_ref = refs[chips] if kv_ready else refs[-1]
    me = lax.axis_index("tensor")
    chip = me // 2
    new = got[0].shape[0]
    kv_heads, span, head = keys_ref.shape
    per_chip = 2 * q_width // head
    group = chips * per_chip // kv_heads

    if not kv_ready:
        for rel in range(2 * chips):
            left = 2 * q_width + (rel % 2) * head
            fresh_ref[step(rel // 2) ^ (rel % 2)] = got[rel // 2][:, left : left + head]

    def rope(values, which):
        values = norm_rows(values.astype(F32))
        turned = pltpu.roll(values, head // 2, 1)
        return (values * rot_ref[2 * which] + turned * rot_ref[2 * which + 1]).astype(BF16)

    scale = head ** (-0.5) * LOG2E
    for j in range(chips):
        kv = (chip ^ j) * per_chip // group
        key_at, value_at = kv, kv + kv_heads
        if not kv_ready:
            key_at, value_at = me ^ key_at, me ^ value_at
        keys = jnp.concatenate([rope(fresh_ref[key_at], 1), keys_ref[kv, new:span]], axis=0)
        values = jnp.concatenate([fresh_ref[value_at], values_ref[kv, new:span]], axis=0)
        query = jnp.concatenate(
            [rope(got[j][:, h * head : (h + 1) * head], 0) for h in range(per_chip)], axis=0
        )
        score = dot_last(query, keys) * scale
        score = score.reshape(per_chip, new, span) + mask_ref[...][None]
        expo = jnp.exp2(score - jnp.max(score, axis=-1, keepdims=True))
        denom = jnp.sum(expo, axis=-1, keepdims=True).reshape(per_chip * new, 1)
        expo = expo.astype(BF16).reshape(per_chip * new, span)
        result = (dot(expo, values) / denom).astype(BF16)
        for h in range(per_chip):
            outs[j][:, h * head : (h + 1) * head] = result[h * new : (h + 1) * new]


def spread_kernel(chips, picks, *refs):
    got = refs[:chips]
    w_ref, w_sib = refs[chips : chips + 2]
    outs = refs[-chips:]
    depth, width = w_ref.shape
    left = jnp.concatenate([got[j][...] for j in range(chips)], axis=0)
    if picks:
        left = dot(refs[chips + 2][...].astype(BF16), left).astype(BF16)
    each = left.shape[0] // chips
    tile = min(512, width)
    for at in range(0, width, tile):
        part = dot(left[:, :depth], w_ref[:, at : at + tile])
        part = (part + dot(left[:, depth:], w_sib[:, at : at + tile])).astype(BF16)
        for j in range(chips):
            outs[j][:, at : at + tile] = part[j * each : (j + 1) * each]


def select_kernel(chips, *refs):
    blocks = refs[:chips]
    pick_ref, _ = refs[chips : chips + 2]
    sources = refs[chips + 2 : chips + 4]
    picked_ref = refs[chips + 4]
    targets = refs[chips + 5 : chips + 7]
    sems = refs[-1]
    copies = [
        pltpu.make_async_copy(source, target, sems.at[which])
        for which, (source, target) in enumerate(zip(sources, targets))
    ]
    for copy in copies:
        copy.start()
    values = jnp.concatenate([block[...] for block in blocks], axis=0)
    pick = pick_ref[0 : picked_ref.shape[0], :].astype(BF16)
    picked_ref[...] = dot(pick, values)
    for copy in copies:
        copy.wait()


def hidden_kernel(chips, *refs):
    got = refs[:chips]
    own_ref, out_ref = refs[chips:]
    total = own_ref[...].astype(F32)
    for j in range(chips):
        total = total + got[j][...].astype(F32)
    out_ref[...] = total


def rows_kernel(chips, *refs):
    got = refs[:chips]
    picked_ref, gain_ref, _, own_ref, other_ref = refs[chips:]
    hidden = picked_ref[...]
    for j in range(chips):
        hidden = hidden + got[j][...].astype(F32)
    normed = (norm_rows(hidden) * gain_ref[...]).astype(BF16)
    half = own_ref.shape[0]
    own_ref[...] = normed[:half]
    other_ref[...] = normed[half:]


def expert_kernel(own_ref, other_ref, gate_ref, up_ref, down_ref, own_out, other_out):
    left = jnp.concatenate([own_ref[...].astype(F32), other_ref[...].astype(F32)], axis=0)
    left = left.astype(BF16)
    gate = dot_last(left, gate_ref[0])
    up = dot_last(left, up_ref[0])
    inner = (gate / (1.0 + jnp.exp(-gate)) * up).astype(BF16)
    result = dot(inner, down_ref[0])
    half = own_ref.shape[0]
    own_out[...] = result[:half]
    other_out[...] = result[half:].astype(BF16)


def pack_kernel(chips, per, own_ref, other_ref, weight_ref, *outs):
    half = own_ref.shape[0]
    own = own_ref[...] * weight_ref[:half, 0:1]
    other = other_ref[...].astype(F32) * weight_ref[half:, 0:1]
    for j in range(chips):
        at = slice(j * per, (j + 1) * per)
        outs[j][...] = jnp.concatenate([own[at], other[at]], axis=0).astype(BF16)


def combine_kernel(chips, *refs):
    hidden_ref, combine_ref = refs[:2]
    got = refs[2 : 2 + chips]
    out_ref = refs[2 + chips]
    rows = jnp.concatenate([block[...].astype(F32) for block in got], axis=0)
    moe = dot(combine_ref[...].astype(BF16), rows.astype(BF16))
    out_ref[...] = (hidden_ref[...] + moe).astype(BF16)


def body(
    residual_in,
    attn_gain,
    w_query,
    w_keyval,
    query_gain,
    key_gain,
    w_out,
    ffn_gain,
    w_gate,
    w_up,
    w_down,
    key_cache,
    value_cache,
    prefix_lens,
    accepted,
    accept_path,
    parents,
    slot_kinds,
    expert_ids,
    gate_probs,
):
    devices = lax.axis_size("tensor")
    chips = devices // 2
    new, width = residual_in.shape
    head = query_gain.shape[0]
    kv_heads = key_cache.shape[2] // head
    q_width = w_query.shape[1]
    new_width = w_keyval.shape[0]
    all_tokens, top = expert_ids.shape
    tokens = chips * new
    per = new * top // EXPERTS
    path_len = accept_path.shape[1]
    rows = 2 * chips * per
    assert key_cache.shape[0] == 1 and w_gate.shape[0] == 1
    assert devices & (devices - 1) == 0
    vmem, smem, hbm, anywhere = pltpu.VMEM, pltpu.SMEM, pltpu.HBM, pl.ANY

    blocks = exchange([residual_in] * chips)
    wq_sib = hop(w_query, 1)
    wkv_sib = hop(w_keyval, 1)

    freq = ROPE_BASE ** (-2.0 * np.arange(head // 2) / head)
    freq = jnp.asarray(np.concatenate([freq, freq])[None, :], F32)
    span = -(-(new + 16 + window_rows(path_len)) // 128) * 128
    weights = [attn_gain[None, :], w_query, w_keyval]
    keys, values, mask, rot, gain, wq, wkv = call(
        functools.partial(prep_kernel, path_len, len(weights)),
        "prep",
        [
            in_vmem((kv_heads, span, head), BF16),
            in_vmem((kv_heads, span, head), BF16),
            in_vmem((new, span), F32),
            in_vmem((4, new, head), F32),
        ]
        + [in_vmem(w.shape, w.dtype) for w in weights],
        [
            (key_cache, hbm),
            (value_cache, hbm),
            (prefix_lens, smem),
            (accepted, smem),
            (slot_kinds, smem),
            (accept_path, hbm),
            (parents, hbm),
            (freq, hbm),
            (query_gain[None, :], hbm),
            (key_gain[None, :], hbm),
        ]
        + [(w, hbm) for w in weights],
        [
            pltpu.SMEM((1, path_len), jnp.int32),
            pltpu.VMEM((1, new), jnp.int32),
            pltpu.VMEM((1, head), F32),
            pltpu.VMEM((1, head), F32),
            pltpu.VMEM((1, head), F32),
            pltpu.SemaphoreType.DMA((5,)),
            pltpu.SemaphoreType.DMA((2, kv_heads, 2)),
            pltpu.SemaphoreType.DMA((len(weights),)),
        ],
        limit=16,
        moved=4 * span * kv_heads * head * 2,
    )

    projected = call(
        functools.partial(project_kernel, chips),
        "project",
        [in_vmem((new, 2 * (q_width + new_width)), BF16)] * chips,
        [(block, vmem) for block in blocks]
        + [(w, vmem) for w in (gain, wq, wkv, wq_sib, wkv_sib)],
        limit=16,
        flops=4 * tokens * width * (q_width + new_width),
        moved=4 * width * (q_width + new_width),
    )
    got = exchange(projected)

    weights = [ffn_gain[None, :], w_out, w_down]
    pick, combine, weight, ffn, wo, wd = call(
        functools.partial(route_kernel, per, new, len(weights)),
        "route",
        [
            in_vmem((chips * rows, tokens), F32),
            in_vmem((new, devices * per), F32),
            in_vmem((rows, 128), F32),
        ]
        + [in_vmem(w.shape, w.dtype) for w in weights],
        [(projected[0], anywhere), (expert_ids.T, hbm), (gate_probs.T, hbm)]
        + [(w, hbm) for w in weights],
        [
            pltpu.VMEM((top, all_tokens), jnp.int32),
            pltpu.VMEM((top, all_tokens), F32),
            pltpu.VMEM((devices, tokens), F32),
            pltpu.VMEM((devices, tokens), F32),
            pltpu.VMEM((devices * per, tokens), F32),
            pltpu.SemaphoreType.DMA((2 + len(weights),)),
        ],
        limit=16,
        moved=4 * width * (q_width + w_down.shape[1]),
    )
    kv_ready = []
    if new_width != head:
        pieces = [None] * devices
        for rel in range(devices):
            left = 2 * q_width + (rel % 2) * new_width
            pieces[step(rel // 2) ^ (rel % 2)] = got[rel // 2][:, left : left + new_width]
        pieces = jnp.stack(pieces)[lax.axis_index("tensor") ^ jnp.arange(devices)]
        pieces = pieces.transpose(1, 0, 2).reshape(new, 2 * kv_heads, head)
        kv_ready = [(pieces.transpose(1, 0, 2), vmem)]
    *attended, wo = call(
        functools.partial(attend_kernel, chips, q_width, bool(kv_ready)),
        "attend",
        [in_vmem((new, 2 * q_width), BF16)] * chips + [in_vmem(wo.shape, wo.dtype)],
        [(block, vmem) for block in got]
        + kv_ready
        + [(keys, vmem), (values, vmem), (mask, vmem), (rot, vmem)]
        + [(wo, vmem)],
        [] if kv_ready else [pltpu.VMEM((devices, new, head), BF16)],
        limit=16,
        same={chips + len(kv_ready) + 4: chips},
        flops=8 * new * chips * q_width * span,
        moved=4 * span * kv_heads * head,
    )
    wo_sib = hop(wo, 1)
    heads = exchange(attended)
    picked, wg, wu = call(
        functools.partial(select_kernel, chips),
        "select",
        [in_vmem((rows, width), F32)] + [in_vmem(w.shape, w.dtype) for w in (w_gate, w_up)],
        [(block, vmem) for block in blocks]
        + [(pick, vmem), (attended[0], anywhere), (w_gate, hbm), (w_up, hbm)],
        [pltpu.SemaphoreType.DMA((2,))],
        limit=8,
        flops=2 * rows * width * tokens,
        moved=8 * width * w_gate.shape[1],
    )

    def spread(name, each, more):
        return call(
            functools.partial(spread_kernel, chips, name == "experts"),
            name,
            [in_vmem((each, width), BF16)] * chips,
            [(block, vmem) for block in heads] + [(wo, vmem), (wo_sib, vmem)] + more,
            limit=16,
            flops=4 * chips * each * width * q_width,
            moved=4 * q_width * width,
        )

    partial = spread("experts", rows, [(pick, vmem), (wg, anywhere)])
    for_experts = exchange(partial)
    partial = spread("slots", new, [(partial[0], anywhere)])
    for_slots = exchange(partial)

    own, other = call(
        functools.partial(rows_kernel, chips),
        "rows",
        [in_vmem((rows // 2, width), BF16)] * 2,
        [(block, vmem) for block in for_experts]
        + [(picked, vmem), (ffn, vmem), (partial[0], anywhere)],
        limit=8,
        moved=2 * chips * rows * width,
    )
    own_out, other_out = call(
        expert_kernel,
        "expert",
        [in_vmem((rows // 2, width), F32), in_vmem((rows // 2, width), BF16)],
        [(own, vmem), (hop(other, 1), vmem), (wg, vmem), (wu, vmem), (wd, vmem)],
        limit=16,
        flops=6 * rows * width * w_gate.shape[1],
        moved=6 * width * w_gate.shape[1],
    )
    results = call(
        functools.partial(pack_kernel, chips, per),
        "pack",
        [in_vmem((2 * per, width), BF16)] * chips,
        [(own_out, vmem), (hop(other_out, 1), vmem), (weight, vmem)],
        limit=8,
        moved=4 * rows * width,
    )
    returned = exchange(results)
    hidden = call(
        functools.partial(hidden_kernel, chips),
        "hidden",
        [in_vmem((new, width), F32)],
        [(block, vmem) for block in for_slots] + [(residual_in, vmem)],
        limit=8,
        moved=2 * chips * new * width,
    )[0]
    return call(
        functools.partial(combine_kernel, chips),
        "combine",
        [jax.ShapeDtypeStruct((new, width), BF16)],
        [(hidden, vmem), (combine, vmem)] + [(block, vmem) for block in returned],
        limit=8,
        moved=6 * new * width,
    )[0]


def solution(mesh):
    in_specs = (
        P(("group", "tensor"), None),
        P(),
        P(None, "tensor"),
        P("tensor", None),
        P(),
        P(),
        P("tensor", None),
        P(),
        P("tensor", None, None),
        P("tensor", None, None),
        P("tensor", None, None),
        P(("group", "tensor"), None, None),
        P(("group", "tensor"), None, None),
        P(("group", "tensor")),
        P(("group", "tensor")),
        P(("group", "tensor"), None),
        P(("group", "tensor"), None),
        P(("group", "tensor")),
        P("group", None),
        P("group", None),
    )
    out_specs = P(("group", "tensor"), None)
    return jax.shard_map(body, mesh=mesh, in_specs=in_specs, out_specs=out_specs, check_vma=False)
```

```python
import functools
import math

import jax
import jax.numpy as jnp
import numpy as np
from jax import lax
from jax.experimental import pallas as pl
from jax.experimental.pallas import tpu as pltpu
from jax.sharding import PartitionSpec as P

EXPERTS = 128
SINK = 4
WIN = 512

EPSILON = 1e-06
NEG_FILL = -1e30
ROPE_BASE = 1000000.0
LOG2E = math.log2(math.e)
F32 = jnp.float32
BF16 = jnp.bfloat16
MIB = 1 << 20


def step(j):
    return 2 * j + bin(j).count("1") % 2


def iota(shape, dim):
    return lax.broadcasted_iota(jnp.int32, shape, dim)


def dot(left, right):
    return jnp.dot(left, right, preferred_element_type=F32)


def dot_last(left, right):
    return lax.dot_general(left, right, (((1,), (1,)), ((), ())), preferred_element_type=F32)


def dot_first(left, right):
    return lax.dot_general(left, right, (((0,), (0,)), ((), ())), preferred_element_type=F32)


def norm_rows(values):
    return values * lax.rsqrt(jnp.mean(values * values, axis=-1, keepdims=True) + EPSILON)


def in_vmem(shape, dtype):
    return pltpu.VMEM(shape, dtype)


def call(kernel, name, outs, args, scratch=(), limit=16, flops=0, moved=0, same=None):
    arrays = []
    specs = []
    for array, space in args:
        if space is pltpu.HBM or space is pltpu.VMEM:
            array = pltpu.with_memory_space_constraint(array, space)
        arrays.append(array)
        specs.append(pl.BlockSpec(memory_space=space))
    return pl.pallas_call(
        kernel,
        out_shape=outs,
        in_specs=specs,
        out_specs=[pl.BlockSpec(memory_space=pltpu.VMEM) for _ in outs],
        scratch_shapes=list(scratch),
        input_output_aliases=same or {},
        compiler_params=pltpu.CompilerParams(vmem_limit_bytes=limit * MIB),
        cost_estimate=pl.CostEstimate(flops=flops, bytes_accessed=moved, transcendentals=0),
        name=name,
    )(*arrays)


def hop(value, step):
    devices = lax.axis_size("tensor")
    return lax.ppermute(value, "tensor", [(i, i ^ step) for i in range(devices)])


def exchange(blocks):
    return [blocks[0]] + [hop(blocks[j], step(j)) for j in range(1, len(blocks))]


def turned(blocks):
    return [blocks[0], *blocks[:0:-1]]


def swap(blocks):
    devices = lax.axis_size("tensor")
    groups = [[step(p) ^ core for p in range(devices // 2)] for core in range(2)]
    return lax.all_to_all(
        blocks, "tensor", split_axis=0, concat_axis=0, axis_index_groups=groups, tiled=True
    )


def window_rows(path_len):
    return -(-(WIN + 2 * (path_len - 1) + 16) // 16) * 16


def prep_kernel(path_len, n_weights, *refs):
    key_cache, value_cache, prefix_ref, accepted_ref, kind_ref = refs[:5]
    small_in = refs[5:10]
    sources = refs[10 : 10 + n_weights]
    refs = refs[10 + n_weights :]
    keys_ref, values_ref, mask_ref, allow_ref, rot_ref = refs[:5]
    targets = refs[5 : 5 + n_weights]
    refs = refs[5 + n_weights :]
    path_ref, parents_ref, freq_ref, q_gain_ref, k_gain_ref = refs[:5]
    small_sems, cache_sems, weight_sems = refs[5:]

    new = mask_ref.shape[0]
    kv_heads, span, head = keys_ref.shape
    cache_len = key_cache.shape[1]
    wide = window_rows(path_len)
    sink_at, win_at = new, new + 16
    end = win_at + wide

    small = [
        pltpu.make_async_copy(source, target, small_sems.at[which])
        for which, (source, target) in enumerate(zip(small_in, refs[:5]))
    ]
    for copy in small:
        copy.start()
    copies = [
        pltpu.make_async_copy(source, target, weight_sems.at[which])
        for which, (source, target) in enumerate(zip(sources, targets))
    ]
    prefix = prefix_ref[0]
    accepted = accepted_ref[0]
    total = prefix + accepted
    low = jnp.maximum(total - WIN, 0)
    start = pl.multiple_of(jnp.minimum((low // 16) * 16, cache_len - wide), 16)
    for which, (cache, buf) in enumerate(((key_cache, keys_ref), (value_cache, values_ref))):
        for kv in range(kv_heads):
            cols = pl.ds(kv * head, head)
            copies.append(
                pltpu.make_async_copy(
                    cache.at[0, pl.ds(start, wide), cols],
                    buf.at[kv, pl.ds(win_at, wide)],
                    cache_sems.at[which, kv, 0],
                )
            )
            copies.append(
                pltpu.make_async_copy(
                    cache.at[0, pl.ds(0, 16), cols],
                    buf.at[kv, pl.ds(sink_at, 16)],
                    cache_sems.at[which, kv, 1],
                )
            )
    for copy in copies:
        copy.start()

    for buf in (keys_ref, values_ref):
        buf[:, 0:new, :] = jnp.zeros((kv_heads, new, head), BF16)
        buf[:, end:span, :] = jnp.zeros((kv_heads, span - end, head), BF16)

    for copy in small:
        copy.wait()
    column = iota((1, span), 1)
    row = jnp.where(column < win_at, column - sink_at, start + column - win_at)
    taken = jnp.zeros((1, span), jnp.bool_)
    for step in range(path_len):
        at = prefix + path_ref[0, step]
        taken = taken | ((row == at) & (step < accepted))
    old = (row < prefix) & ((row < SINK) | (row >= total - WIN))
    in_window = (column >= win_at) & (column < end) & (old | taken)
    in_sink = (column >= sink_at) & (column < win_at) & (row < SINK) & (row < prefix) & (start > 0)
    seen = jnp.where(in_window | in_sink, 0.0, NEG_FILL)
    mask_ref[...] = jnp.broadcast_to(seen, mask_ref.shape)

    down, across = iota((new, new), 0), iota((new, new), 1)
    eye = (down == across).astype(F32)
    back = eye + (down == parents_ref[...]).astype(F32)
    for _ in range((new - 1).bit_length()):
        half = back.astype(BF16)
        back = jnp.minimum(dot(half, half), 1.0)
    reach = dot_first(back.astype(BF16), eye.astype(BF16))
    tree = (kind_ref[0] == 1).astype(F32)
    causal = (across <= down).astype(F32)
    allowed = tree * reach + (1.0 - tree) * causal
    allow_ref[...] = jnp.where(allowed > 0.5, 0.0, NEG_FILL)
    depth = tree * (jnp.sum(reach, axis=1, keepdims=True) - 1.0)
    depth = depth + (1.0 - tree) * iota((new, 1), 0).astype(F32)
    angle = (total.astype(F32) + depth) * freq_ref[...]
    lane = iota(angle.shape, 1)
    cosine, sine = jnp.cos(angle), jnp.sin(angle)
    sine = jnp.where(lane < head // 2, -sine, sine)
    for which, gain_ref in enumerate((q_gain_ref, k_gain_ref)):
        gain = jnp.broadcast_to(gain_ref[...], angle.shape)
        rot_ref[2 * which] = cosine * gain
        rot_ref[2 * which + 1] = sine * pltpu.roll(gain, head // 2, 1)
    for copy in copies:
        copy.wait()


def route_kernel(per, new, n_weights, *refs):
    small_in = refs[1:3]
    sources = refs[3 : 3 + n_weights]
    refs = refs[3 + n_weights :]
    pick_ref, combine_ref, weight_ref = refs[:3]
    targets = refs[3 : 3 + n_weights]
    ids_ref, gates_ref, hit_ref, rank_ref, own_ref, sems = refs[3 + n_weights :]
    sources, targets = (*small_in, *sources), (ids_ref, gates_ref, *targets)
    copies = [
        pltpu.make_async_copy(source, target, sems.at[which])
        for which, (source, target) in enumerate(zip(sources, targets))
    ]
    for copy in copies:
        copy.start()
    for copy in copies[:2]:
        copy.wait()

    me = lax.axis_index("tensor")
    all_tokens = ids_ref.shape[1]
    devices = hit_ref.shape[0]
    chips = devices // 2
    tokens = chips * new
    slot = iota((all_tokens, tokens), 1) // new
    odd = slot
    for shift in (4, 2, 1):
        odd = odd ^ (odd >> shift)
    source = (me ^ (2 * slot + (odd & 1))) * new + iota((all_tokens, tokens), 1) % new
    order = (iota((all_tokens, tokens), 0) == source).astype(F32)
    ids = dot(ids_ref[...].astype(F32).astype(BF16), order.astype(BF16))
    gates = lax.dot_general(
        gates_ref[...],
        order,
        (((1,), (0,)), ((), ())),
        precision=lax.Precision.HIGHEST,
        preferred_element_type=F32,
    )
    for rel in range(devices):
        expert = (me ^ step(rel // 2) ^ (rel % 2)).astype(F32)
        named = (ids == expert).astype(F32)
        hit_ref[rel : rel + 1, :] = jnp.max(named, axis=0, keepdims=True)
    before, later = iota((tokens, tokens), 0), iota((tokens, tokens), 1)
    earlier = (before < later) & (before // new == later // new)
    rank_ref[...] = dot(hit_ref[...].astype(BF16), earlier.astype(F32).astype(BF16))
    rows = chips * per
    slot_of = iota((rows, tokens), 1) // new
    row_slot = iota((rows, tokens), 0) // per
    row_rank = (iota((rows, tokens), 0) % per).astype(F32)
    in_first = iota((1, tokens), 1) < new
    for rel in range(devices):
        hit = hit_ref[rel : rel + 1, :] > 0.5
        rank = rank_ref[rel : rel + 1, :]
        chosen = (slot_of == (row_slot ^ (rel // 2))) & hit & (rank == row_rank)
        pick_ref[rel * rows : (rel + 1) * rows, :] = chosen.astype(F32)
        if rel < 2:
            named = ids == (me ^ rel).astype(F32)
            weight = jnp.sum(jnp.where(named, gates, 0.0), axis=0, keepdims=True)
            weight = jnp.sum(jnp.where(chosen, weight, 0.0), axis=1, keepdims=True)
            weight_ref[rel * rows : (rel + 1) * rows, :] = jnp.broadcast_to(
                weight, (rows, weight_ref.shape[1])
            )
        for place in range(per):
            at = rel * per + place
            own_ref[at : at + 1, :] = (in_first & hit & (rank == float(place))).astype(F32)
    first = (iota((tokens, new), 0) == iota((tokens, new), 1)).astype(F32)
    combine_ref[...] = lax.dot_general(
        first.astype(BF16),
        own_ref[...].astype(BF16),
        (((0,), (1,)), ((), ())),
        preferred_element_type=F32,
    )
    for copy in copies[2:]:
        copy.wait()


def project_kernel(count, *refs):
    blocks = refs[:count]
    gain_ref, wq_ref, wkv_ref, wq_sib, wkv_sib = refs[count : count + 5]
    outs = refs[count + 5 :]
    rows = blocks[0].shape[0]
    gain = gain_ref[...]
    values = [(norm_rows(block[...].astype(F32)) * gain).astype(BF16) for block in blocks]
    values = jnp.concatenate(values, axis=0)

    def put(result, at):
        result = result.astype(BF16)
        for j in range(count):
            outs[j][:, at : at + result.shape[1]] = result[j * rows : (j + 1) * rows]

    wide, narrow = wq_ref.shape[1], wkv_ref.shape[0]
    put(dot(values, wq_ref[...]), 0)
    put(dot(values, wq_sib[...]), wide)
    put(dot_last(values, wkv_ref[...]), 2 * wide)
    put(dot_last(values, wkv_sib[...]), 2 * wide + narrow)


def rope(values, rot_ref, which):
    values = norm_rows(values.astype(F32))
    turn = pltpu.roll(values, values.shape[1] // 2, 1)
    return (values * rot_ref[2 * which] + turn * rot_ref[2 * which + 1]).astype(BF16)


def attend_cache(block_ref, j, keys_ref, values_ref, mask_ref, rot_ref, chips, q_width):
    chip = lax.axis_index("tensor") // 2
    kv_heads, span, head = keys_ref.shape
    new = mask_ref.shape[0]
    per_chip = 2 * q_width // head
    kv = (chip ^ j) * per_chip // (chips * per_chip // kv_heads)
    query = jnp.concatenate(
        [rope(block_ref[:, h * head : (h + 1) * head], rot_ref, 0) for h in range(per_chip)], axis=0
    )
    score = dot_last(query, keys_ref[kv]) * (head ** (-0.5) * LOG2E)
    score = score.reshape(per_chip, new, span) + mask_ref[...][None]
    top = jnp.max(score, axis=-1, keepdims=True)
    expo = jnp.exp2(score - top)
    total = jnp.sum(expo, axis=-1, keepdims=True).reshape(per_chip * new, 1)
    expo = expo.astype(BF16).reshape(per_chip * new, span)
    return query, total, top.reshape(per_chip * new, 1), dot(expo, values_ref[kv])


def cache_kernel(chips, q_width, some, *refs):
    got = refs[: len(some)]
    keys_ref, values_ref, mask_ref, rot_ref = refs[len(some) : len(some) + 4]
    outs = refs[len(some) + 4 :]
    for at, j in enumerate(some):
        query, total, top, value = attend_cache(
            got[at], j, keys_ref, values_ref, mask_ref, rot_ref, chips, q_width
        )
        query_ref, state_ref = outs[2 * at : 2 * at + 2]
        query_ref[...] = query
        state_ref[0] = value
        state_ref[1] = jnp.broadcast_to(total, value.shape)
        state_ref[2] = jnp.broadcast_to(top, value.shape)


def attend_kernel(chips, q_width, some, kv_ready, *refs):
    got = refs[:chips]
    done = refs[chips : chips + 2 * len(some)]
    refs = refs[chips + 2 * len(some) :]
    fresh_ref = refs[0] if kv_ready else refs[-1]
    refs = refs[kv_ready:]
    keys_ref, values_ref, mask_ref, allow_ref, rot_ref, _ = refs[:6]
    outs = refs[6 : 6 + chips]
    me = lax.axis_index("tensor")
    chip = me // 2
    kv_heads, _, head = keys_ref.shape
    new = mask_ref.shape[0]
    per_chip = 2 * q_width // head
    if not kv_ready:
        for rel in range(2 * chips):
            left = 2 * q_width + (rel % 2) * head
            fresh_ref[step(rel // 2) ^ (rel % 2)] = got[rel // 2][:, left : left + head]

    for j in range(chips):
        if j in some:
            query_ref, state_ref = done[2 * some.index(j) : 2 * some.index(j) + 2]
            query, value = query_ref[...], state_ref[0]
            total, top = state_ref[1][:, 0:1], state_ref[2][:, 0:1]
        else:
            query, total, top, value = attend_cache(
                got[j], j, keys_ref, values_ref, mask_ref, rot_ref, chips, q_width
            )
        key_at = (chip ^ j) * per_chip // (chips * per_chip // kv_heads)
        value_at = key_at + kv_heads
        if not kv_ready:
            key_at, value_at = me ^ key_at, me ^ value_at
        score = dot_last(query, rope(fresh_ref[key_at], rot_ref, 1)) * (head ** (-0.5) * LOG2E)
        score = score.reshape(per_chip, new, new) + allow_ref[...][None]
        score = score.reshape(per_chip * new, new)
        peak = jnp.maximum(top, jnp.max(score, axis=-1, keepdims=True))
        shrink = jnp.exp2(top - peak)
        expo = jnp.exp2(score - peak)
        total = total * shrink + jnp.sum(expo, axis=-1, keepdims=True)
        value = value * shrink + dot(expo.astype(BF16), fresh_ref[value_at])
        result = (value / total).astype(BF16)
        for h in range(per_chip):
            outs[j][:, h * head : (h + 1) * head] = result[h * new : (h + 1) * new]


def spread_kernel(chips, picks, *refs):
    got = turned(refs[:chips])
    w_ref, w_sib = refs[chips : chips + 2]
    outs = refs[-chips:]
    depth, width = w_ref.shape
    left = jnp.concatenate([got[j][...] for j in range(chips)], axis=0)
    if picks:
        left = dot(refs[chips + 2][...].astype(BF16), left).astype(BF16)
    each = left.shape[0] // chips
    tile = min(512, width)
    for at in range(0, width, tile):
        part = dot(left[:, :depth], w_ref[:, at : at + tile])
        part = (part + dot(left[:, depth:], w_sib[:, at : at + tile])).astype(BF16)
        for j in range(chips):
            outs[j][:, at : at + tile] = part[j * each : (j + 1) * each]


def select_kernel(chips, *refs):
    blocks = refs[:chips]
    pick_ref, _ = refs[chips : chips + 2]
    sources = refs[chips + 2 : chips + 4]
    picked_ref = refs[chips + 4]
    targets = refs[chips + 5 : chips + 7]
    sems = refs[-1]
    copies = [
        pltpu.make_async_copy(source, target, sems.at[which])
        for which, (source, target) in enumerate(zip(sources, targets))
    ]
    for copy in copies:
        copy.start()
    values = jnp.concatenate([block[...] for block in blocks], axis=0)
    pick = pick_ref[0 : picked_ref.shape[0], :].astype(BF16)
    picked_ref[...] = dot(pick, values)
    for copy in copies:
        copy.wait()


def hidden_kernel(chips, *refs):
    got = refs[:chips]
    own_ref, out_ref = refs[chips:]
    total = own_ref[...].astype(F32)
    for j in range(chips):
        total = total + got[j][...].astype(F32)
    out_ref[...] = total


def rows_kernel(chips, *refs):
    got = refs[:chips]
    picked_ref, gain_ref, _, own_ref, other_ref = refs[chips:]
    hidden = picked_ref[...]
    for j in range(chips):
        hidden = hidden + got[j][...].astype(F32)
    normed = (norm_rows(hidden) * gain_ref[...]).astype(BF16)
    half = own_ref.shape[0]
    own_ref[...] = normed[:half]
    other_ref[...] = normed[half:]


def expert_kernel(own_ref, other_ref, gate_ref, up_ref, down_ref, own_out, other_out):
    left = jnp.concatenate([own_ref[...].astype(F32), other_ref[...].astype(F32)], axis=0)
    left = left.astype(BF16)
    gate = dot_last(left, gate_ref[0])
    up = dot_last(left, up_ref[0])
    inner = (gate / (1.0 + jnp.exp(-gate)) * up).astype(BF16)
    result = dot(inner, down_ref[0])
    half = own_ref.shape[0]
    own_out[...] = result[:half]
    other_out[...] = result[half:].astype(BF16)


def pack_kernel(per, own_ref, other_ref, weight_ref, out_ref):
    chip = lax.axis_index("tensor") // 2
    half = own_ref.shape[0]
    own = own_ref[...] * weight_ref[:half, 0:1]
    other = other_ref[...].astype(F32) * weight_ref[half:, 0:1]
    for j in range(out_ref.shape[0]):
        at = slice(j * per, (j + 1) * per)
        out_ref[chip ^ j] = jnp.concatenate([own[at], other[at]], axis=0).astype(BF16)


def combine_kernel(hidden_ref, combine_ref, got_ref, out_ref):
    chip = lax.axis_index("tensor") // 2
    rows = [got_ref[chip ^ j].astype(F32) for j in range(got_ref.shape[0])]
    moe = dot(combine_ref[...].astype(BF16), jnp.concatenate(rows, axis=0).astype(BF16))
    out_ref[...] = (hidden_ref[...] + moe).astype(BF16)


def body(
    residual_in,
    attn_gain,
    w_query,
    w_keyval,
    query_gain,
    key_gain,
    w_out,
    ffn_gain,
    w_gate,
    w_up,
    w_down,
    key_cache,
    value_cache,
    prefix_lens,
    accepted,
    accept_path,
    parents,
    slot_kinds,
    expert_ids,
    gate_probs,
):
    devices = lax.axis_size("tensor")
    chips = devices // 2
    new, width = residual_in.shape
    head = query_gain.shape[0]
    kv_heads = key_cache.shape[2] // head
    q_width = w_query.shape[1]
    new_width = w_keyval.shape[0]
    all_tokens, top = expert_ids.shape
    tokens = chips * new
    per = new * top // EXPERTS
    path_len = accept_path.shape[1]
    rows = 2 * chips * per
    assert key_cache.shape[0] == 1 and w_gate.shape[0] == 1
    assert devices & (devices - 1) == 0
    vmem, smem, hbm, anywhere = pltpu.VMEM, pltpu.SMEM, pltpu.HBM, pl.ANY

    blocks = exchange([residual_in] * chips)
    wq_sib = hop(w_query, 1)
    wkv_sib = hop(w_keyval, 1)

    freq = ROPE_BASE ** (-2.0 * np.arange(head // 2) / head)
    freq = jnp.asarray(np.concatenate([freq, freq])[None, :], F32)
    span = -(-(new + 16 + window_rows(path_len)) // 128) * 128
    weights = [attn_gain[None, :], w_query, w_keyval]
    keys, values, mask, allow, rot, gain, wq, wkv = call(
        functools.partial(prep_kernel, path_len, len(weights)),
        "prep",
        [
            in_vmem((kv_heads, span, head), BF16),
            in_vmem((kv_heads, span, head), BF16),
            in_vmem((new, span), F32),
            in_vmem((new, new), F32),
            in_vmem((4, new, head), F32),
        ]
        + [in_vmem(w.shape, w.dtype) for w in weights],
        [
            (key_cache, hbm),
            (value_cache, hbm),
            (prefix_lens, smem),
            (accepted, smem),
            (slot_kinds, smem),
            (accept_path, hbm),
            (parents, hbm),
            (freq, hbm),
            (query_gain[None, :], hbm),
            (key_gain[None, :], hbm),
        ]
        + [(w, hbm) for w in weights],
        [
            pltpu.SMEM((1, path_len), jnp.int32),
            pltpu.VMEM((1, new), jnp.int32),
            pltpu.VMEM((1, head), F32),
            pltpu.VMEM((1, head), F32),
            pltpu.VMEM((1, head), F32),
            pltpu.SemaphoreType.DMA((5,)),
            pltpu.SemaphoreType.DMA((2, kv_heads, 2)),
            pltpu.SemaphoreType.DMA((len(weights),)),
        ],
        limit=16,
        moved=4 * span * kv_heads * head * 2,
    )

    projected = call(
        functools.partial(project_kernel, chips),
        "project",
        [in_vmem((new, 2 * (q_width + new_width)), BF16)] * chips,
        [(block, vmem) for block in blocks]
        + [(w, vmem) for w in (gain, wq, wkv, wq_sib, wkv_sib)],
        limit=16,
        flops=4 * tokens * width * (q_width + new_width),
        moved=4 * width * (q_width + new_width),
    )
    got = exchange(projected)

    weights = [ffn_gain[None, :], w_out, w_down]
    pick, combine, weight, ffn, wo, wd = call(
        functools.partial(route_kernel, per, new, len(weights)),
        "route",
        [
            in_vmem((chips * rows, tokens), F32),
            in_vmem((new, devices * per), F32),
            in_vmem((rows, 128), F32),
        ]
        + [in_vmem(w.shape, w.dtype) for w in weights],
        [(projected[0], anywhere), (expert_ids.T, hbm), (gate_probs.T, hbm)]
        + [(w, hbm) for w in weights],
        [
            pltpu.VMEM((top, all_tokens), jnp.int32),
            pltpu.VMEM((top, all_tokens), F32),
            pltpu.VMEM((devices, tokens), F32),
            pltpu.VMEM((devices, tokens), F32),
            pltpu.VMEM((devices * per, tokens), F32),
            pltpu.SemaphoreType.DMA((2 + len(weights),)),
        ],
        limit=16,
        moved=4 * width * (q_width + w_down.shape[1]),
    )
    kv_ready = []
    if new_width != head:
        pieces = [None] * devices
        for rel in range(devices):
            left = 2 * q_width + (rel % 2) * new_width
            pieces[step(rel // 2) ^ (rel % 2)] = got[rel // 2][:, left : left + new_width]
        pieces = jnp.stack(pieces)[lax.axis_index("tensor") ^ jnp.arange(devices)]
        pieces = pieces.transpose(1, 0, 2).reshape(new, 2 * kv_heads, head)
        kv_ready = [(pieces.transpose(1, 0, 2), vmem)]
    some = [j for j in turned(range(chips)) if j != 1]
    lines = 2 * q_width // head * new
    cached = call(
        functools.partial(cache_kernel, chips, q_width, some),
        "cache",
        [in_vmem((lines, head), BF16), in_vmem((3, lines, head), F32)] * len(some),
        [(got[j], vmem) for j in some]
        + [(keys, vmem), (values, vmem), (mask, vmem), (rot, vmem)],
        limit=16,
        flops=8 * new * len(some) * q_width * span,
        moved=4 * span * kv_heads * head,
    )
    *attended, wo = call(
        functools.partial(attend_kernel, chips, q_width, some, len(kv_ready)),
        "attend",
        [in_vmem((new, 2 * q_width), BF16)] * chips + [in_vmem(wo.shape, wo.dtype)],
        [(block, vmem) for block in got]
        + [(array, vmem) for array in cached]
        + kv_ready
        + [(keys, vmem), (values, vmem), (mask, vmem), (allow, vmem), (rot, vmem), (wo, vmem)],
        [] if kv_ready else [pltpu.VMEM((devices, new, head), BF16)],
        limit=16,
        same={chips + len(cached) + len(kv_ready) + 5: chips},
        flops=8 * new * q_width * span,
        moved=4 * span * kv_heads * head,
    )
    wo_sib = hop(wo, 1)
    heads = exchange(attended)
    picked, wg, wu = call(
        functools.partial(select_kernel, chips),
        "select",
        [in_vmem((rows, width), F32)] + [in_vmem(w.shape, w.dtype) for w in (w_gate, w_up)],
        [(block, vmem) for block in blocks]
        + [(pick, vmem), (attended[0], anywhere), (w_gate, hbm), (w_up, hbm)],
        [pltpu.SemaphoreType.DMA((2,))],
        limit=8,
        flops=2 * rows * width * tokens,
        moved=8 * width * w_gate.shape[1],
    )

    def spread(name, each, more):
        return call(
            functools.partial(spread_kernel, chips, name == "experts"),
            name,
            [in_vmem((each, width), BF16)] * chips,
            [(block, vmem) for block in turned(heads)]
            + [(wo, vmem), (wo_sib, vmem)]
            + more,
            limit=16,
            flops=4 * chips * each * width * q_width,
            moved=4 * q_width * width,
        )

    partial = spread("experts", rows, [(pick, vmem), (wg, anywhere)])
    for_experts = exchange(partial)
    partial = spread("slots", new, [(partial[0], anywhere)])
    for_slots = exchange(partial)

    own, other = call(
        functools.partial(rows_kernel, chips),
        "rows",
        [in_vmem((rows // 2, width), BF16)] * 2,
        [(block, vmem) for block in turned(for_experts)]
        + [(picked, vmem), (ffn, vmem), (partial[0], anywhere)],
        limit=8,
        moved=2 * chips * rows * width,
    )
    own_out, other_out = call(
        expert_kernel,
        "expert",
        [in_vmem((rows // 2, width), F32), in_vmem((rows // 2, width), BF16)],
        [(own, vmem), (hop(other, 1), vmem), (wg, vmem), (wu, vmem), (wd, vmem)],
        limit=16,
        flops=6 * rows * width * w_gate.shape[1],
        moved=6 * width * w_gate.shape[1],
    )
    results = call(
        functools.partial(pack_kernel, per),
        "pack",
        [in_vmem((chips, 2 * per, width), BF16)],
        [(own_out, vmem), (hop(other_out, 1), vmem), (weight, vmem)],
        limit=8,
        moved=4 * rows * width,
    )
    returned = swap(results[0])
    hidden = call(
        functools.partial(hidden_kernel, chips),
        "hidden",
        [in_vmem((new, width), F32)],
        [(block, vmem) for block in turned(for_slots)] + [(residual_in, vmem)],
        limit=8,
        moved=2 * chips * new * width,
    )[0]
    return call(
        combine_kernel,
        "combine",
        [jax.ShapeDtypeStruct((new, width), BF16)],
        [(hidden, vmem), (combine, vmem), (returned, vmem)],
        limit=8,
        moved=6 * new * width,
    )[0]


def solution(mesh):
    in_specs = (
        P(("group", "tensor"), None),
        P(),
        P(None, "tensor"),
        P("tensor", None),
        P(),
        P(),
        P("tensor", None),
        P(),
        P("tensor", None, None),
        P("tensor", None, None),
        P("tensor", None, None),
        P(("group", "tensor"), None, None),
        P(("group", "tensor"), None, None),
        P(("group", "tensor")),
        P(("group", "tensor")),
        P(("group", "tensor"), None),
        P(("group", "tensor"), None),
        P(("group", "tensor")),
        P("group", None),
        P("group", None),
    )
    out_specs = P(("group", "tensor"), None)
    return jax.shard_map(body, mesh=mesh, in_specs=in_specs, out_specs=out_specs, check_vma=False)
```

```python
import functools
import math

import jax
import jax.numpy as jnp
import numpy as np
from jax import lax
from jax.experimental import pallas as pl
from jax.experimental.pallas import tpu as pltpu
from jax.sharding import PartitionSpec as P

EXPERTS = 128
SINK = 4
WIN = 512

EPSILON = 1e-06
NEG_FILL = -1e30
ROPE_BASE = 1000000.0
LOG2E = math.log2(math.e)
F32 = jnp.float32
BF16 = jnp.bfloat16
MIB = 1 << 20


def step(j):
    return 2 * j + bin(j).count("1") % 2


def iota(shape, dim):
    return lax.broadcasted_iota(jnp.int32, shape, dim)


def dot(left, right):
    return jnp.dot(left, right, preferred_element_type=F32)


def dot_last(left, right):
    return lax.dot_general(left, right, (((1,), (1,)), ((), ())), preferred_element_type=F32)


def dot_first(left, right):
    return lax.dot_general(left, right, (((0,), (0,)), ((), ())), preferred_element_type=F32)


def norm_rows(values):
    return values * lax.rsqrt(jnp.mean(values * values, axis=-1, keepdims=True) + EPSILON)


def in_vmem(shape, dtype):
    return pltpu.VMEM(shape, dtype)


def call(kernel, name, outs, args, scratch=(), limit=16, flops=0, moved=0, same=None):
    arrays = []
    specs = []
    for array, space in args:
        if space is pltpu.HBM or space is pltpu.VMEM:
            array = pltpu.with_memory_space_constraint(array, space)
        arrays.append(array)
        specs.append(pl.BlockSpec(memory_space=space))
    return pl.pallas_call(
        kernel,
        out_shape=outs,
        in_specs=specs,
        out_specs=[pl.BlockSpec(memory_space=pltpu.VMEM) for _ in outs],
        scratch_shapes=list(scratch),
        input_output_aliases=same or {},
        compiler_params=pltpu.CompilerParams(vmem_limit_bytes=limit * MIB),
        cost_estimate=pl.CostEstimate(flops=flops, bytes_accessed=moved, transcendentals=0),
        name=name,
    )(*arrays)


def hop(value, step):
    devices = lax.axis_size("tensor")
    return lax.ppermute(value, "tensor", [(i, i ^ step) for i in range(devices)])


def exchange(blocks):
    return [blocks[0]] + [hop(blocks[j], step(j)) for j in range(1, len(blocks))]


def window_rows(path_len):
    return -(-(WIN + 2 * (path_len - 1) + 16) // 16) * 16


def prep_kernel(path_len, n_weights, *refs):
    key_cache, value_cache, prefix_ref, accepted_ref, kind_ref = refs[:5]
    small_in = refs[5:10]
    sources = refs[10 : 10 + n_weights]
    refs = refs[10 + n_weights :]
    keys_ref, values_ref, mask_ref, rot_ref = refs[:4]
    targets = refs[4 : 4 + n_weights]
    refs = refs[4 + n_weights :]
    path_ref, parents_ref, freq_ref, q_gain_ref, k_gain_ref = refs[:5]
    small_sems, cache_sems, weight_sems = refs[5:]

    new = mask_ref.shape[0]
    kv_heads, span, head = keys_ref.shape
    cache_len = key_cache.shape[1]
    wide = window_rows(path_len)
    sink_at, win_at = new, new + 16
    end = win_at + wide

    small = [
        pltpu.make_async_copy(source, target, small_sems.at[which])
        for which, (source, target) in enumerate(zip(small_in, refs[:5]))
    ]
    for copy in small:
        copy.start()
    copies = [
        pltpu.make_async_copy(source, target, weight_sems.at[which])
        for which, (source, target) in enumerate(zip(sources, targets))
    ]
    prefix = prefix_ref[0]
    accepted = accepted_ref[0]
    total = prefix + accepted
    low = jnp.maximum(total - WIN, 0)
    start = pl.multiple_of(jnp.minimum((low // 16) * 16, cache_len - wide), 16)
    for which, (cache, buf) in enumerate(((key_cache, keys_ref), (value_cache, values_ref))):
        for kv in range(kv_heads):
            cols = pl.ds(kv * head, head)
            copies.append(
                pltpu.make_async_copy(
                    cache.at[0, pl.ds(start, wide), cols],
                    buf.at[kv, pl.ds(win_at, wide)],
                    cache_sems.at[which, kv, 0],
                )
            )
            copies.append(
                pltpu.make_async_copy(
                    cache.at[0, pl.ds(0, 16), cols],
                    buf.at[kv, pl.ds(sink_at, 16)],
                    cache_sems.at[which, kv, 1],
                )
            )
    for copy in copies:
        copy.start()

    for buf in (keys_ref, values_ref):
        buf[:, 0:new, :] = jnp.zeros((kv_heads, new, head), BF16)
        buf[:, end:span, :] = jnp.zeros((kv_heads, span - end, head), BF16)

    for copy in small:
        copy.wait()
    column = iota((1, span), 1)
    row = jnp.where(column < win_at, column - sink_at, start + column - win_at)
    taken = jnp.zeros((1, span), jnp.bool_)
    for step in range(path_len):
        at = prefix + path_ref[0, step]
        taken = taken | ((row == at) & (step < accepted))
    old = (row < prefix) & ((row < SINK) | (row >= total - WIN))
    in_window = (column >= win_at) & (column < end) & (old | taken)
    in_sink = (column >= sink_at) & (column < win_at) & (row < SINK) & (row < prefix) & (start > 0)
    seen = jnp.where(in_window | in_sink, 0.0, NEG_FILL)
    mask_ref[...] = jnp.broadcast_to(seen, mask_ref.shape)

    down, across = iota((new, new), 0), iota((new, new), 1)
    eye = (down == across).astype(F32)
    back = eye + (down == parents_ref[...]).astype(F32)
    for _ in range((new - 1).bit_length()):
        half = back.astype(BF16)
        back = jnp.minimum(dot(half, half), 1.0)
    reach = dot_first(back.astype(BF16), eye.astype(BF16))
    tree = (kind_ref[0] == 1).astype(F32)
    causal = (across <= down).astype(F32)
    allowed = tree * reach + (1.0 - tree) * causal
    mask_ref[:, 0:new] = jnp.where(allowed > 0.5, 0.0, NEG_FILL)
    depth = tree * (jnp.sum(reach, axis=1, keepdims=True) - 1.0)
    depth = depth + (1.0 - tree) * iota((new, 1), 0).astype(F32)
    angle = (total.astype(F32) + depth) * freq_ref[...]
    lane = iota(angle.shape, 1)
    cosine, sine = jnp.cos(angle), jnp.sin(angle)
    sine = jnp.where(lane < head // 2, -sine, sine)
    for which, gain_ref in enumerate((q_gain_ref, k_gain_ref)):
        gain = jnp.broadcast_to(gain_ref[...], angle.shape)
        rot_ref[2 * which] = cosine * gain
        rot_ref[2 * which + 1] = sine * pltpu.roll(gain, head // 2, 1)
    for copy in copies:
        copy.wait()


def route_kernel(per, new, n_weights, *refs):
    small_in = refs[1:3]
    sources = refs[3 : 3 + n_weights]
    refs = refs[3 + n_weights :]
    pick_ref, combine_ref, weight_ref = refs[:3]
    targets = refs[3 : 3 + n_weights]
    ids_ref, gates_ref, hit_ref, rank_ref, own_ref, sems = refs[3 + n_weights :]
    sources, targets = (*small_in, *sources), (ids_ref, gates_ref, *targets)
    copies = [
        pltpu.make_async_copy(source, target, sems.at[which])
        for which, (source, target) in enumerate(zip(sources, targets))
    ]
    for copy in copies:
        copy.start()
    for copy in copies[:2]:
        copy.wait()

    me = lax.axis_index("tensor")
    all_tokens = ids_ref.shape[1]
    devices = hit_ref.shape[0]
    chips = devices // 2
    tokens = chips * new
    slot = iota((all_tokens, tokens), 1) // new
    odd = slot
    for shift in (4, 2, 1):
        odd = odd ^ (odd >> shift)
    source = (me ^ (2 * slot + (odd & 1))) * new + iota((all_tokens, tokens), 1) % new
    order = (iota((all_tokens, tokens), 0) == source).astype(F32)
    ids = dot(ids_ref[...].astype(F32).astype(BF16), order.astype(BF16))
    gates = lax.dot_general(
        gates_ref[...],
        order,
        (((1,), (0,)), ((), ())),
        precision=lax.Precision.HIGHEST,
        preferred_element_type=F32,
    )
    for rel in range(devices):
        expert = (me ^ step(rel // 2) ^ (rel % 2)).astype(F32)
        named = (ids == expert).astype(F32)
        hit_ref[rel : rel + 1, :] = jnp.max(named, axis=0, keepdims=True)
    before, later = iota((tokens, tokens), 0), iota((tokens, tokens), 1)
    earlier = (before < later) & (before // new == later // new)
    rank_ref[...] = dot(hit_ref[...].astype(BF16), earlier.astype(F32).astype(BF16))
    rows = chips * per
    slot_of = iota((rows, tokens), 1) // new
    row_slot = iota((rows, tokens), 0) // per
    row_rank = (iota((rows, tokens), 0) % per).astype(F32)
    in_first = iota((1, tokens), 1) < new
    for rel in range(devices):
        hit = hit_ref[rel : rel + 1, :] > 0.5
        rank = rank_ref[rel : rel + 1, :]
        chosen = (slot_of == (row_slot ^ (rel // 2))) & hit & (rank == row_rank)
        pick_ref[rel * rows : (rel + 1) * rows, :] = chosen.astype(F32)
        if rel < 2:
            named = ids == (me ^ rel).astype(F32)
            weight = jnp.sum(jnp.where(named, gates, 0.0), axis=0, keepdims=True)
            weight = jnp.sum(jnp.where(chosen, weight, 0.0), axis=1, keepdims=True)
            weight_ref[rel * rows : (rel + 1) * rows, :] = jnp.broadcast_to(
                weight, (rows, weight_ref.shape[1])
            )
        for place in range(per):
            at = rel * per + place
            own_ref[at : at + 1, :] = (in_first & hit & (rank == float(place))).astype(F32)
    first = (iota((tokens, new), 0) == iota((tokens, new), 1)).astype(F32)
    combine_ref[...] = lax.dot_general(
        first.astype(BF16),
        own_ref[...].astype(BF16),
        (((0,), (1,)), ((), ())),
        preferred_element_type=F32,
    )
    for copy in copies[2:]:
        copy.wait()


def project_kernel(count, *refs):
    blocks = refs[:count]
    gain_ref, wq_ref, wkv_ref, wq_sib, wkv_sib = refs[count : count + 5]
    outs = refs[count + 5 :]
    rows = blocks[0].shape[0]
    gain = gain_ref[...]
    values = [(norm_rows(block[...].astype(F32)) * gain).astype(BF16) for block in blocks]
    values = jnp.concatenate(values, axis=0)

    def put(result, at):
        result = result.astype(BF16)
        for j in range(count):
            outs[j][:, at : at + result.shape[1]] = result[j * rows : (j + 1) * rows]

    wide, narrow = wq_ref.shape[1], wkv_ref.shape[0]
    put(dot(values, wq_ref[...]), 0)
    put(dot(values, wq_sib[...]), wide)
    put(dot_last(values, wkv_ref[...]), 2 * wide)
    put(dot_last(values, wkv_sib[...]), 2 * wide + narrow)


def rope(values, rot_ref, which):
    values = norm_rows(values.astype(F32))
    turn = pltpu.roll(values, values.shape[1] // 2, 1)
    return (values * rot_ref[2 * which] + turn * rot_ref[2 * which + 1]).astype(BF16)


def heads_of(block_ref, rot_ref, count):
    head = rot_ref.shape[2]
    parts = [rope(block_ref[:, h * head : (h + 1) * head], rot_ref, 0) for h in range(count)]
    return jnp.concatenate(parts, axis=0)


def attend_part(query, keys, values, mask, floor=None):
    new, span = mask.shape
    lines, head = query.shape
    score = dot_last(query, keys) * (head ** (-0.5) * LOG2E)
    score = (score.reshape(lines // new, new, span) + mask[None]).reshape(lines, span)
    top = jnp.broadcast_to(jnp.max(score, axis=-1, keepdims=True), (lines, head))
    if floor is not None:
        top = jnp.maximum(top, floor)
    expo = jnp.exp2(score - (top if span == head else top[:, 0:1])).astype(BF16)
    return dot(expo, values), dot(expo, jnp.ones((span, head), BF16)), top


def cache_kernel(chips, q_width, *refs):
    got = refs[: chips - 1]
    keys_ref, values_ref, mask_ref, rot_ref = refs[chips - 1 : chips + 3]
    outs = refs[chips + 3 :]
    chip = lax.axis_index("tensor") // 2
    kv_heads, _, head = keys_ref.shape
    per_chip = 2 * q_width // head
    mask = mask_ref[...]
    mask = jnp.where(iota(mask.shape, 1) < mask.shape[0], NEG_FILL, mask)
    for j in range(chips - 1):
        kv = (chip ^ j) * per_chip // (chips * per_chip // kv_heads)
        query = heads_of(got[j], rot_ref, per_chip)
        outs[2 * j][...] = query
        parts = attend_part(query, keys_ref[kv], values_ref[kv], mask)
        for at, part in enumerate(parts):
            outs[2 * j + 1][at] = part


def attend_kernel(chips, q_width, kv_ready, *refs):
    got = refs[:chips]
    cached = refs[chips : 3 * chips - 2]
    refs = refs[3 * chips - 2 :]
    fresh_ref = refs[0] if kv_ready else refs[-1]
    keys_ref, values_ref, mask_ref, rot_ref = refs[kv_ready : kv_ready + 4]
    outs = refs[kv_ready + 5 : kv_ready + 5 + chips]
    me = lax.axis_index("tensor")
    chip = me // 2
    kv_heads, span, head = keys_ref.shape
    new = mask_ref.shape[0]
    per_chip = 2 * q_width // head
    if not kv_ready:
        for rel in range(2 * chips):
            left = 2 * q_width + (rel % 2) * head
            fresh_ref[step(rel // 2) ^ (rel % 2)] = got[rel // 2][:, left : left + head]

    allow = mask_ref[:, 0:head]
    allow = jnp.where(iota(allow.shape, 1) < new, allow, NEG_FILL)
    empty = jnp.zeros((head - new, head), BF16)
    for j in reversed(range(chips)):
        kv = (chip ^ j) * per_chip // (chips * per_chip // kv_heads)
        key_at, value_at = kv, kv + kv_heads
        if not kv_ready:
            key_at, value_at = me ^ key_at, me ^ value_at
        key, value = rope(fresh_ref[key_at], rot_ref, 1), fresh_ref[value_at]
        if j == chips - 1:
            keys = jnp.concatenate([key, keys_ref[kv, new:span]], axis=0)
            values = jnp.concatenate([value, values_ref[kv, new:span]], axis=0)
            query = heads_of(got[j], rot_ref, per_chip)
            result, total, _ = attend_part(query, keys, values, mask_ref[...])
        else:
            query, before = cached[2 * j][...], cached[2 * j + 1]
            keys = jnp.concatenate([key, empty], axis=0)
            values = jnp.concatenate([value, empty], axis=0)
            result, total, top = attend_part(query, keys, values, allow, before[2])
            shrink = jnp.exp2(before[2] - top)
            result = result + before[0] * shrink
            total = total + before[1] * shrink
        result = (result / total).astype(BF16)
        for h in range(per_chip):
            outs[j][:, h * head : (h + 1) * head] = result[h * new : (h + 1) * new]


def spread_kernel(chips, picks, *refs):
    got = refs[:chips]
    w_ref, w_sib = refs[chips : chips + 2]
    outs = refs[-chips:]
    depth, width = w_ref.shape
    left = jnp.concatenate([got[j][...] for j in range(chips)], axis=0)
    if picks:
        left = dot(refs[chips + 2][...].astype(BF16), left).astype(BF16)
    each = left.shape[0] // chips
    tile = min(512, width)
    for at in range(0, width, tile):
        part = dot(left[:, :depth], w_ref[:, at : at + tile])
        part = (part + dot(left[:, depth:], w_sib[:, at : at + tile])).astype(BF16)
        for j in range(chips):
            outs[j][:, at : at + tile] = part[j * each : (j + 1) * each]


def select_kernel(chips, *refs):
    blocks = refs[:chips]
    pick_ref, _ = refs[chips : chips + 2]
    sources = refs[chips + 2 : chips + 4]
    picked_ref = refs[chips + 4]
    targets = refs[chips + 5 : chips + 7]
    sems = refs[-1]
    copies = [
        pltpu.make_async_copy(source, target, sems.at[which])
        for which, (source, target) in enumerate(zip(sources, targets))
    ]
    for copy in copies:
        copy.start()
    values = jnp.concatenate([block[...] for block in blocks], axis=0)
    pick = pick_ref[0 : picked_ref.shape[0], :].astype(BF16)
    picked_ref[...] = dot(pick, values)
    for copy in copies:
        copy.wait()


def hidden_kernel(chips, *refs):
    got = refs[:chips]
    own_ref, out_ref = refs[chips:]
    total = own_ref[...].astype(F32)
    for j in range(chips):
        total = total + got[j][...].astype(F32)
    out_ref[...] = total


def rows_kernel(chips, *refs):
    got = refs[:chips]
    picked_ref, gain_ref, _, own_ref, other_ref = refs[chips:]
    hidden = picked_ref[...]
    for j in range(chips):
        hidden = hidden + got[j][...].astype(F32)
    normed = (norm_rows(hidden) * gain_ref[...]).astype(BF16)
    half = own_ref.shape[0]
    own_ref[...] = normed[:half]
    other_ref[...] = normed[half:]


def expert_kernel(own_ref, other_ref, gate_ref, up_ref, down_ref, own_out, other_out):
    left = jnp.concatenate([own_ref[...].astype(F32), other_ref[...].astype(F32)], axis=0)
    left = left.astype(BF16)
    gate = dot_last(left, gate_ref[0])
    up = dot_last(left, up_ref[0])
    inner = (gate / (1.0 + jnp.exp(-gate)) * up).astype(BF16)
    result = dot(inner, down_ref[0])
    half = own_ref.shape[0]
    own_out[...] = result[:half]
    other_out[...] = result[half:].astype(BF16)


def pack_kernel(chips, per, own_ref, other_ref, weight_ref, *outs):
    half = own_ref.shape[0]
    own = own_ref[...] * weight_ref[:half, 0:1]
    other = other_ref[...].astype(F32) * weight_ref[half:, 0:1]
    for j in range(chips):
        at = slice(j * per, (j + 1) * per)
        outs[j][...] = jnp.concatenate([own[at], other[at]], axis=0).astype(BF16)


def combine_kernel(chips, *refs):
    hidden_ref, combine_ref = refs[:2]
    got = refs[2 : 2 + chips]
    out_ref = refs[2 + chips]
    rows = jnp.concatenate([block[...].astype(F32) for block in got], axis=0)
    moe = dot(combine_ref[...].astype(BF16), rows.astype(BF16))
    out_ref[...] = (hidden_ref[...] + moe).astype(BF16)


def body(
    residual_in,
    attn_gain,
    w_query,
    w_keyval,
    query_gain,
    key_gain,
    w_out,
    ffn_gain,
    w_gate,
    w_up,
    w_down,
    key_cache,
    value_cache,
    prefix_lens,
    accepted,
    accept_path,
    parents,
    slot_kinds,
    expert_ids,
    gate_probs,
):
    devices = lax.axis_size("tensor")
    chips = devices // 2
    new, width = residual_in.shape
    head = query_gain.shape[0]
    kv_heads = key_cache.shape[2] // head
    q_width = w_query.shape[1]
    new_width = w_keyval.shape[0]
    all_tokens, top = expert_ids.shape
    tokens = chips * new
    per = new * top // EXPERTS
    path_len = accept_path.shape[1]
    rows = 2 * chips * per
    assert key_cache.shape[0] == 1 and w_gate.shape[0] == 1
    assert devices & (devices - 1) == 0
    vmem, smem, hbm, anywhere = pltpu.VMEM, pltpu.SMEM, pltpu.HBM, pl.ANY

    blocks = exchange([residual_in] * chips)
    wq_sib = hop(w_query, 1)
    wkv_sib = hop(w_keyval, 1)

    freq = ROPE_BASE ** (-2.0 * np.arange(head // 2) / head)
    freq = jnp.asarray(np.concatenate([freq, freq])[None, :], F32)
    span = -(-(new + 16 + window_rows(path_len)) // 128) * 128
    weights = [attn_gain[None, :], w_query, w_keyval]
    keys, values, mask, rot, gain, wq, wkv = call(
        functools.partial(prep_kernel, path_len, len(weights)),
        "prep",
        [
            in_vmem((kv_heads, span, head), BF16),
            in_vmem((kv_heads, span, head), BF16),
            in_vmem((new, span), F32),
            in_vmem((4, new, head), F32),
        ]
        + [in_vmem(w.shape, w.dtype) for w in weights],
        [
            (key_cache, hbm),
            (value_cache, hbm),
            (prefix_lens, smem),
            (accepted, smem),
            (slot_kinds, smem),
            (accept_path, hbm),
            (parents, hbm),
            (freq, hbm),
            (query_gain[None, :], hbm),
            (key_gain[None, :], hbm),
        ]
        + [(w, hbm) for w in weights],
        [
            pltpu.SMEM((1, path_len), jnp.int32),
            pltpu.VMEM((1, new), jnp.int32),
            pltpu.VMEM((1, head), F32),
            pltpu.VMEM((1, head), F32),
            pltpu.VMEM((1, head), F32),
            pltpu.SemaphoreType.DMA((5,)),
            pltpu.SemaphoreType.DMA((2, kv_heads, 2)),
            pltpu.SemaphoreType.DMA((len(weights),)),
        ],
        limit=16,
        moved=4 * span * kv_heads * head * 2,
    )

    projected = call(
        functools.partial(project_kernel, chips),
        "project",
        [in_vmem((new, 2 * (q_width + new_width)), BF16)] * chips,
        [(block, vmem) for block in blocks]
        + [(w, vmem) for w in (gain, wq, wkv, wq_sib, wkv_sib)],
        limit=16,
        flops=4 * tokens * width * (q_width + new_width),
        moved=4 * width * (q_width + new_width),
    )
    got = exchange(projected)

    weights = [ffn_gain[None, :], w_out, w_down]
    pick, combine, weight, ffn, wo, wd = call(
        functools.partial(route_kernel, per, new, len(weights)),
        "route",
        [
            in_vmem((chips * rows, tokens), F32),
            in_vmem((new, devices * per), F32),
            in_vmem((rows, 128), F32),
        ]
        + [in_vmem(w.shape, w.dtype) for w in weights],
        [(projected[0], anywhere), (expert_ids.T, hbm), (gate_probs.T, hbm)]
        + [(w, hbm) for w in weights],
        [
            pltpu.VMEM((top, all_tokens), jnp.int32),
            pltpu.VMEM((top, all_tokens), F32),
            pltpu.VMEM((devices, tokens), F32),
            pltpu.VMEM((devices, tokens), F32),
            pltpu.VMEM((devices * per, tokens), F32),
            pltpu.SemaphoreType.DMA((2 + len(weights),)),
        ],
        limit=16,
        moved=4 * width * (q_width + w_down.shape[1]),
    )
    kv_ready = []
    if new_width != head:
        pieces = [None] * devices
        for rel in range(devices):
            left = 2 * q_width + (rel % 2) * new_width
            pieces[step(rel // 2) ^ (rel % 2)] = got[rel // 2][:, left : left + new_width]
        pieces = jnp.stack(pieces)[lax.axis_index("tensor") ^ jnp.arange(devices)]
        pieces = pieces.transpose(1, 0, 2).reshape(new, 2 * kv_heads, head)
        kv_ready = [(pieces.transpose(1, 0, 2), vmem)]
    lines = 2 * q_width // head * new
    cached = call(
        functools.partial(cache_kernel, chips, q_width),
        "cache",
        [in_vmem((lines, head), BF16), in_vmem((3, lines, head), F32)] * (chips - 1),
        [(block, vmem) for block in got[:-1]]
        + [(keys, vmem), (values, vmem), (mask, vmem), (rot, vmem)],
        limit=16,
        flops=8 * new * (chips - 1) * q_width * span,
        moved=4 * span * kv_heads * head,
    )
    *attended, wo = call(
        functools.partial(attend_kernel, chips, q_width, len(kv_ready)),
        "attend",
        [in_vmem((new, 2 * q_width), BF16)] * chips + [in_vmem(wo.shape, wo.dtype)],
        [(block, vmem) for block in got]
        + [(array, vmem) for array in cached]
        + kv_ready
        + [(keys, vmem), (values, vmem), (mask, vmem), (rot, vmem), (wo, vmem)],
        [] if kv_ready else [pltpu.VMEM((devices, new, head), BF16)],
        limit=16,
        same={chips + len(cached) + len(kv_ready) + 4: chips},
        flops=8 * new * q_width * span,
        moved=4 * span * kv_heads * head,
    )
    wo_sib = hop(wo, 1)
    heads = exchange(attended)
    picked, wg, wu = call(
        functools.partial(select_kernel, chips),
        "select",
        [in_vmem((rows, width), F32)] + [in_vmem(w.shape, w.dtype) for w in (w_gate, w_up)],
        [(block, vmem) for block in blocks]
        + [(pick, vmem), (attended[0], anywhere), (w_gate, hbm), (w_up, hbm)],
        [pltpu.SemaphoreType.DMA((2,))],
        limit=8,
        flops=2 * rows * width * tokens,
        moved=8 * width * w_gate.shape[1],
    )

    def spread(name, each, more):
        return call(
            functools.partial(spread_kernel, chips, name == "experts"),
            name,
            [in_vmem((each, width), BF16)] * chips,
            [(block, vmem) for block in heads] + [(wo, vmem), (wo_sib, vmem)] + more,
            limit=16,
            flops=4 * chips * each * width * q_width,
            moved=4 * q_width * width,
        )

    partial = spread("experts", rows, [(pick, vmem), (wg, anywhere)])
    for_experts = exchange(partial)
    partial = spread("slots", new, [(partial[0], anywhere)])
    for_slots = exchange(partial)

    own, other = call(
        functools.partial(rows_kernel, chips),
        "rows",
        [in_vmem((rows // 2, width), BF16)] * 2,
        [(block, vmem) for block in for_experts]
        + [(picked, vmem), (ffn, vmem), (partial[0], anywhere)],
        limit=8,
        moved=2 * chips * rows * width,
    )
    own_out, other_out = call(
        expert_kernel,
        "expert",
        [in_vmem((rows // 2, width), F32), in_vmem((rows // 2, width), BF16)],
        [(own, vmem), (hop(other, 1), vmem), (wg, vmem), (wu, vmem), (wd, vmem)],
        limit=16,
        flops=6 * rows * width * w_gate.shape[1],
        moved=6 * width * w_gate.shape[1],
    )
    results = call(
        functools.partial(pack_kernel, chips, per),
        "pack",
        [in_vmem((2 * per, width), BF16)] * chips,
        [(own_out, vmem), (hop(other_out, 1), vmem), (weight, vmem)],
        limit=8,
        moved=4 * rows * width,
    )
    returned = exchange(results)
    hidden = call(
        functools.partial(hidden_kernel, chips),
        "hidden",
        [in_vmem((new, width), F32)],
        [(block, vmem) for block in for_slots] + [(residual_in, vmem)],
        limit=8,
        moved=2 * chips * new * width,
    )[0]
    return call(
        functools.partial(combine_kernel, chips),
        "combine",
        [jax.ShapeDtypeStruct((new, width), BF16)],
        [(hidden, vmem), (combine, vmem)] + [(block, vmem) for block in returned],
        limit=8,
        moved=6 * new * width,
    )[0]


def solution(mesh):
    in_specs = (
        P(("group", "tensor"), None),
        P(),
        P(None, "tensor"),
        P("tensor", None),
        P(),
        P(),
        P("tensor", None),
        P(),
        P("tensor", None, None),
        P("tensor", None, None),
        P("tensor", None, None),
        P(("group", "tensor"), None, None),
        P(("group", "tensor"), None, None),
        P(("group", "tensor")),
        P(("group", "tensor")),
        P(("group", "tensor"), None),
        P(("group", "tensor"), None),
        P(("group", "tensor")),
        P("group", None),
        P("group", None),
    )
    out_specs = P(("group", "tensor"), None)
    return jax.shard_map(body, mesh=mesh, in_specs=in_specs, out_specs=out_specs, check_vma=False)
```

```python
import functools
import math

import jax
import jax.numpy as jnp
import numpy as np
from jax import lax
from jax.experimental import pallas as pl
from jax.experimental.pallas import tpu as pltpu
from jax.sharding import PartitionSpec as P

EXPERTS = 128
SINK = 4
WIN = 512

EPSILON = 1e-06
NEG_FILL = -1e30
ROPE_BASE = 1000000.0
LOG2E = math.log2(math.e)
F32 = jnp.float32
BF16 = jnp.bfloat16
MIB = 1 << 20


def step(j):
    return 2 * j + bin(j).count("1") % 2


def iota(shape, dim):
    return lax.broadcasted_iota(jnp.int32, shape, dim)


def dot(left, right):
    return jnp.dot(left, right, preferred_element_type=F32)


def dot_last(left, right):
    return lax.dot_general(left, right, (((1,), (1,)), ((), ())), preferred_element_type=F32)


def dot_first(left, right):
    return lax.dot_general(left, right, (((0,), (0,)), ((), ())), preferred_element_type=F32)


def norm_rows(values):
    return values * lax.rsqrt(jnp.mean(values * values, axis=-1, keepdims=True) + EPSILON)


def in_vmem(shape, dtype):
    return pltpu.VMEM(shape, dtype)


def call(kernel, name, outs, args, scratch=(), limit=16, flops=0, moved=0, same=None):
    arrays = []
    specs = []
    for array, space in args:
        if space is pltpu.HBM or space is pltpu.VMEM:
            array = pltpu.with_memory_space_constraint(array, space)
        arrays.append(array)
        specs.append(pl.BlockSpec(memory_space=space))
    return pl.pallas_call(
        kernel,
        out_shape=outs,
        in_specs=specs,
        out_specs=[pl.BlockSpec(memory_space=pltpu.VMEM) for _ in outs],
        scratch_shapes=list(scratch),
        input_output_aliases=same or {},
        compiler_params=pltpu.CompilerParams(vmem_limit_bytes=limit * MIB),
        cost_estimate=pl.CostEstimate(flops=flops, bytes_accessed=moved, transcendentals=0),
        name=name,
    )(*arrays)


def hop(value, step):
    devices = lax.axis_size("tensor")
    return lax.ppermute(value, "tensor", [(i, i ^ step) for i in range(devices)])


def exchange(blocks):
    return [blocks[0]] + [hop(blocks[j], step(j)) for j in range(1, len(blocks))]


def window_rows(path_len):
    return -(-(WIN + 2 * (path_len - 1) + 16) // 16) * 16


def prep_kernel(path_len, per_chip, n_weights, *refs):
    key_cache, value_cache, prefix_ref, accepted_ref, kind_ref = refs[:5]
    small_in = refs[5:7]
    sources = refs[7 : 7 + n_weights]
    refs = refs[7 + n_weights :]
    chips = len(refs) - 5 - n_weights
    outs = refs[:chips]
    targets = refs[chips : chips + n_weights]
    path_ref, parents_ref, small_sems, cache_sems, weight_sems = refs[chips + n_weights :]

    new = parents_ref.shape[1]
    cache_len, kv_width = key_cache.shape[1:]
    head = outs[0].shape[1]
    group = chips * per_chip // (kv_width // head)
    wide = window_rows(path_len)
    kept = wide + 16
    chip = lax.axis_index("tensor") // 2

    small = [
        pltpu.make_async_copy(source, target, small_sems.at[which])
        for which, (source, target) in enumerate(zip(small_in, (path_ref, parents_ref)))
    ]
    for copy in small:
        copy.start()
    prefix = prefix_ref[0]
    accepted = accepted_ref[0]
    total = prefix + accepted
    low = jnp.maximum(total - WIN, 0)
    start = pl.multiple_of(jnp.minimum((low // 16) * 16, cache_len - wide), 16)
    copies = []
    for j in range(chips):
        at = pl.multiple_of((chip ^ j) * per_chip // group * head, head)
        for which, cache in enumerate((key_cache, value_cache)):
            base = which * kept
            copies.append(
                pltpu.make_async_copy(
                    cache.at[0, pl.ds(start, wide), pl.ds(at, head)],
                    outs[j].at[pl.ds(base, wide)],
                    cache_sems.at[which, j, 0],
                )
            )
            copies.append(
                pltpu.make_async_copy(
                    cache.at[0, pl.ds(0, 16), pl.ds(at, head)],
                    outs[j].at[pl.ds(base + wide, 16)],
                    cache_sems.at[which, j, 1],
                )
            )
    for which, (source, target) in enumerate(zip(sources, targets)):
        copies.append(pltpu.make_async_copy(source, target, weight_sems.at[which]))
    for copy in copies:
        copy.start()

    for copy in small:
        copy.wait()
    span = -(-(new + kept) // head) * head
    column = iota((1, span), 1)
    sink_at = new + wide
    row = jnp.where(column < sink_at, start + column - new, column - sink_at)
    taken = jnp.zeros((1, span), jnp.bool_)
    for place in range(path_len):
        at = prefix + path_ref[0, place]
        taken = taken | ((row == at) & (place < accepted))
    old = (row < prefix) & ((row < SINK) | (row >= total - WIN))
    in_window = (column >= new) & (column < sink_at) & (old | taken)
    in_sink = (column >= sink_at) & (column < sink_at + 16)
    in_sink = in_sink & (row < SINK) & (row < prefix) & (start > 0)
    seen = jnp.where(in_window | in_sink, 1.0, 0.0)

    down, across = iota((new, new), 0), iota((new, new), 1)
    eye = (down == across).astype(F32)
    back = eye + (down == parents_ref[...]).astype(F32)
    for _ in range((new - 1).bit_length()):
        half = back.astype(BF16)
        back = jnp.minimum(dot(half, half), 1.0)
    reach = dot_first(back.astype(BF16), eye.astype(BF16))
    tree = (kind_ref[0] == 1).astype(F32)
    causal = (across <= down).astype(F32)
    allowed = tree * reach + (1.0 - tree) * causal
    depth = tree * (jnp.sum(reach, axis=1, keepdims=True) - 1.0)
    depth = depth + (1.0 - tree) * iota((new, 1), 0).astype(F32)
    position = total.astype(F32) + depth
    high = jnp.floor(position * (1.0 / 128.0))
    lane = iota((new, head), 1)
    spread = (iota((new, head), 0) == lane).astype(F32)
    facts = dot(allowed.astype(BF16), spread.astype(BF16))
    facts = facts + jnp.where(lane == new, high, 0.0)
    facts = facts + jnp.where(lane == new + 1, position - 128.0 * high, 0.0)
    lines = [facts] + [seen[:, at : at + head] for at in range(0, span, head)]
    lines.append(jnp.zeros((16 - span // head, head), F32))
    facts = jnp.concatenate(lines, axis=0).astype(BF16)
    for j in range(chips):
        outs[j][2 * kept : 2 * kept + new + 16, :] = facts
    for copy in copies:
        copy.wait()


def route_kernel(per, new, n_weights, *refs):
    small_in = refs[1:3]
    sources = refs[3 : 3 + n_weights]
    refs = refs[3 + n_weights :]
    pick_ref, combine_ref, weight_ref = refs[:3]
    targets = refs[3 : 3 + n_weights]
    ids_ref, gates_ref, hit_ref, rank_ref, own_ref, sems = refs[3 + n_weights :]
    sources, targets = (*small_in, *sources), (ids_ref, gates_ref, *targets)
    copies = [
        pltpu.make_async_copy(source, target, sems.at[which])
        for which, (source, target) in enumerate(zip(sources, targets))
    ]
    for copy in copies:
        copy.start()
    for copy in copies[:2]:
        copy.wait()

    me = lax.axis_index("tensor")
    all_tokens = ids_ref.shape[1]
    devices = hit_ref.shape[0]
    chips = devices // 2
    tokens = chips * new
    slot = iota((all_tokens, tokens), 1) // new
    odd = slot
    for shift in (4, 2, 1):
        odd = odd ^ (odd >> shift)
    source = (me ^ (2 * slot + (odd & 1))) * new + iota((all_tokens, tokens), 1) % new
    order = (iota((all_tokens, tokens), 0) == source).astype(F32)
    ids = dot(ids_ref[...].astype(F32).astype(BF16), order.astype(BF16))
    gates = lax.dot_general(
        gates_ref[...],
        order,
        (((1,), (0,)), ((), ())),
        precision=lax.Precision.HIGHEST,
        preferred_element_type=F32,
    )
    for rel in range(devices):
        expert = (me ^ step(rel // 2) ^ (rel % 2)).astype(F32)
        named = (ids == expert).astype(F32)
        hit_ref[rel : rel + 1, :] = jnp.max(named, axis=0, keepdims=True)
    before, later = iota((tokens, tokens), 0), iota((tokens, tokens), 1)
    earlier = (before < later) & (before // new == later // new)
    rank_ref[...] = dot(hit_ref[...].astype(BF16), earlier.astype(F32).astype(BF16))
    rows = chips * per
    slot_of = iota((rows, tokens), 1) // new
    row_slot = iota((rows, tokens), 0) // per
    row_rank = (iota((rows, tokens), 0) % per).astype(F32)
    in_first = iota((1, tokens), 1) < new
    for rel in range(devices):
        hit = hit_ref[rel : rel + 1, :] > 0.5
        rank = rank_ref[rel : rel + 1, :]
        chosen = (slot_of == (row_slot ^ (rel // 2))) & hit & (rank == row_rank)
        pick_ref[rel * rows : (rel + 1) * rows, :] = chosen.astype(F32)
        if rel < 2:
            named = ids == (me ^ rel).astype(F32)
            weight = jnp.sum(jnp.where(named, gates, 0.0), axis=0, keepdims=True)
            weight = jnp.sum(jnp.where(chosen, weight, 0.0), axis=1, keepdims=True)
            weight_ref[rel * rows : (rel + 1) * rows, :] = jnp.broadcast_to(
                weight, (rows, weight_ref.shape[1])
            )
        for place in range(per):
            at = rel * per + place
            own_ref[at : at + 1, :] = (in_first & hit & (rank == float(place))).astype(F32)
    first = (iota((tokens, new), 0) == iota((tokens, new), 1)).astype(F32)
    combine_ref[...] = lax.dot_general(
        first.astype(BF16),
        own_ref[...].astype(BF16),
        (((0,), (1,)), ((), ())),
        preferred_element_type=F32,
    )
    for copy in copies[2:]:
        copy.wait()


def project_kernel(chips, pairs, *refs):
    blocks = refs[:chips]
    gain_ref, wq_ref, wkv_ref, wq_sib, wkv_sib = refs[chips : chips + 5]
    outs = refs[chips + 5 : 2 * chips + 5]
    sent = refs[2 * chips + 5 :]
    me = lax.axis_index("tensor")
    chip = me // 2
    rows = blocks[0].shape[0]
    gain = gain_ref[...]
    values = [(norm_rows(block[...].astype(F32)) * gain).astype(BF16) for block in blocks]
    values = jnp.concatenate(values, axis=0)
    wide = wq_ref.shape[1]
    for which, w_ref in enumerate((wq_ref, wq_sib)):
        result = dot(values, w_ref[...]).astype(BF16)
        for j in range(chips):
            outs[j][:, which * wide : (which + 1) * wide] = result[j * rows : (j + 1) * rows]
    first, second = dot_last(values, wkv_ref[...]), dot_last(values, wkv_sib[...])
    turn = me % 2 == 1
    if pairs:
        turn = turn ^ ((chip == 0) | (chip == chips - 1))
    lower, upper = jnp.where(turn, second, first), jnp.where(turn, first, second)
    narrow = lower.shape[1]
    for which, part in enumerate((lower.astype(BF16), upper.astype(BF16))):
        for j in range(chips):
            block = part[j * rows : (j + 1) * rows]
            if pairs:
                sent[which][chip ^ j] = block
            else:
                sent[0][chip ^ j, :, which * narrow : (which + 1) * narrow] = block


def hold_kernel(*_):
    pass


def fresh_kernel(one_ref, two_ref, key_ref, value_ref):
    chip = lax.axis_index("tensor") // 2
    turn = (chip == 0) | (chip == one_ref.shape[0] - 1)
    one, two = one_ref[...].astype(F32), two_ref[...].astype(F32)
    key_ref[...] = jnp.where(turn, two, one).astype(BF16)
    value_ref[...] = jnp.where(turn, one, two).astype(BF16)


def attend_kernel(chips, *refs):
    queries = refs[:chips]
    caches = refs[chips : 2 * chips]
    key_ref, value_ref, freq_ref, q_gain_ref, k_gain_ref = refs[2 * chips : 2 * chips + 5]
    outs = refs[-chips:]
    chip = lax.axis_index("tensor") // 2
    new, wide = queries[0].shape
    head = key_ref.shape[2]
    per_chip = wide // head
    kept = (caches[0].shape[0] - new - 16) // 2
    span = -(-(new + kept) // head) * head
    empty = jnp.zeros((span - new - kept, head), BF16)
    lane = iota((new, head), 1)
    scale = head ** (-0.5) * LOG2E
    for j in range(chips):
        facts = caches[j][2 * kept : 2 * kept + new + 16, :].astype(F32)
        own = facts[:new]
        high = jnp.sum(jnp.where(lane == new, own, 0.0), axis=1, keepdims=True)
        rest = jnp.sum(jnp.where(lane == new + 1, own, 0.0), axis=1, keepdims=True)
        angle = (128.0 * high + rest) * freq_ref[...]
        cosine, sine = jnp.cos(angle), jnp.sin(angle)
        sine = jnp.where(lane < head // 2, -sine, sine)

        def rope(values, gain_ref):
            values = norm_rows(values.astype(F32)) * gain_ref[...]
            return (values * cosine + pltpu.roll(values, head // 2, 1) * sine).astype(BF16)

        masks = []
        for at in range(span // head):
            seen = jnp.broadcast_to(facts[new + at : new + at + 1], (new, head))
            if at == 0:
                seen = jnp.where(lane < new, own, seen)
            masks.append(jnp.where(seen > 0.5, 0.0, NEG_FILL))
        mask = jnp.concatenate(masks, axis=1)
        key = rope(key_ref[chip ^ j], k_gain_ref)
        keys = jnp.concatenate([key, caches[j][0:kept, :], empty], axis=0)
        values = jnp.concatenate([value_ref[chip ^ j], caches[j][kept : 2 * kept, :], empty], axis=0)
        query = jnp.concatenate(
            [rope(queries[j][:, h * head : (h + 1) * head], q_gain_ref) for h in range(per_chip)],
            axis=0,
        )
        score = dot_last(query, keys) * scale
        score = score.reshape(per_chip, new, span) + mask[None]
        expo = jnp.exp2(score - jnp.max(score, axis=-1, keepdims=True))
        denom = jnp.sum(expo, axis=-1, keepdims=True).reshape(per_chip * new, 1)
        expo = expo.astype(BF16).reshape(per_chip * new, span)
        result = (dot(expo, values) / denom).astype(BF16)
        for h in range(per_chip):
            outs[j][:, h * head : (h + 1) * head] = result[h * new : (h + 1) * new]


def spread_kernel(chips, picks, *refs):
    got = refs[:chips]
    w_ref, w_sib = refs[chips : chips + 2]
    outs = refs[-chips:]
    depth, width = w_ref.shape
    left = jnp.concatenate([got[j][...] for j in range(chips)], axis=0)
    if picks:
        left = dot(refs[chips + 2][...].astype(BF16), left).astype(BF16)
    each = left.shape[0] // chips
    tile = min(512, width)
    for at in range(0, width, tile):
        part = dot(left[:, :depth], w_ref[:, at : at + tile])
        part = (part + dot(left[:, depth:], w_sib[:, at : at + tile])).astype(BF16)
        for j in range(chips):
            outs[j][:, at : at + tile] = part[j * each : (j + 1) * each]


def select_kernel(chips, *refs):
    blocks = refs[:chips]
    pick_ref, _ = refs[chips : chips + 2]
    sources = refs[chips + 2 : chips + 4]
    picked_ref = refs[chips + 4]
    targets = refs[chips + 5 : chips + 7]
    sems = refs[-1]
    copies = [
        pltpu.make_async_copy(source, target, sems.at[which])
        for which, (source, target) in enumerate(zip(sources, targets))
    ]
    for copy in copies:
        copy.start()
    values = jnp.concatenate([block[...] for block in blocks], axis=0)
    pick = pick_ref[0 : picked_ref.shape[0], :].astype(BF16)
    picked_ref[...] = dot(pick, values)
    for copy in copies:
        copy.wait()


def hidden_kernel(chips, *refs):
    got = refs[:chips]
    own_ref, out_ref = refs[chips:]
    total = own_ref[...].astype(F32)
    for j in range(chips):
        total = total + got[j][...].astype(F32)
    out_ref[...] = total


def rows_kernel(chips, *refs):
    got = refs[:chips]
    picked_ref, gain_ref, _, own_ref, other_ref = refs[chips:]
    hidden = picked_ref[...]
    for j in range(chips):
        hidden = hidden + got[j][...].astype(F32)
    normed = (norm_rows(hidden) * gain_ref[...]).astype(BF16)
    half = own_ref.shape[0]
    own_ref[...] = normed[:half]
    other_ref[...] = normed[half:]


def expert_kernel(own_ref, other_ref, gate_ref, up_ref, down_ref, own_out, other_out):
    left = jnp.concatenate([own_ref[...].astype(F32), other_ref[...].astype(F32)], axis=0)
    left = left.astype(BF16)
    gate = dot_last(left, gate_ref[0])
    up = dot_last(left, up_ref[0])
    inner = (gate / (1.0 + jnp.exp(-gate)) * up).astype(BF16)
    result = dot(inner, down_ref[0])
    half = own_ref.shape[0]
    own_out[...] = result[:half]
    other_out[...] = result[half:].astype(BF16)


def pack_kernel(chips, per, own_ref, other_ref, weight_ref, *outs):
    half = own_ref.shape[0]
    own = own_ref[...] * weight_ref[:half, 0:1]
    other = other_ref[...].astype(F32) * weight_ref[half:, 0:1]
    for j in range(chips):
        at = slice(j * per, (j + 1) * per)
        outs[j][...] = jnp.concatenate([own[at], other[at]], axis=0).astype(BF16)


def combine_kernel(chips, *refs):
    hidden_ref, combine_ref = refs[:2]
    got = refs[2 : 2 + chips]
    out_ref = refs[2 + chips]
    rows = jnp.concatenate([block[...].astype(F32) for block in got], axis=0)
    moe = dot(combine_ref[...].astype(BF16), rows.astype(BF16))
    out_ref[...] = (hidden_ref[...] + moe).astype(BF16)


def body(
    residual_in,
    attn_gain,
    w_query,
    w_keyval,
    query_gain,
    key_gain,
    w_out,
    ffn_gain,
    w_gate,
    w_up,
    w_down,
    key_cache,
    value_cache,
    prefix_lens,
    accepted,
    accept_path,
    parents,
    slot_kinds,
    expert_ids,
    gate_probs,
):
    devices = lax.axis_size("tensor")
    chips = devices // 2
    new, width = residual_in.shape
    head = query_gain.shape[0]
    kv_heads = key_cache.shape[2] // head
    q_width = w_query.shape[1]
    new_width = w_keyval.shape[0]
    all_tokens, top = expert_ids.shape
    tokens = chips * new
    per = new * top // EXPERTS
    path_len = accept_path.shape[1]
    rows = 2 * chips * per
    assert key_cache.shape[0] == 1 and w_gate.shape[0] == 1
    assert devices & (devices - 1) == 0
    vmem, smem, hbm, anywhere = pltpu.VMEM, pltpu.SMEM, pltpu.HBM, pl.ANY

    blocks = exchange([residual_in] * chips)
    wq_sib = hop(w_query, 1)
    wkv_sib = hop(w_keyval, 1)

    freq = ROPE_BASE ** (-2.0 * np.arange(head // 2) / head)
    freq = jnp.asarray(np.concatenate([freq, freq])[None, :], F32)
    length = 2 * (window_rows(path_len) + 16) + new + 16
    weights = [attn_gain[None, :], query_gain[None, :], key_gain[None, :], freq, w_query, w_keyval]
    prepared = call(
        functools.partial(prep_kernel, path_len, 2 * q_width // head, len(weights)),
        "prep",
        [in_vmem((length, head), BF16)] * chips + [in_vmem(w.shape, w.dtype) for w in weights],
        [
            (key_cache, hbm),
            (value_cache, hbm),
            (prefix_lens, smem),
            (accepted, smem),
            (slot_kinds, smem),
            (accept_path, hbm),
            (parents, hbm),
        ]
        + [(w, hbm) for w in weights],
        [
            pltpu.SMEM((1, path_len), jnp.int32),
            pltpu.VMEM((1, new), jnp.int32),
            pltpu.SemaphoreType.DMA((2,)),
            pltpu.SemaphoreType.DMA((2, chips, 2)),
            pltpu.SemaphoreType.DMA((len(weights),)),
        ],
        limit=16,
        moved=4 * chips * length * head,
    )
    gain, q_gain, k_gain, freq, wq, wkv = prepared[chips:]
    caches = exchange(prepared[:chips])

    pairs = new_width == head and chips == 4
    if pairs:
        sent = [in_vmem((chips, new, head), BF16)] * 2
    else:
        sent = [in_vmem((chips, new, 2 * new_width), BF16)]
    projected = call(
        functools.partial(project_kernel, chips, pairs),
        "project",
        [in_vmem((new, 2 * q_width), BF16)] * chips + sent,
        [(block, vmem) for block in blocks]
        + [(w, vmem) for w in (gain, wq, wkv, wq_sib, wkv_sib)],
        limit=16,
    )
    queries, sent = projected[:chips], projected[chips:]
    wo_sib = hop(w_out, 1)

    weights = [ffn_gain[None, :], w_out, w_down]
    pick, combine, weight, ffn, wo, wd = call(
        functools.partial(route_kernel, per, new, len(weights)),
        "route",
        [
            in_vmem((chips * rows, tokens), F32),
            in_vmem((new, devices * per), F32),
            in_vmem((rows, 128), F32),
        ]
        + [in_vmem(w.shape, w.dtype) for w in weights],
        [(queries[0], anywhere), (expert_ids.T, hbm), (gate_probs.T, hbm)]
        + [(w, hbm) for w in weights],
        [
            pltpu.VMEM((top, all_tokens), jnp.int32),
            pltpu.VMEM((top, all_tokens), F32),
            pltpu.VMEM((devices, tokens), F32),
            pltpu.VMEM((devices, tokens), F32),
            pltpu.VMEM((devices * per, tokens), F32),
            pltpu.SemaphoreType.DMA((2 + len(weights),)),
        ],
        limit=16,
    )
    if pairs:
        routes = ([(0, 1), (1, 2), (2, 0), (3, 3)], [(0, 0), (1, 3), (2, 1), (3, 2)])
        came = []
        second = call(
            hold_kernel,
            "hold",
            [in_vmem((chips, new, head), BF16)],
            [(sent[1], vmem), (wo_sib, anywhere)],
            limit=8,
            same={0: 0},
        )[0]
        for part, route in zip((sent[0], second), routes):
            links = [(step(p) ^ core, step(q) ^ core) for p, q in route for core in range(2)]
            came.append(lax.ppermute(part, "tensor", links))
        key_new, value_new = call(
            fresh_kernel,
            "fresh",
            [in_vmem((chips, new, head), BF16)] * 2,
            [(came[0], vmem), (came[1], vmem)],
            limit=8,
        )
    else:
        groups = [[step(p) ^ core for p in range(chips)] for core in range(2)]
        every = lax.all_gather(sent[0], "tensor", axis_index_groups=groups)
        every = every.transpose(1, 2, 0, 3).reshape(chips, new, 2 * kv_heads * head)
        at = lax.axis_index("tensor") // 2 * kv_heads // chips * head
        key_new = lax.dynamic_slice_in_dim(every, at, head, 2)
        value_new = lax.dynamic_slice_in_dim(every, at + kv_heads * head, head, 2)
    picked, wg, wu = call(
        functools.partial(select_kernel, chips),
        "select",
        [in_vmem((rows, width), F32)] + [in_vmem(w.shape, w.dtype) for w in (w_gate, w_up)],
        [(block, vmem) for block in blocks]
        + [(pick, vmem), (queries[0], anywhere), (w_gate, hbm), (w_up, hbm)],
        [pltpu.SemaphoreType.DMA((2,))],
        limit=8,
    )
    heads = call(
        functools.partial(attend_kernel, chips),
        "attend",
        [in_vmem((new, 2 * q_width), BF16)] * chips,
        [(block, vmem) for block in queries]
        + [(block, vmem) for block in caches]
        + [(x, vmem) for x in (key_new, value_new, freq, q_gain, k_gain)]
        + [(wg, anywhere)],
        limit=16,
        flops=8 * new * chips * q_width * length // 2,
        moved=2 * chips * length * head,
    )

    def spread(name, each, more):
        return call(
            functools.partial(spread_kernel, chips, name == "experts"),
            name,
            [in_vmem((each, width), BF16)] * chips,
            [(block, vmem) for block in heads] + [(wo, vmem), (wo_sib, vmem)] + more,
            limit=16,
            flops=4 * chips * each * width * q_width,
            moved=4 * q_width * width,
        )

    partial = spread("experts", rows, [(pick, vmem), (wg, anywhere)])
    for_experts = exchange(partial)
    partial = spread("slots", new, [(partial[0], anywhere)])
    for_slots = exchange(partial)

    own, other = call(
        functools.partial(rows_kernel, chips),
        "rows",
        [in_vmem((rows // 2, width), BF16)] * 2,
        [(block, vmem) for block in for_experts]
        + [(picked, vmem), (ffn, vmem), (partial[0], anywhere)],
        limit=8,
        moved=2 * chips * rows * width,
    )
    own_out, other_out = call(
        expert_kernel,
        "expert",
        [in_vmem((rows // 2, width), F32), in_vmem((rows // 2, width), BF16)],
        [(own, vmem), (hop(other, 1), vmem), (wg, vmem), (wu, vmem), (wd, vmem)],
        limit=16,
        flops=6 * rows * width * w_gate.shape[1],
        moved=6 * width * w_gate.shape[1],
    )
    results = call(
        functools.partial(pack_kernel, chips, per),
        "pack",
        [in_vmem((2 * per, width), BF16)] * chips,
        [(own_out, vmem), (hop(other_out, 1), vmem), (weight, vmem)],
        limit=8,
        moved=4 * rows * width,
    )
    returned = exchange(results)
    hidden = call(
        functools.partial(hidden_kernel, chips),
        "hidden",
        [in_vmem((new, width), F32)],
        [(block, vmem) for block in for_slots] + [(residual_in, vmem)],
        limit=8,
        moved=2 * chips * new * width,
    )[0]
    return call(
        functools.partial(combine_kernel, chips),
        "combine",
        [jax.ShapeDtypeStruct((new, width), BF16)],
        [(hidden, vmem), (combine, vmem)] + [(block, vmem) for block in returned],
        limit=8,
        moved=6 * new * width,
    )[0]


def solution(mesh):
    in_specs = (
        P(("group", "tensor"), None),
        P(),
        P(None, "tensor"),
        P("tensor", None),
        P(),
        P(),
        P("tensor", None),
        P(),
        P("tensor", None, None),
        P("tensor", None, None),
        P("tensor", None, None),
        P(("group", "tensor"), None, None),
        P(("group", "tensor"), None, None),
        P(("group", "tensor")),
        P(("group", "tensor")),
        P(("group", "tensor"), None),
        P(("group", "tensor"), None),
        P(("group", "tensor")),
        P("group", None),
        P("group", None),
    )
    out_specs = P(("group", "tensor"), None)
    return jax.shard_map(body, mesh=mesh, in_specs=in_specs, out_specs=out_specs, check_vma=False)
```

```python
import functools
import math

import jax
import jax.numpy as jnp
import numpy as np
from jax import lax
from jax.experimental import pallas as pl
from jax.experimental.pallas import tpu as pltpu
from jax.sharding import PartitionSpec as P

EXPERTS = 128
SINK = 4
WIN = 512

EPSILON = 1e-06
NEG_FILL = -1e30
ROPE_BASE = 1000000.0
LOG2E = math.log2(math.e)
F32 = jnp.float32
BF16 = jnp.bfloat16
MIB = 1 << 20


def step(j):
    return 2 * j + (j >> 1) % 2


def iota(shape, dim):
    return lax.broadcasted_iota(jnp.int32, shape, dim)


def dot(left, right):
    return jnp.dot(left, right, preferred_element_type=F32)


def dot_last(left, right):
    return lax.dot_general(left, right, (((1,), (1,)), ((), ())), preferred_element_type=F32)


def dot_first(left, right):
    return lax.dot_general(left, right, (((0,), (0,)), ((), ())), preferred_element_type=F32)


def norm_rows(values):
    return values * lax.rsqrt(jnp.mean(values * values, axis=-1, keepdims=True) + EPSILON)


def in_vmem(shape, dtype):
    return pltpu.VMEM(shape, dtype)


def call(kernel, name, outs, args, scratch=(), limit=16, flops=0, moved=0, same=None):
    arrays = []
    specs = []
    for array, space in args:
        if space is pltpu.HBM or space is pltpu.VMEM:
            array = pltpu.with_memory_space_constraint(array, space)
        arrays.append(array)
        specs.append(pl.BlockSpec(memory_space=space))
    return pl.pallas_call(
        kernel,
        out_shape=outs,
        in_specs=specs,
        out_specs=[pl.BlockSpec(memory_space=pltpu.VMEM) for _ in outs],
        scratch_shapes=list(scratch),
        input_output_aliases=same or {},
        compiler_params=pltpu.CompilerParams(vmem_limit_bytes=limit * MIB),
        cost_estimate=pl.CostEstimate(flops=flops, bytes_accessed=moved, transcendentals=0),
        name=name,
    )(*arrays)


def hop(value, step):
    devices = lax.axis_size("tensor")
    return lax.ppermute(value, "tensor", [(i, i ^ step) for i in range(devices)])


def exchange(blocks):
    return [blocks[0]] + [hop(blocks[j], step(j)) for j in range(1, len(blocks))]


def window_rows(path_len):
    return -(-(WIN + 2 * (path_len - 1) + 16) // 16) * 16


def prep_kernel(path_len, n_weights, *refs):
    key_cache, value_cache, prefix_ref, accepted_ref, kind_ref = refs[:5]
    small_in = refs[5:10]
    sources = refs[10 : 10 + n_weights]
    refs = refs[10 + n_weights :]
    keys_ref, values_ref, mask_ref, rot_ref = refs[:4]
    targets = refs[4 : 4 + n_weights]
    refs = refs[4 + n_weights :]
    path_ref, parents_ref, freq_ref, q_gain_ref, k_gain_ref = refs[:5]
    small_sems, cache_sems, weight_sems = refs[5:]

    new = mask_ref.shape[0]
    kv_heads, span, head = keys_ref.shape
    cache_len = key_cache.shape[1]
    wide = window_rows(path_len)
    sink_at, win_at = new, new + 16
    end = win_at + wide

    small = [
        pltpu.make_async_copy(source, target, small_sems.at[which])
        for which, (source, target) in enumerate(zip(small_in, refs[:5]))
    ]
    for copy in small:
        copy.start()
    copies = [
        pltpu.make_async_copy(source, target, weight_sems.at[which])
        for which, (source, target) in enumerate(zip(sources, targets))
    ]
    prefix = prefix_ref[0]
    accepted = accepted_ref[0]
    total = prefix + accepted
    low = jnp.maximum(total - WIN, 0)
    start = pl.multiple_of(jnp.minimum((low // 16) * 16, cache_len - wide), 16)
    for which, (cache, buf) in enumerate(((key_cache, keys_ref), (value_cache, values_ref))):
        for kv in range(kv_heads):
            cols = pl.ds(kv * head, head)
            copies.append(
                pltpu.make_async_copy(
                    cache.at[0, pl.ds(start, wide), cols],
                    buf.at[kv, pl.ds(win_at, wide)],
                    cache_sems.at[which, kv, 0],
                )
            )
            copies.append(
                pltpu.make_async_copy(
                    cache.at[0, pl.ds(0, 16), cols],
                    buf.at[kv, pl.ds(sink_at, 16)],
                    cache_sems.at[which, kv, 1],
                )
            )
    for copy in copies:
        copy.start()

    for buf in (keys_ref, values_ref):
        buf[:, 0:new, :] = jnp.zeros((kv_heads, new, head), BF16)
        buf[:, end:span, :] = jnp.zeros((kv_heads, span - end, head), BF16)

    for copy in small:
        copy.wait()
    column = iota((1, span), 1)
    row = jnp.where(column < win_at, column - sink_at, start + column - win_at)
    taken = jnp.zeros((1, span), jnp.bool_)
    for step in range(path_len):
        at = prefix + path_ref[0, step]
        taken = taken | ((row == at) & (step < accepted))
    old = (row < prefix) & ((row < SINK) | (row >= total - WIN))
    in_window = (column >= win_at) & (column < end) & (old | taken)
    in_sink = (column >= sink_at) & (column < win_at) & (row < SINK) & (row < prefix) & (start > 0)
    seen = jnp.where(in_window | in_sink, 0.0, NEG_FILL)
    mask_ref[...] = jnp.broadcast_to(seen, mask_ref.shape)

    down, across = iota((new, new), 0), iota((new, new), 1)
    eye = (down == across).astype(F32)
    back = eye + (down == parents_ref[...]).astype(F32)
    for _ in range((new - 1).bit_length()):
        half = back.astype(BF16)
        back = jnp.minimum(dot(half, half), 1.0)
    reach = dot_first(back.astype(BF16), eye.astype(BF16))
    tree = (kind_ref[0] == 1).astype(F32)
    causal = (across <= down).astype(F32)
    allowed = tree * reach + (1.0 - tree) * causal
    mask_ref[:, 0:new] = jnp.where(allowed > 0.5, 0.0, NEG_FILL)
    depth = tree * (jnp.sum(reach, axis=1, keepdims=True) - 1.0)
    depth = depth + (1.0 - tree) * iota((new, 1), 0).astype(F32)
    angle = (total.astype(F32) + depth) * freq_ref[...]
    lane = iota(angle.shape, 1)
    cosine, sine = jnp.cos(angle), jnp.sin(angle)
    sine = jnp.where(lane < head // 2, -sine, sine)
    for which, gain_ref in enumerate((q_gain_ref, k_gain_ref)):
        gain = jnp.broadcast_to(gain_ref[...], angle.shape)
        rot_ref[2 * which] = cosine * gain
        rot_ref[2 * which + 1] = sine * pltpu.roll(gain, head // 2, 1)
    for copy in copies:
        copy.wait()


def route_kernel(per, new, n_weights, *refs):
    small_in = refs[1:3]
    sources = refs[3 : 3 + n_weights]
    refs = refs[3 + n_weights :]
    pick_ref, combine_ref, weight_ref = refs[:3]
    targets = refs[3 : 3 + n_weights]
    ids_ref, gates_ref, hit_ref, rank_ref, own_ref, sems = refs[3 + n_weights :]
    sources, targets = (*small_in, *sources), (ids_ref, gates_ref, *targets)
    copies = [
        pltpu.make_async_copy(source, target, sems.at[which])
        for which, (source, target) in enumerate(zip(sources, targets))
    ]
    for copy in copies:
        copy.start()
    for copy in copies[:2]:
        copy.wait()

    me = lax.axis_index("tensor")
    all_tokens = ids_ref.shape[1]
    devices = hit_ref.shape[0]
    chips = devices // 2
    tokens = chips * new
    slot = iota((all_tokens, tokens), 1) // new
    source = (me ^ (2 * slot + ((slot >> 1) & 1))) * new + iota((all_tokens, tokens), 1) % new
    order = (iota((all_tokens, tokens), 0) == source).astype(F32)
    ids = dot(ids_ref[...].astype(F32).astype(BF16), order.astype(BF16))
    gates = lax.dot_general(
        gates_ref[...],
        order,
        (((1,), (0,)), ((), ())),
        precision=lax.Precision.HIGHEST,
        preferred_element_type=F32,
    )
    for rel in range(devices):
        expert = (me ^ step(rel // 2) ^ (rel % 2)).astype(F32)
        named = (ids == expert).astype(F32)
        hit_ref[rel : rel + 1, :] = jnp.max(named, axis=0, keepdims=True)
    before, later = iota((tokens, tokens), 0), iota((tokens, tokens), 1)
    earlier = (before < later) & (before // new == later // new)
    rank_ref[...] = dot(hit_ref[...].astype(BF16), earlier.astype(F32).astype(BF16))
    rows = chips * per
    slot_of = iota((rows, tokens), 1) // new
    row_slot = iota((rows, tokens), 0) // per
    row_rank = (iota((rows, tokens), 0) % per).astype(F32)
    in_first = iota((1, tokens), 1) < new
    for rel in range(devices):
        hit = hit_ref[rel : rel + 1, :] > 0.5
        rank = rank_ref[rel : rel + 1, :]
        chosen = (slot_of == (row_slot ^ (rel // 2))) & hit & (rank == row_rank)
        pick_ref[rel * rows : (rel + 1) * rows, :] = chosen.astype(F32)
        if rel < 2:
            named = ids == (me ^ rel).astype(F32)
            weight = jnp.sum(jnp.where(named, gates, 0.0), axis=0, keepdims=True)
            weight = jnp.sum(jnp.where(chosen, weight, 0.0), axis=1, keepdims=True)
            weight_ref[rel * rows : (rel + 1) * rows, :] = jnp.broadcast_to(
                weight, (rows, weight_ref.shape[1])
            )
        for place in range(per):
            at = rel * per + place
            own_ref[at : at + 1, :] = (in_first & hit & (rank == float(place))).astype(F32)
    first = (iota((tokens, new), 0) == iota((tokens, new), 1)).astype(F32)
    combine_ref[...] = lax.dot_general(
        first.astype(BF16),
        own_ref[...].astype(BF16),
        (((0,), (1,)), ((), ())),
        preferred_element_type=F32,
    )
    for copy in copies[2:]:
        copy.wait()


def project_kernel(count, *refs):
    blocks = refs[:count]
    gain_ref, wq_ref, wkv_ref, wq_sib, wkv_sib = refs[count : count + 5]
    outs = refs[count + 5 :]
    rows = blocks[0].shape[0]
    gain = gain_ref[...]
    values = [(norm_rows(block[...].astype(F32)) * gain).astype(BF16) for block in blocks]
    values = jnp.concatenate(values, axis=0)

    def put(result, at):
        result = result.astype(BF16)
        for j in range(count):
            outs[j][:, at : at + result.shape[1]] = result[j * rows : (j + 1) * rows]

    wide, narrow = wq_ref.shape[1], wkv_ref.shape[0]
    put(dot(values, wq_ref[...]), 0)
    put(dot(values, wq_sib[...]), wide)
    put(dot_last(values, wkv_ref[...]), 2 * wide)
    put(dot_last(values, wkv_sib[...]), 2 * wide + narrow)


def attend_kernel(chips, q_width, kv_ready, *refs):
    got = refs[:chips]
    at = chips + 1 if kv_ready else chips
    keys_ref, values_ref, mask_ref, rot_ref = refs[at : at + 4]
    outs = refs[at + 5 : at + 5 + chips]
    fresh_ref = refs[chips] if kv_ready else refs[-1]
    me = lax.axis_index("tensor")
    chip = me // 2
    new = got[0].shape[0]
    kv_heads, span, head = keys_ref.shape
    per_chip = 2 * q_width // head
    group = chips * per_chip // kv_heads

    if not kv_ready:
        for rel in range(2 * chips):
            left = 2 * q_width + (rel % 2) * head
            fresh_ref[step(rel // 2) ^ (rel % 2)] = got[rel // 2][:, left : left + head]

    def rope(values, which):
        values = norm_rows(values.astype(F32))
        turned = pltpu.roll(values, head // 2, 1)
        return (values * rot_ref[2 * which] + turned * rot_ref[2 * which + 1]).astype(BF16)

    scale = head ** (-0.5) * LOG2E
    for j in range(chips):
        kv = (chip ^ j) * per_chip // group
        key_at, value_at = kv, kv + kv_heads
        if not kv_ready:
            key_at, value_at = me ^ key_at, me ^ value_at
        keys = jnp.concatenate([rope(fresh_ref[key_at], 1), keys_ref[kv, new:span]], axis=0)
        values = jnp.concatenate([fresh_ref[value_at], values_ref[kv, new:span]], axis=0)
        query = jnp.concatenate(
            [rope(got[j][:, h * head : (h + 1) * head], 0) for h in range(per_chip)], axis=0
        )
        score = dot_last(query, keys) * scale
        score = score.reshape(per_chip, new, span) + mask_ref[...][None]
        expo = jnp.exp2(score - jnp.max(score, axis=-1, keepdims=True))
        denom = jnp.sum(expo, axis=-1, keepdims=True).reshape(per_chip * new, 1)
        expo = expo.astype(BF16).reshape(per_chip * new, span)
        result = (dot(expo, values) / denom).astype(BF16)
        for h in range(per_chip):
            outs[j][:, h * head : (h + 1) * head] = result[h * new : (h + 1) * new]


def spread_kernel(chips, picks, *refs):
    got = refs[:chips]
    w_ref, w_sib = refs[chips : chips + 2]
    outs = refs[-chips:]
    depth, width = w_ref.shape
    left = jnp.concatenate([got[j][...] for j in range(chips)], axis=0)
    if picks:
        left = dot(refs[chips + 2][...].astype(BF16), left).astype(BF16)
    each = left.shape[0] // chips
    tile = min(512, width)
    for at in range(0, width, tile):
        part = dot(left[:, :depth], w_ref[:, at : at + tile])
        part = (part + dot(left[:, depth:], w_sib[:, at : at + tile])).astype(BF16)
        for j in range(chips):
            outs[j][:, at : at + tile] = part[j * each : (j + 1) * each]


def select_kernel(chips, *refs):
    blocks = refs[:chips]
    pick_ref, _ = refs[chips : chips + 2]
    sources = refs[chips + 2 : chips + 4]
    picked_ref = refs[chips + 4]
    targets = refs[chips + 5 : chips + 7]
    sems = refs[-1]
    copies = [
        pltpu.make_async_copy(source, target, sems.at[which])
        for which, (source, target) in enumerate(zip(sources, targets))
    ]
    for copy in copies:
        copy.start()
    values = jnp.concatenate([block[...] for block in blocks], axis=0)
    pick = pick_ref[0 : picked_ref.shape[0], :].astype(BF16)
    picked_ref[...] = dot(pick, values)
    for copy in copies:
        copy.wait()


def hidden_kernel(chips, *refs):
    got = refs[:chips]
    own_ref, out_ref = refs[chips:]
    total = own_ref[...].astype(F32)
    for j in range(chips):
        total = total + got[j][...].astype(F32)
    out_ref[...] = total


def rows_kernel(chips, *refs):
    got = refs[:chips]
    picked_ref, gain_ref, _, own_ref, other_ref = refs[chips:]
    hidden = picked_ref[...]
    for j in range(chips):
        hidden = hidden + got[j][...].astype(F32)
    normed = (norm_rows(hidden) * gain_ref[...]).astype(BF16)
    half = own_ref.shape[0]
    own_ref[...] = normed[:half]
    other_ref[...] = normed[half:]


def expert_kernel(own_ref, other_ref, gate_ref, up_ref, down_ref, own_out, other_out):
    left = jnp.concatenate([own_ref[...].astype(F32), other_ref[...].astype(F32)], axis=0)
    left = left.astype(BF16)
    gate = dot_last(left, gate_ref[0])
    up = dot_last(left, up_ref[0])
    inner = (gate / (1.0 + jnp.exp(-gate)) * up).astype(BF16)
    result = dot(inner, down_ref[0])
    half = own_ref.shape[0]
    own_out[...] = result[:half]
    other_out[...] = result[half:].astype(BF16)


def pack_kernel(chips, per, own_ref, other_ref, weight_ref, *outs):
    half = own_ref.shape[0]
    own = own_ref[...] * weight_ref[:half, 0:1]
    other = other_ref[...].astype(F32) * weight_ref[half:, 0:1]
    for j in range(chips):
        at = slice(j * per, (j + 1) * per)
        outs[j][...] = jnp.concatenate([own[at], other[at]], axis=0).astype(BF16)


def combine_kernel(chips, *refs):
    hidden_ref, combine_ref = refs[:2]
    got = refs[2 : 2 + chips]
    out_ref = refs[2 + chips]
    rows = jnp.concatenate([block[...].astype(F32) for block in got], axis=0)
    moe = dot(combine_ref[...].astype(BF16), rows.astype(BF16))
    out_ref[...] = (hidden_ref[...] + moe).astype(BF16)


def body(
    residual_in,
    attn_gain,
    w_query,
    w_keyval,
    query_gain,
    key_gain,
    w_out,
    ffn_gain,
    w_gate,
    w_up,
    w_down,
    key_cache,
    value_cache,
    prefix_lens,
    accepted,
    accept_path,
    parents,
    slot_kinds,
    expert_ids,
    gate_probs,
):
    devices = lax.axis_size("tensor")
    chips = devices // 2
    new, width = residual_in.shape
    head = query_gain.shape[0]
    kv_heads = key_cache.shape[2] // head
    q_width = w_query.shape[1]
    new_width = w_keyval.shape[0]
    all_tokens, top = expert_ids.shape
    tokens = chips * new
    per = new * top // EXPERTS
    path_len = accept_path.shape[1]
    rows = 2 * chips * per
    assert key_cache.shape[0] == 1 and w_gate.shape[0] == 1
    assert devices & (devices - 1) == 0
    vmem, smem, hbm, anywhere = pltpu.VMEM, pltpu.SMEM, pltpu.HBM, pl.ANY

    blocks = exchange([residual_in] * chips)
    wq_sib = hop(w_query, 1)
    wkv_sib = hop(w_keyval, 1)

    freq = ROPE_BASE ** (-2.0 * np.arange(head // 2) / head)
    freq = jnp.asarray(np.concatenate([freq, freq])[None, :], F32)
    span = -(-(new + 16 + window_rows(path_len)) // 128) * 128
    weights = [attn_gain[None, :], w_query, w_keyval]
    keys, values, mask, rot, gain, wq, wkv = call(
        functools.partial(prep_kernel, path_len, len(weights)),
        "prep",
        [
            in_vmem((kv_heads, span, head), BF16),
            in_vmem((kv_heads, span, head), BF16),
            in_vmem((new, span), F32),
            in_vmem((4, new, head), F32),
        ]
        + [in_vmem(w.shape, w.dtype) for w in weights],
        [
            (key_cache, hbm),
            (value_cache, hbm),
            (prefix_lens, smem),
            (accepted, smem),
            (slot_kinds, smem),
            (accept_path, hbm),
            (parents, hbm),
            (freq, hbm),
            (query_gain[None, :], hbm),
            (key_gain[None, :], hbm),
        ]
        + [(w, hbm) for w in weights],
        [
            pltpu.SMEM((1, path_len), jnp.int32),
            pltpu.VMEM((1, new), jnp.int32),
            pltpu.VMEM((1, head), F32),
            pltpu.VMEM((1, head), F32),
            pltpu.VMEM((1, head), F32),
            pltpu.SemaphoreType.DMA((5,)),
            pltpu.SemaphoreType.DMA((2, kv_heads, 2)),
            pltpu.SemaphoreType.DMA((len(weights),)),
        ],
        limit=16,
        moved=4 * span * kv_heads * head * 2,
    )

    projected = call(
        functools.partial(project_kernel, chips),
        "project",
        [in_vmem((new, 2 * (q_width + new_width)), BF16)] * chips,
        [(block, vmem) for block in blocks]
        + [(w, vmem) for w in (gain, wq, wkv, wq_sib, wkv_sib)],
        limit=16,
        flops=4 * tokens * width * (q_width + new_width),
        moved=4 * width * (q_width + new_width),
    )
    got = exchange(projected)

    weights = [ffn_gain[None, :], w_out, w_down]
    pick, combine, weight, ffn, wo, wd = call(
        functools.partial(route_kernel, per, new, len(weights)),
        "route",
        [
            in_vmem((chips * rows, tokens), F32),
            in_vmem((new, devices * per), F32),
            in_vmem((rows, 128), F32),
        ]
        + [in_vmem(w.shape, w.dtype) for w in weights],
        [(projected[0], anywhere), (expert_ids.T, hbm), (gate_probs.T, hbm)]
        + [(w, hbm) for w in weights],
        [
            pltpu.VMEM((top, all_tokens), jnp.int32),
            pltpu.VMEM((top, all_tokens), F32),
            pltpu.VMEM((devices, tokens), F32),
            pltpu.VMEM((devices, tokens), F32),
            pltpu.VMEM((devices * per, tokens), F32),
            pltpu.SemaphoreType.DMA((2 + len(weights),)),
        ],
        limit=16,
        moved=4 * width * (q_width + w_down.shape[1]),
    )
    kv_ready = []
    if new_width != head:
        pieces = [None] * devices
        for rel in range(devices):
            left = 2 * q_width + (rel % 2) * new_width
            pieces[step(rel // 2) ^ (rel % 2)] = got[rel // 2][:, left : left + new_width]
        pieces = jnp.stack(pieces)[lax.axis_index("tensor") ^ jnp.arange(devices)]
        pieces = pieces.transpose(1, 0, 2).reshape(new, 2 * kv_heads, head)
        kv_ready = [(pieces.transpose(1, 0, 2), vmem)]
    *attended, wo = call(
        functools.partial(attend_kernel, chips, q_width, bool(kv_ready)),
        "attend",
        [in_vmem((new, 2 * q_width), BF16)] * chips + [in_vmem(wo.shape, wo.dtype)],
        [(block, vmem) for block in got]
        + kv_ready
        + [(keys, vmem), (values, vmem), (mask, vmem), (rot, vmem)]
        + [(wo, vmem)],
        [] if kv_ready else [pltpu.VMEM((devices, new, head), BF16)],
        limit=16,
        same={chips + len(kv_ready) + 4: chips},
        flops=8 * new * chips * q_width * span,
        moved=4 * span * kv_heads * head,
    )
    wo_sib = hop(wo, 1)
    heads = exchange(attended)
    picked, wg, wu = call(
        functools.partial(select_kernel, chips),
        "select",
        [in_vmem((rows, width), F32)] + [in_vmem(w.shape, w.dtype) for w in (w_gate, w_up)],
        [(block, vmem) for block in blocks]
        + [(pick, vmem), (attended[0], anywhere), (w_gate, hbm), (w_up, hbm)],
        [pltpu.SemaphoreType.DMA((2,))],
        limit=8,
        flops=2 * rows * width * tokens,
        moved=8 * width * w_gate.shape[1],
    )

    def spread(name, each, more):
        return call(
            functools.partial(spread_kernel, chips, name == "experts"),
            name,
            [in_vmem((each, width), BF16)] * chips,
            [(block, vmem) for block in heads] + [(wo, vmem), (wo_sib, vmem)] + more,
            limit=16,
            flops=4 * chips * each * width * q_width,
            moved=4 * q_width * width,
        )

    partial = spread("experts", rows, [(pick, vmem), (wg, anywhere)])
    for_experts = exchange(partial)
    partial = spread("slots", new, [(partial[0], anywhere)])
    for_slots = exchange(partial)

    own, other = call(
        functools.partial(rows_kernel, chips),
        "rows",
        [in_vmem((rows // 2, width), BF16)] * 2,
        [(block, vmem) for block in for_experts]
        + [(picked, vmem), (ffn, vmem), (partial[0], anywhere)],
        limit=8,
        moved=2 * chips * rows * width,
    )
    own_out, other_out = call(
        expert_kernel,
        "expert",
        [in_vmem((rows // 2, width), F32), in_vmem((rows // 2, width), BF16)],
        [(own, vmem), (hop(other, 1), vmem), (wg, vmem), (wu, vmem), (wd, vmem)],
        limit=16,
        flops=6 * rows * width * w_gate.shape[1],
        moved=6 * width * w_gate.shape[1],
    )
    results = call(
        functools.partial(pack_kernel, chips, per),
        "pack",
        [in_vmem((2 * per, width), BF16)] * chips,
        [(own_out, vmem), (hop(other_out, 1), vmem), (weight, vmem)],
        limit=8,
        moved=4 * rows * width,
    )
    returned = exchange(results)
    hidden = call(
        functools.partial(hidden_kernel, chips),
        "hidden",
        [in_vmem((new, width), F32)],
        [(block, vmem) for block in for_slots] + [(residual_in, vmem)],
        limit=8,
        moved=2 * chips * new * width,
    )[0]
    return call(
        functools.partial(combine_kernel, chips),
        "combine",
        [jax.ShapeDtypeStruct((new, width), BF16)],
        [(hidden, vmem), (combine, vmem)] + [(block, vmem) for block in returned],
        limit=8,
        moved=6 * new * width,
    )[0]


def solution(mesh):
    in_specs = (
        P(("group", "tensor"), None),
        P(),
        P(None, "tensor"),
        P("tensor", None),
        P(),
        P(),
        P("tensor", None),
        P(),
        P("tensor", None, None),
        P("tensor", None, None),
        P("tensor", None, None),
        P(("group", "tensor"), None, None),
        P(("group", "tensor"), None, None),
        P(("group", "tensor")),
        P(("group", "tensor")),
        P(("group", "tensor"), None),
        P(("group", "tensor"), None),
        P(("group", "tensor")),
        P("group", None),
        P("group", None),
    )
    out_specs = P(("group", "tensor"), None)
    return jax.shard_map(body, mesh=mesh, in_specs=in_specs, out_specs=out_specs, check_vma=False)
```

```python
import functools
import math

import jax
import jax.numpy as jnp
import numpy as np
from jax import lax
from jax.experimental import pallas as pl
from jax.experimental.pallas import tpu as pltpu
from jax.sharding import PartitionSpec as P

EXPERTS = 128
SINK = 4
WIN = 512

EPSILON = 1e-06
NEG_FILL = -1e30
ROPE_BASE = 1000000.0
LOG2E = math.log2(math.e)
F32 = jnp.float32
BF16 = jnp.bfloat16
MIB = 1 << 20


def step(j):
    return 2 * j + (j >> 1) % 2


def iota(shape, dim):
    return lax.broadcasted_iota(jnp.int32, shape, dim)


def dot(left, right):
    return jnp.dot(left, right, preferred_element_type=F32)


def dot_last(left, right):
    return lax.dot_general(left, right, (((1,), (1,)), ((), ())), preferred_element_type=F32)


def dot_first(left, right):
    return lax.dot_general(left, right, (((0,), (0,)), ((), ())), preferred_element_type=F32)


def norm_rows(values):
    return values * lax.rsqrt(jnp.mean(values * values, axis=-1, keepdims=True) + EPSILON)


def in_vmem(shape, dtype):
    return pltpu.VMEM(shape, dtype)


def call(kernel, name, outs, args, scratch=(), limit=16, flops=0, moved=0, same=None):
    arrays = []
    specs = []
    for array, space in args:
        if space is pltpu.HBM or space is pltpu.VMEM:
            array = pltpu.with_memory_space_constraint(array, space)
        arrays.append(array)
        specs.append(pl.BlockSpec(memory_space=space))
    return pl.pallas_call(
        kernel,
        out_shape=outs,
        in_specs=specs,
        out_specs=[pl.BlockSpec(memory_space=pltpu.VMEM) for _ in outs],
        scratch_shapes=list(scratch),
        input_output_aliases=same or {},
        compiler_params=pltpu.CompilerParams(vmem_limit_bytes=limit * MIB),
        cost_estimate=pl.CostEstimate(flops=flops, bytes_accessed=moved, transcendentals=0),
        name=name,
    )(*arrays)


def hop(value, step):
    devices = lax.axis_size("tensor")
    return lax.ppermute(value, "tensor", [(i, i ^ step) for i in range(devices)])


def exchange(blocks):
    return [blocks[0]] + [hop(blocks[j], step(j)) for j in range(1, len(blocks))]


def window_rows(path_len):
    return -(-(WIN + 2 * (path_len - 1) + 16) // 16) * 16


def prep_kernel(path_len, n_weights, *refs):
    key_cache, value_cache, prefix_ref, accepted_ref, kind_ref = refs[:5]
    small_in = refs[5:10]
    sources = refs[10 : 10 + n_weights]
    refs = refs[10 + n_weights :]
    keys_ref, values_ref, mask_ref, rot_ref = refs[:4]
    targets = refs[4 : 4 + n_weights]
    refs = refs[4 + n_weights :]
    path_ref, parents_ref, freq_ref, q_gain_ref, k_gain_ref = refs[:5]
    small_sems, cache_sems, weight_sems = refs[5:]

    new = mask_ref.shape[0]
    kv_heads, span, head = keys_ref.shape
    cache_len = key_cache.shape[1]
    wide = window_rows(path_len)
    sink_at, win_at = new, new + 16
    end = win_at + wide

    small = [
        pltpu.make_async_copy(source, target, small_sems.at[which])
        for which, (source, target) in enumerate(zip(small_in, refs[:5]))
    ]
    for copy in small:
        copy.start()
    copies = [
        pltpu.make_async_copy(source, target, weight_sems.at[which])
        for which, (source, target) in enumerate(zip(sources, targets))
    ]
    prefix = prefix_ref[0]
    accepted = accepted_ref[0]
    total = prefix + accepted
    low = jnp.maximum(total - WIN, 0)
    start = pl.multiple_of(jnp.minimum((low // 16) * 16, cache_len - wide), 16)
    for which, (cache, buf) in enumerate(((key_cache, keys_ref), (value_cache, values_ref))):
        for kv in range(kv_heads):
            cols = pl.ds(kv * head, head)
            copies.append(
                pltpu.make_async_copy(
                    cache.at[0, pl.ds(start, wide), cols],
                    buf.at[kv, pl.ds(win_at, wide)],
                    cache_sems.at[which, kv, 0],
                )
            )
            copies.append(
                pltpu.make_async_copy(
                    cache.at[0, pl.ds(0, 16), cols],
                    buf.at[kv, pl.ds(sink_at, 16)],
                    cache_sems.at[which, kv, 1],
                )
            )
    for copy in copies:
        copy.start()

    for buf in (keys_ref, values_ref):
        buf[:, 0:new, :] = jnp.zeros((kv_heads, new, head), BF16)
        buf[:, end:span, :] = jnp.zeros((kv_heads, span - end, head), BF16)

    for copy in small:
        copy.wait()
    column = iota((1, span), 1)
    row = jnp.where(column < win_at, column - sink_at, start + column - win_at)
    taken = jnp.zeros((1, span), jnp.bool_)
    for step in range(path_len):
        at = prefix + path_ref[0, step]
        taken = taken | ((row == at) & (step < accepted))
    old = (row < prefix) & ((row < SINK) | (row >= total - WIN))
    in_window = (column >= win_at) & (column < end) & (old | taken)
    in_sink = (column >= sink_at) & (column < win_at) & (row < SINK) & (row < prefix) & (start > 0)
    seen = jnp.where(in_window | in_sink, 0.0, NEG_FILL)
    mask_ref[...] = jnp.broadcast_to(seen, mask_ref.shape)

    down, across = iota((new, new), 0), iota((new, new), 1)
    eye = (down == across).astype(F32)
    back = eye + (down == parents_ref[...]).astype(F32)
    for _ in range((new - 1).bit_length()):
        half = back.astype(BF16)
        back = jnp.minimum(dot(half, half), 1.0)
    reach = dot_first(back.astype(BF16), eye.astype(BF16))
    tree = (kind_ref[0] == 1).astype(F32)
    causal = (across <= down).astype(F32)
    allowed = tree * reach + (1.0 - tree) * causal
    mask_ref[:, 0:new] = jnp.where(allowed > 0.5, 0.0, NEG_FILL)
    depth = tree * (jnp.sum(reach, axis=1, keepdims=True) - 1.0)
    depth = depth + (1.0 - tree) * iota((new, 1), 0).astype(F32)
    angle = (total.astype(F32) + depth) * freq_ref[...]
    lane = iota(angle.shape, 1)
    cosine, sine = jnp.cos(angle), jnp.sin(angle)
    sine = jnp.where(lane < head // 2, -sine, sine)
    for which, gain_ref in enumerate((q_gain_ref, k_gain_ref)):
        gain = jnp.broadcast_to(gain_ref[...], angle.shape)
        if which == 0:
            gain = gain * (head ** (-0.5) * LOG2E)
        rot_ref[2 * which] = cosine * gain
        rot_ref[2 * which + 1] = sine * pltpu.roll(gain, head // 2, 1)
    for copy in copies:
        copy.wait()


def route_kernel(per, new, n_weights, *refs):
    small_in = refs[1:3]
    sources = refs[3 : 3 + n_weights]
    refs = refs[3 + n_weights :]
    pick_ref, combine_ref, weight_ref = refs[:3]
    targets = refs[3 : 3 + n_weights]
    ids_ref, gates_ref, hit_ref, rank_ref, own_ref, sems = refs[3 + n_weights :]
    sources, targets = (*small_in, *sources), (ids_ref, gates_ref, *targets)
    copies = [
        pltpu.make_async_copy(source, target, sems.at[which])
        for which, (source, target) in enumerate(zip(sources, targets))
    ]
    for copy in copies:
        copy.start()
    for copy in copies[:2]:
        copy.wait()

    me = lax.axis_index("tensor")
    all_tokens = ids_ref.shape[1]
    devices = hit_ref.shape[0]
    chips = devices // 2
    tokens = chips * new
    slot = iota((all_tokens, tokens), 1) // new
    source = (me ^ (2 * slot + ((slot >> 1) & 1))) * new + iota((all_tokens, tokens), 1) % new
    order = (iota((all_tokens, tokens), 0) == source).astype(F32)
    ids = dot(ids_ref[...].astype(F32).astype(BF16), order.astype(BF16))
    gates = lax.dot_general(
        gates_ref[...],
        order,
        (((1,), (0,)), ((), ())),
        precision=lax.Precision.HIGHEST,
        preferred_element_type=F32,
    )
    for rel in range(devices):
        expert = (me ^ step(rel // 2) ^ (rel % 2)).astype(F32)
        named = (ids == expert).astype(F32)
        hit_ref[rel : rel + 1, :] = jnp.max(named, axis=0, keepdims=True)
    before, later = iota((tokens, tokens), 0), iota((tokens, tokens), 1)
    earlier = (before < later) & (before // new == later // new)
    rank_ref[...] = dot(hit_ref[...].astype(BF16), earlier.astype(F32).astype(BF16))
    rows = chips * per
    slot_of = iota((rows, tokens), 1) // new
    row_slot = iota((rows, tokens), 0) // per
    row_rank = (iota((rows, tokens), 0) % per).astype(F32)
    in_first = iota((1, tokens), 1) < new
    for rel in range(devices):
        hit = hit_ref[rel : rel + 1, :] > 0.5
        rank = rank_ref[rel : rel + 1, :]
        chosen = (slot_of == (row_slot ^ (rel // 2))) & hit & (rank == row_rank)
        pick_ref[rel * rows : (rel + 1) * rows, :] = chosen.astype(F32)
        if rel < 2:
            named = ids == (me ^ rel).astype(F32)
            weight = jnp.sum(jnp.where(named, gates, 0.0), axis=0, keepdims=True)
            weight = jnp.sum(jnp.where(chosen, weight, 0.0), axis=1, keepdims=True)
            weight_ref[rel * rows : (rel + 1) * rows, :] = jnp.broadcast_to(
                weight, (rows, weight_ref.shape[1])
            )
        for place in range(per):
            at = rel * per + place
            own_ref[at : at + 1, :] = (in_first & hit & (rank == float(place))).astype(F32)
    first = (iota((tokens, new), 0) == iota((tokens, new), 1)).astype(F32)
    combine_ref[...] = lax.dot_general(
        first.astype(BF16),
        own_ref[...].astype(BF16),
        (((0,), (1,)), ((), ())),
        preferred_element_type=F32,
    )
    for copy in copies[2:]:
        copy.wait()


def project_kernel(count, *refs):
    blocks = refs[:count]
    gain_ref, wq_ref, wkv_ref, wq_sib, wkv_sib = refs[count : count + 5]
    outs = refs[count + 5 :]
    rows = blocks[0].shape[0]
    gain = gain_ref[...]
    values = [(norm_rows(block[...].astype(F32)) * gain).astype(BF16) for block in blocks]
    values = jnp.concatenate(values, axis=0)

    def put(result, at):
        result = result.astype(BF16)
        for j in range(count):
            outs[j][:, at : at + result.shape[1]] = result[j * rows : (j + 1) * rows]

    wide, narrow = wq_ref.shape[1], wkv_ref.shape[0]
    put(dot(values, wq_ref[...]), 0)
    put(dot(values, wq_sib[...]), wide)
    put(dot_last(values, wkv_ref[...]), 2 * wide)
    put(dot_last(values, wkv_sib[...]), 2 * wide + narrow)


def attend_kernel(chips, q_width, kv_ready, *refs):
    got = refs[:chips]
    at = chips + 1 if kv_ready else chips
    keys_ref, values_ref, mask_ref, rot_ref = refs[at : at + 4]
    outs = refs[at + 5 : at + 5 + chips]
    fresh_ref = refs[chips] if kv_ready else refs[-1]
    me = lax.axis_index("tensor")
    chip = me // 2
    new = got[0].shape[0]
    kv_heads, span, head = keys_ref.shape
    per_chip = 2 * q_width // head
    group = chips * per_chip // kv_heads

    if not kv_ready:
        for rel in range(2 * chips):
            left = 2 * q_width + (rel % 2) * head
            fresh_ref[step(rel // 2) ^ (rel % 2)] = got[rel // 2][:, left : left + head]

    def rope(values, which):
        values = norm_rows(values.astype(F32))
        turned = pltpu.roll(values, head // 2, 1)
        return (values * rot_ref[2 * which] + turned * rot_ref[2 * which + 1]).astype(BF16)

    ones = jnp.ones((span, head), BF16)
    for j in range(chips):
        kv = (chip ^ j) * per_chip // group
        key_at, value_at = kv, kv + kv_heads
        if not kv_ready:
            key_at, value_at = me ^ key_at, me ^ value_at
        keys = jnp.concatenate([rope(fresh_ref[key_at], 1), keys_ref[kv, new:span]], axis=0)
        values = jnp.concatenate([fresh_ref[value_at], values_ref[kv, new:span]], axis=0)
        query = jnp.concatenate(
            [rope(got[j][:, h * head : (h + 1) * head], 0) for h in range(per_chip)], axis=0
        )
        score = dot_last(query, keys).reshape(per_chip, new, span) + mask_ref[...][None]
        expo = jnp.exp2(score - jnp.max(score, axis=-1, keepdims=True))
        expo = expo.astype(BF16).reshape(per_chip * new, span)
        result = (dot(expo, values) / dot(expo, ones)).astype(BF16)
        for h in range(per_chip):
            outs[j][:, h * head : (h + 1) * head] = result[h * new : (h + 1) * new]


def spread_kernel(chips, picks, *refs):
    got = refs[:chips]
    w_ref, w_sib = refs[chips : chips + 2]
    outs = refs[-chips:]
    depth, width = w_ref.shape
    left = jnp.concatenate([got[j][...] for j in range(chips)], axis=0)
    if picks:
        left = dot(refs[chips + 2][...].astype(BF16), left).astype(BF16)
    each = left.shape[0] // chips
    tile = min(512, width)
    for at in range(0, width, tile):
        part = dot(left[:, :depth], w_ref[:, at : at + tile])
        part = (part + dot(left[:, depth:], w_sib[:, at : at + tile])).astype(BF16)
        for j in range(chips):
            outs[j][:, at : at + tile] = part[j * each : (j + 1) * each]


def select_kernel(chips, *refs):
    blocks = refs[:chips]
    pick_ref, _ = refs[chips : chips + 2]
    sources = refs[chips + 2 : chips + 4]
    picked_ref = refs[chips + 4]
    targets = refs[chips + 5 : chips + 7]
    sems = refs[-1]
    copies = [
        pltpu.make_async_copy(source, target, sems.at[which])
        for which, (source, target) in enumerate(zip(sources, targets))
    ]
    for copy in copies:
        copy.start()
    values = jnp.concatenate([block[...] for block in blocks], axis=0)
    pick = pick_ref[0 : picked_ref.shape[0], :].astype(BF16)
    picked_ref[...] = dot(pick, values)
    for copy in copies:
        copy.wait()


def hidden_kernel(chips, *refs):
    got = refs[:chips]
    own_ref, out_ref = refs[chips:]
    total = own_ref[...].astype(F32)
    for j in range(chips):
        total = total + got[j][...].astype(F32)
    out_ref[...] = total


def rows_kernel(chips, *refs):
    got = refs[:chips]
    picked_ref, gain_ref, _, own_ref, other_ref = refs[chips:]
    hidden = picked_ref[...]
    for j in range(chips):
        hidden = hidden + got[j][...].astype(F32)
    normed = (norm_rows(hidden) * gain_ref[...]).astype(BF16)
    half = own_ref.shape[0]
    own_ref[...] = normed[:half]
    other_ref[...] = normed[half:]


def expert_kernel(own_ref, other_ref, gate_ref, up_ref, down_ref, own_out, other_out):
    left = jnp.concatenate([own_ref[...].astype(F32), other_ref[...].astype(F32)], axis=0)
    left = left.astype(BF16)
    gate = dot_last(left, gate_ref[0])
    up = dot_last(left, up_ref[0])
    inner = (gate / (1.0 + jnp.exp(-gate)) * up).astype(BF16)
    result = dot(inner, down_ref[0])
    half = own_ref.shape[0]
    own_out[...] = result[:half]
    other_out[...] = result[half:].astype(BF16)


def pack_kernel(chips, per, own_ref, other_ref, weight_ref, *outs):
    half = own_ref.shape[0]
    own = own_ref[...] * weight_ref[:half, 0:1]
    other = other_ref[...].astype(F32) * weight_ref[half:, 0:1]
    for j in range(chips):
        at = slice(j * per, (j + 1) * per)
        outs[j][...] = jnp.concatenate([own[at], other[at]], axis=0).astype(BF16)


def combine_kernel(chips, *refs):
    hidden_ref, combine_ref = refs[:2]
    got = refs[2 : 2 + chips]
    out_ref = refs[2 + chips]
    rows = jnp.concatenate([block[...].astype(F32) for block in got], axis=0)
    moe = dot(combine_ref[...].astype(BF16), rows.astype(BF16))
    out_ref[...] = (hidden_ref[...] + moe).astype(BF16)


def body(
    residual_in,
    attn_gain,
    w_query,
    w_keyval,
    query_gain,
    key_gain,
    w_out,
    ffn_gain,
    w_gate,
    w_up,
    w_down,
    key_cache,
    value_cache,
    prefix_lens,
    accepted,
    accept_path,
    parents,
    slot_kinds,
    expert_ids,
    gate_probs,
):
    devices = lax.axis_size("tensor")
    chips = devices // 2
    new, width = residual_in.shape
    head = query_gain.shape[0]
    kv_heads = key_cache.shape[2] // head
    q_width = w_query.shape[1]
    new_width = w_keyval.shape[0]
    all_tokens, top = expert_ids.shape
    tokens = chips * new
    per = new * top // EXPERTS
    path_len = accept_path.shape[1]
    rows = 2 * chips * per
    assert key_cache.shape[0] == 1 and w_gate.shape[0] == 1
    assert devices & (devices - 1) == 0
    vmem, smem, hbm, anywhere = pltpu.VMEM, pltpu.SMEM, pltpu.HBM, pl.ANY

    blocks = exchange([residual_in] * chips)
    wq_sib = hop(w_query, 1)
    wkv_sib = hop(w_keyval, 1)

    freq = ROPE_BASE ** (-2.0 * np.arange(head // 2) / head)
    freq = jnp.asarray(np.concatenate([freq, freq])[None, :], F32)
    span = -(-(new + 16 + window_rows(path_len)) // 128) * 128
    weights = [attn_gain[None, :], w_query, w_keyval]
    keys, values, mask, rot, gain, wq, wkv = call(
        functools.partial(prep_kernel, path_len, len(weights)),
        "prep",
        [
            in_vmem((kv_heads, span, head), BF16),
            in_vmem((kv_heads, span, head), BF16),
            in_vmem((new, span), F32),
            in_vmem((4, new, head), F32),
        ]
        + [in_vmem(w.shape, w.dtype) for w in weights],
        [
            (key_cache, hbm),
            (value_cache, hbm),
            (prefix_lens, smem),
            (accepted, smem),
            (slot_kinds, smem),
            (accept_path, hbm),
            (parents, hbm),
            (freq, hbm),
            (query_gain[None, :], hbm),
            (key_gain[None, :], hbm),
        ]
        + [(w, hbm) for w in weights],
        [
            pltpu.SMEM((1, path_len), jnp.int32),
            pltpu.VMEM((1, new), jnp.int32),
            pltpu.VMEM((1, head), F32),
            pltpu.VMEM((1, head), F32),
            pltpu.VMEM((1, head), F32),
            pltpu.SemaphoreType.DMA((5,)),
            pltpu.SemaphoreType.DMA((2, kv_heads, 2)),
            pltpu.SemaphoreType.DMA((len(weights),)),
        ],
        limit=16,
        moved=4 * span * kv_heads * head * 2,
    )

    projected = call(
        functools.partial(project_kernel, chips),
        "project",
        [in_vmem((new, 2 * (q_width + new_width)), BF16)] * chips,
        [(block, vmem) for block in blocks]
        + [(w, vmem) for w in (gain, wq, wkv, wq_sib, wkv_sib)],
        limit=16,
        flops=4 * tokens * width * (q_width + new_width),
        moved=4 * width * (q_width + new_width),
    )
    got = exchange(projected)

    weights = [ffn_gain[None, :], w_out, w_down]
    pick, combine, weight, ffn, wo, wd = call(
        functools.partial(route_kernel, per, new, len(weights)),
        "route",
        [
            in_vmem((chips * rows, tokens), F32),
            in_vmem((new, devices * per), F32),
            in_vmem((rows, 128), F32),
        ]
        + [in_vmem(w.shape, w.dtype) for w in weights],
        [(projected[0], anywhere), (expert_ids.T, hbm), (gate_probs.T, hbm)]
        + [(w, hbm) for w in weights],
        [
            pltpu.VMEM((top, all_tokens), jnp.int32),
            pltpu.VMEM((top, all_tokens), F32),
            pltpu.VMEM((devices, tokens), F32),
            pltpu.VMEM((devices, tokens), F32),
            pltpu.VMEM((devices * per, tokens), F32),
            pltpu.SemaphoreType.DMA((2 + len(weights),)),
        ],
        limit=16,
        moved=4 * width * (q_width + w_down.shape[1]),
    )
    kv_ready = []
    if new_width != head:
        pieces = [None] * devices
        for rel in range(devices):
            left = 2 * q_width + (rel % 2) * new_width
            pieces[step(rel // 2) ^ (rel % 2)] = got[rel // 2][:, left : left + new_width]
        pieces = jnp.stack(pieces)[lax.axis_index("tensor") ^ jnp.arange(devices)]
        pieces = pieces.transpose(1, 0, 2).reshape(new, 2 * kv_heads, head)
        kv_ready = [(pieces.transpose(1, 0, 2), vmem)]
    *attended, wo = call(
        functools.partial(attend_kernel, chips, q_width, bool(kv_ready)),
        "attend",
        [in_vmem((new, 2 * q_width), BF16)] * chips + [in_vmem(wo.shape, wo.dtype)],
        [(block, vmem) for block in got]
        + kv_ready
        + [(keys, vmem), (values, vmem), (mask, vmem), (rot, vmem)]
        + [(wo, vmem)],
        [] if kv_ready else [pltpu.VMEM((devices, new, head), BF16)],
        limit=16,
        same={chips + len(kv_ready) + 4: chips},
        flops=8 * new * chips * q_width * span,
        moved=4 * span * kv_heads * head,
    )
    wo_sib = hop(wo, 1)
    heads = exchange(attended)
    picked, wg, wu = call(
        functools.partial(select_kernel, chips),
        "select",
        [in_vmem((rows, width), F32)] + [in_vmem(w.shape, w.dtype) for w in (w_gate, w_up)],
        [(block, vmem) for block in blocks]
        + [(pick, vmem), (attended[0], anywhere), (w_gate, hbm), (w_up, hbm)],
        [pltpu.SemaphoreType.DMA((2,))],
        limit=8,
        flops=2 * rows * width * tokens,
        moved=8 * width * w_gate.shape[1],
    )

    def spread(name, each, more):
        return call(
            functools.partial(spread_kernel, chips, name == "experts"),
            name,
            [in_vmem((each, width), BF16)] * chips,
            [(block, vmem) for block in heads] + [(wo, vmem), (wo_sib, vmem)] + more,
            limit=16,
            flops=4 * chips * each * width * q_width,
            moved=4 * q_width * width,
        )

    partial = spread("experts", rows, [(pick, vmem), (wg, anywhere)])
    for_experts = exchange(partial)
    partial = spread("slots", new, [(partial[0], anywhere)])
    for_slots = exchange(partial)

    own, other = call(
        functools.partial(rows_kernel, chips),
        "rows",
        [in_vmem((rows // 2, width), BF16)] * 2,
        [(block, vmem) for block in for_experts]
        + [(picked, vmem), (ffn, vmem), (partial[0], anywhere)],
        limit=8,
        moved=2 * chips * rows * width,
    )
    own_out, other_out = call(
        expert_kernel,
        "expert",
        [in_vmem((rows // 2, width), F32), in_vmem((rows // 2, width), BF16)],
        [(own, vmem), (hop(other, 1), vmem), (wg, vmem), (wu, vmem), (wd, vmem)],
        limit=16,
        flops=6 * rows * width * w_gate.shape[1],
        moved=6 * width * w_gate.shape[1],
    )
    results = call(
        functools.partial(pack_kernel, chips, per),
        "pack",
        [in_vmem((2 * per, width), BF16)] * chips,
        [(own_out, vmem), (hop(other_out, 1), vmem), (weight, vmem)],
        limit=8,
        moved=4 * rows * width,
    )
    returned = exchange(results)
    hidden = call(
        functools.partial(hidden_kernel, chips),
        "hidden",
        [in_vmem((new, width), F32)],
        [(block, vmem) for block in for_slots] + [(residual_in, vmem)],
        limit=8,
        moved=2 * chips * new * width,
    )[0]
    return call(
        functools.partial(combine_kernel, chips),
        "combine",
        [jax.ShapeDtypeStruct((new, width), BF16)],
        [(hidden, vmem), (combine, vmem)] + [(block, vmem) for block in returned],
        limit=8,
        moved=6 * new * width,
    )[0]


def solution(mesh):
    in_specs = (
        P(("group", "tensor"), None),
        P(),
        P(None, "tensor"),
        P("tensor", None),
        P(),
        P(),
        P("tensor", None),
        P(),
        P("tensor", None, None),
        P("tensor", None, None),
        P("tensor", None, None),
        P(("group", "tensor"), None, None),
        P(("group", "tensor"), None, None),
        P(("group", "tensor")),
        P(("group", "tensor")),
        P(("group", "tensor"), None),
        P(("group", "tensor"), None),
        P(("group", "tensor")),
        P("group", None),
        P("group", None),
    )
    out_specs = P(("group", "tensor"), None)
    return jax.shard_map(body, mesh=mesh, in_specs=in_specs, out_specs=out_specs, check_vma=False)
```

```python
import functools
import math

import jax
import jax.numpy as jnp
import numpy as np
from jax import lax
from jax.experimental import pallas as pl
from jax.experimental.pallas import tpu as pltpu
from jax.sharding import PartitionSpec as P

EXPERTS = 128
SINK = 4
WIN = 512

EPSILON = 1e-06
NEG_FILL = -1e30
ROPE_BASE = 1000000.0
LOG2E = math.log2(math.e)
F32 = jnp.float32
BF16 = jnp.bfloat16
MIB = 1 << 20


def step(j):
    return 2 * j + j % 2


def iota(shape, dim):
    return lax.broadcasted_iota(jnp.int32, shape, dim)


def dot(left, right):
    return jnp.dot(left, right, preferred_element_type=F32)


def dot_last(left, right):
    return lax.dot_general(left, right, (((1,), (1,)), ((), ())), preferred_element_type=F32)


def dot_first(left, right):
    return lax.dot_general(left, right, (((0,), (0,)), ((), ())), preferred_element_type=F32)


def norm_rows(values):
    return values * lax.rsqrt(jnp.mean(values * values, axis=-1, keepdims=True) + EPSILON)


def in_vmem(shape, dtype):
    return pltpu.VMEM(shape, dtype)


def call(kernel, name, outs, args, scratch=(), limit=16, flops=0, moved=0, same=None):
    arrays = []
    specs = []
    for array, space in args:
        if space is pltpu.HBM or space is pltpu.VMEM:
            array = pltpu.with_memory_space_constraint(array, space)
        arrays.append(array)
        specs.append(pl.BlockSpec(memory_space=space))
    return pl.pallas_call(
        kernel,
        out_shape=outs,
        in_specs=specs,
        out_specs=[pl.BlockSpec(memory_space=pltpu.VMEM) for _ in outs],
        scratch_shapes=list(scratch),
        input_output_aliases=same or {},
        compiler_params=pltpu.CompilerParams(vmem_limit_bytes=limit * MIB),
        cost_estimate=pl.CostEstimate(flops=flops, bytes_accessed=moved, transcendentals=0),
        name=name,
    )(*arrays)


def hop(value, step):
    devices = lax.axis_size("tensor")
    return lax.ppermute(value, "tensor", [(i, i ^ step) for i in range(devices)])


def exchange(blocks):
    return [blocks[0]] + [hop(blocks[j], step(j)) for j in range(1, len(blocks))]


def window_rows(path_len):
    return -(-(WIN + 2 * (path_len - 1) + 16) // 16) * 16


def prep_kernel(path_len, n_weights, *refs):
    key_cache, value_cache, prefix_ref, accepted_ref, kind_ref = refs[:5]
    small_in = refs[5:10]
    sources = refs[10 : 10 + n_weights]
    refs = refs[10 + n_weights :]
    keys_ref, values_ref, mask_ref, rot_ref = refs[:4]
    targets = refs[4 : 4 + n_weights]
    refs = refs[4 + n_weights :]
    path_ref, parents_ref, freq_ref, q_gain_ref, k_gain_ref = refs[:5]
    small_sems, cache_sems, weight_sems = refs[5:]

    new = mask_ref.shape[0]
    kv_heads, span, head = keys_ref.shape
    cache_len = key_cache.shape[1]
    wide = window_rows(path_len)
    sink_at, win_at = new, new + 16
    end = win_at + wide

    small = [
        pltpu.make_async_copy(source, target, small_sems.at[which])
        for which, (source, target) in enumerate(zip(small_in, refs[:5]))
    ]
    for copy in small:
        copy.start()
    copies = [
        pltpu.make_async_copy(source, target, weight_sems.at[which])
        for which, (source, target) in enumerate(zip(sources, targets))
    ]
    prefix = prefix_ref[0]
    accepted = accepted_ref[0]
    total = prefix + accepted
    low = jnp.maximum(total - WIN, 0)
    start = pl.multiple_of(jnp.minimum((low // 16) * 16, cache_len - wide), 16)
    for which, (cache, buf) in enumerate(((key_cache, keys_ref), (value_cache, values_ref))):
        for kv in range(kv_heads):
            cols = pl.ds(kv * head, head)
            copies.append(
                pltpu.make_async_copy(
                    cache.at[0, pl.ds(start, wide), cols],
                    buf.at[kv, pl.ds(win_at, wide)],
                    cache_sems.at[which, kv, 0],
                )
            )
            copies.append(
                pltpu.make_async_copy(
                    cache.at[0, pl.ds(0, 16), cols],
                    buf.at[kv, pl.ds(sink_at, 16)],
                    cache_sems.at[which, kv, 1],
                )
            )
    for copy in copies:
        copy.start()

    for buf in (keys_ref, values_ref):
        buf[:, 0:new, :] = jnp.zeros((kv_heads, new, head), BF16)
        buf[:, end:span, :] = jnp.zeros((kv_heads, span - end, head), BF16)

    for copy in small:
        copy.wait()
    column = iota((1, span), 1)
    row = jnp.where(column < win_at, column - sink_at, start + column - win_at)
    taken = jnp.zeros((1, span), jnp.bool_)
    for step in range(path_len):
        at = prefix + path_ref[0, step]
        taken = taken | ((row == at) & (step < accepted))
    old = (row < prefix) & ((row < SINK) | (row >= total - WIN))
    in_window = (column >= win_at) & (column < end) & (old | taken)
    in_sink = (column >= sink_at) & (column < win_at) & (row < SINK) & (row < prefix) & (start > 0)
    seen = jnp.where(in_window | in_sink, 0.0, NEG_FILL)
    mask_ref[...] = jnp.broadcast_to(seen, mask_ref.shape)

    down, across = iota((new, new), 0), iota((new, new), 1)
    eye = (down == across).astype(F32)
    back = eye + (down == parents_ref[...]).astype(F32)
    for _ in range((new - 1).bit_length()):
        half = back.astype(BF16)
        back = jnp.minimum(dot(half, half), 1.0)
    reach = dot_first(back.astype(BF16), eye.astype(BF16))
    tree = (kind_ref[0] == 1).astype(F32)
    causal = (across <= down).astype(F32)
    allowed = tree * reach + (1.0 - tree) * causal
    mask_ref[:, 0:new] = jnp.where(allowed > 0.5, 0.0, NEG_FILL)
    depth = tree * (jnp.sum(reach, axis=1, keepdims=True) - 1.0)
    depth = depth + (1.0 - tree) * iota((new, 1), 0).astype(F32)
    angle = (total.astype(F32) + depth) * freq_ref[...]
    lane = iota(angle.shape, 1)
    cosine, sine = jnp.cos(angle), jnp.sin(angle)
    sine = jnp.where(lane < head // 2, -sine, sine)
    for which, gain_ref in enumerate((q_gain_ref, k_gain_ref)):
        gain = jnp.broadcast_to(gain_ref[...], angle.shape)
        if which == 0:
            gain = gain * (head ** (-0.5) * LOG2E)
        rot_ref[2 * which] = cosine * gain
        rot_ref[2 * which + 1] = sine * pltpu.roll(gain, head // 2, 1)
    for copy in copies:
        copy.wait()


def route_kernel(per, new, n_weights, *refs):
    small_in = refs[1:3]
    sources = refs[3 : 3 + n_weights]
    refs = refs[3 + n_weights :]
    pick_ref, combine_ref, weight_ref = refs[:3]
    targets = refs[3 : 3 + n_weights]
    ids_ref, gates_ref, hit_ref, rank_ref, own_ref, sems = refs[3 + n_weights :]
    sources, targets = (*small_in, *sources), (ids_ref, gates_ref, *targets)
    copies = [
        pltpu.make_async_copy(source, target, sems.at[which])
        for which, (source, target) in enumerate(zip(sources, targets))
    ]
    for copy in copies:
        copy.start()
    for copy in copies[:2]:
        copy.wait()

    me = lax.axis_index("tensor")
    all_tokens = ids_ref.shape[1]
    devices = hit_ref.shape[0]
    chips = devices // 2
    tokens = chips * new
    slot = iota((all_tokens, tokens), 1) // new
    source = (me ^ (2 * slot + (slot & 1))) * new + iota((all_tokens, tokens), 1) % new
    order = (iota((all_tokens, tokens), 0) == source).astype(F32)
    ids = dot(ids_ref[...].astype(F32).astype(BF16), order.astype(BF16))
    gates = lax.dot_general(
        gates_ref[...],
        order,
        (((1,), (0,)), ((), ())),
        precision=lax.Precision.HIGHEST,
        preferred_element_type=F32,
    )
    for rel in range(devices):
        expert = (me ^ step(rel // 2) ^ (rel % 2)).astype(F32)
        named = (ids == expert).astype(F32)
        hit_ref[rel : rel + 1, :] = jnp.max(named, axis=0, keepdims=True)
    before, later = iota((tokens, tokens), 0), iota((tokens, tokens), 1)
    earlier = (before < later) & (before // new == later // new)
    rank_ref[...] = dot(hit_ref[...].astype(BF16), earlier.astype(F32).astype(BF16))
    rows = chips * per
    slot_of = iota((rows, tokens), 1) // new
    row_slot = iota((rows, tokens), 0) // per
    row_rank = (iota((rows, tokens), 0) % per).astype(F32)
    in_first = iota((1, tokens), 1) < new
    for rel in range(devices):
        hit = hit_ref[rel : rel + 1, :] > 0.5
        rank = rank_ref[rel : rel + 1, :]
        chosen = (slot_of == (row_slot ^ (rel // 2))) & hit & (rank == row_rank)
        pick_ref[rel * rows : (rel + 1) * rows, :] = chosen.astype(F32)
        if rel < 2:
            named = ids == (me ^ rel).astype(F32)
            weight = jnp.sum(jnp.where(named, gates, 0.0), axis=0, keepdims=True)
            weight = jnp.sum(jnp.where(chosen, weight, 0.0), axis=1, keepdims=True)
            weight_ref[rel * rows : (rel + 1) * rows, :] = jnp.broadcast_to(
                weight, (rows, weight_ref.shape[1])
            )
        for place in range(per):
            at = rel * per + place
            own_ref[at : at + 1, :] = (in_first & hit & (rank == float(place))).astype(F32)
    first = (iota((tokens, new), 0) == iota((tokens, new), 1)).astype(F32)
    combine_ref[...] = lax.dot_general(
        first.astype(BF16),
        own_ref[...].astype(BF16),
        (((0,), (1,)), ((), ())),
        preferred_element_type=F32,
    )
    for copy in copies[2:]:
        copy.wait()


def project_kernel(count, *refs):
    blocks = refs[:count]
    gain_ref, wq_ref, wkv_ref, wq_sib, wkv_sib = refs[count : count + 5]
    outs = refs[count + 5 :]
    rows = blocks[0].shape[0]
    gain = gain_ref[...]
    values = [(norm_rows(block[...].astype(F32)) * gain).astype(BF16) for block in blocks]
    values = jnp.concatenate(values, axis=0)

    def put(result, at):
        result = result.astype(BF16)
        for j in range(count):
            outs[j][:, at : at + result.shape[1]] = result[j * rows : (j + 1) * rows]

    wide, narrow = wq_ref.shape[1], wkv_ref.shape[0]
    put(dot(values, wq_ref[...]), 0)
    put(dot(values, wq_sib[...]), wide)
    put(dot_last(values, wkv_ref[...]), 2 * wide)
    put(dot_last(values, wkv_sib[...]), 2 * wide + narrow)


def attend_kernel(chips, q_width, kv_ready, *refs):
    got = refs[:chips]
    at = chips + 1 if kv_ready else chips
    keys_ref, values_ref, mask_ref, rot_ref = refs[at : at + 4]
    outs = refs[at + 5 : at + 5 + chips]
    fresh_ref = refs[chips] if kv_ready else refs[-1]
    me = lax.axis_index("tensor")
    chip = me // 2
    new = got[0].shape[0]
    kv_heads, span, head = keys_ref.shape
    per_chip = 2 * q_width // head
    group = chips * per_chip // kv_heads

    if not kv_ready:
        for rel in range(2 * chips):
            left = 2 * q_width + (rel % 2) * head
            fresh_ref[step(rel // 2) ^ (rel % 2)] = got[rel // 2][:, left : left + head]

    def rope(values, which):
        values = norm_rows(values.astype(F32))
        turned = pltpu.roll(values, head // 2, 1)
        return (values * rot_ref[2 * which] + turned * rot_ref[2 * which + 1]).astype(BF16)

    for j in range(chips):
        kv = (chip ^ j) * per_chip // group
        key_at, value_at = kv, kv + kv_heads
        if not kv_ready:
            key_at, value_at = me ^ key_at, me ^ value_at
        keys = jnp.concatenate([rope(fresh_ref[key_at], 1), keys_ref[kv, new:span]], axis=0)
        values = jnp.concatenate([fresh_ref[value_at], values_ref[kv, new:span]], axis=0)
        query = jnp.concatenate(
            [rope(got[j][:, h * head : (h + 1) * head], 0) for h in range(per_chip)], axis=0
        )
        score = dot_last(query, keys).reshape(per_chip, new, span) + mask_ref[...][None]
        expo = jnp.exp2(score - jnp.max(score, axis=-1, keepdims=True))
        denom = jnp.sum(expo, axis=-1, keepdims=True).reshape(per_chip * new, 1)
        expo = expo.astype(BF16).reshape(per_chip * new, span)
        result = (dot(expo, values) / denom).astype(BF16)
        for h in range(per_chip):
            outs[j][:, h * head : (h + 1) * head] = result[h * new : (h + 1) * new]


def spread_kernel(chips, picks, *refs):
    got = refs[:chips]
    w_ref, w_sib = refs[chips : chips + 2]
    outs = refs[-chips:]
    depth, width = w_ref.shape
    left = jnp.concatenate([got[j][...] for j in range(chips)], axis=0)
    if picks:
        left = dot(refs[chips + 2][...].astype(BF16), left).astype(BF16)
    each = left.shape[0] // chips
    tile = min(512, width)
    for at in range(0, width, tile):
        part = dot(left[:, :depth], w_ref[:, at : at + tile])
        part = (part + dot(left[:, depth:], w_sib[:, at : at + tile])).astype(BF16)
        for j in range(chips):
            outs[j][:, at : at + tile] = part[j * each : (j + 1) * each]


def select_kernel(chips, *refs):
    blocks = refs[:chips]
    pick_ref, _ = refs[chips : chips + 2]
    sources = refs[chips + 2 : chips + 4]
    picked_ref = refs[chips + 4]
    targets = refs[chips + 5 : chips + 7]
    sems = refs[-1]
    copies = [
        pltpu.make_async_copy(source, target, sems.at[which])
        for which, (source, target) in enumerate(zip(sources, targets))
    ]
    for copy in copies:
        copy.start()
    values = jnp.concatenate([block[...] for block in blocks], axis=0)
    pick = pick_ref[0 : picked_ref.shape[0], :].astype(BF16)
    picked_ref[...] = dot(pick, values)
    for copy in copies:
        copy.wait()


def hidden_kernel(chips, *refs):
    got = refs[:chips]
    own_ref, out_ref = refs[chips:]
    total = own_ref[...].astype(F32)
    for j in range(chips):
        total = total + got[j][...].astype(F32)
    out_ref[...] = total


def rows_kernel(chips, *refs):
    got = refs[:chips]
    picked_ref, gain_ref, _, own_ref, other_ref = refs[chips:]
    hidden = picked_ref[...]
    for j in range(chips):
        hidden = hidden + got[j][...].astype(F32)
    normed = (norm_rows(hidden) * gain_ref[...]).astype(BF16)
    half = own_ref.shape[0]
    own_ref[...] = normed[:half]
    other_ref[...] = normed[half:]


def expert_kernel(own_ref, other_ref, gate_ref, up_ref, down_ref, own_out, other_out):
    left = jnp.concatenate([own_ref[...].astype(F32), other_ref[...].astype(F32)], axis=0)
    left = left.astype(BF16)
    gate = dot_last(left, gate_ref[0])
    up = dot_last(left, up_ref[0])
    inner = (gate / (1.0 + jnp.exp(-gate)) * up).astype(BF16)
    result = dot(inner, down_ref[0])
    half = own_ref.shape[0]
    own_out[...] = result[:half]
    other_out[...] = result[half:].astype(BF16)


def pack_kernel(chips, per, own_ref, other_ref, weight_ref, *outs):
    half = own_ref.shape[0]
    own = own_ref[...] * weight_ref[:half, 0:1]
    other = other_ref[...].astype(F32) * weight_ref[half:, 0:1]
    for j in range(chips):
        at = slice(j * per, (j + 1) * per)
        outs[j][...] = jnp.concatenate([own[at], other[at]], axis=0).astype(BF16)


def combine_kernel(chips, *refs):
    hidden_ref, combine_ref = refs[:2]
    got = refs[2 : 2 + chips]
    out_ref = refs[2 + chips]
    rows = jnp.concatenate([block[...].astype(F32) for block in got], axis=0)
    moe = dot(combine_ref[...].astype(BF16), rows.astype(BF16))
    out_ref[...] = (hidden_ref[...] + moe).astype(BF16)


def body(
    residual_in,
    attn_gain,
    w_query,
    w_keyval,
    query_gain,
    key_gain,
    w_out,
    ffn_gain,
    w_gate,
    w_up,
    w_down,
    key_cache,
    value_cache,
    prefix_lens,
    accepted,
    accept_path,
    parents,
    slot_kinds,
    expert_ids,
    gate_probs,
):
    devices = lax.axis_size("tensor")
    chips = devices // 2
    new, width = residual_in.shape
    head = query_gain.shape[0]
    kv_heads = key_cache.shape[2] // head
    q_width = w_query.shape[1]
    new_width = w_keyval.shape[0]
    all_tokens, top = expert_ids.shape
    tokens = chips * new
    per = new * top // EXPERTS
    path_len = accept_path.shape[1]
    rows = 2 * chips * per
    assert key_cache.shape[0] == 1 and w_gate.shape[0] == 1
    assert devices & (devices - 1) == 0
    vmem, smem, hbm, anywhere = pltpu.VMEM, pltpu.SMEM, pltpu.HBM, pl.ANY

    blocks = exchange([residual_in] * chips)
    wq_sib = hop(w_query, 1)
    wkv_sib = hop(w_keyval, 1)

    freq = ROPE_BASE ** (-2.0 * np.arange(head // 2) / head)
    freq = jnp.asarray(np.concatenate([freq, freq])[None, :], F32)
    span = -(-(new + 16 + window_rows(path_len)) // 128) * 128
    weights = [attn_gain[None, :], w_query, w_keyval]
    keys, values, mask, rot, gain, wq, wkv = call(
        functools.partial(prep_kernel, path_len, len(weights)),
        "prep",
        [
            in_vmem((kv_heads, span, head), BF16),
            in_vmem((kv_heads, span, head), BF16),
            in_vmem((new, span), F32),
            in_vmem((4, new, head), F32),
        ]
        + [in_vmem(w.shape, w.dtype) for w in weights],
        [
            (key_cache, hbm),
            (value_cache, hbm),
            (prefix_lens, smem),
            (accepted, smem),
            (slot_kinds, smem),
            (accept_path, hbm),
            (parents, hbm),
            (freq, hbm),
            (query_gain[None, :], hbm),
            (key_gain[None, :], hbm),
        ]
        + [(w, hbm) for w in weights],
        [
            pltpu.SMEM((1, path_len), jnp.int32),
            pltpu.VMEM((1, new), jnp.int32),
            pltpu.VMEM((1, head), F32),
            pltpu.VMEM((1, head), F32),
            pltpu.VMEM((1, head), F32),
            pltpu.SemaphoreType.DMA((5,)),
            pltpu.SemaphoreType.DMA((2, kv_heads, 2)),
            pltpu.SemaphoreType.DMA((len(weights),)),
        ],
        limit=16,
        moved=4 * span * kv_heads * head * 2,
    )

    projected = call(
        functools.partial(project_kernel, chips),
        "project",
        [in_vmem((new, 2 * (q_width + new_width)), BF16)] * chips,
        [(block, vmem) for block in blocks]
        + [(w, vmem) for w in (gain, wq, wkv, wq_sib, wkv_sib)],
        limit=16,
        flops=4 * tokens * width * (q_width + new_width),
        moved=4 * width * (q_width + new_width),
    )
    got = exchange(projected)

    weights = [ffn_gain[None, :], w_out, w_down]
    pick, combine, weight, ffn, wo, wd = call(
        functools.partial(route_kernel, per, new, len(weights)),
        "route",
        [
            in_vmem((chips * rows, tokens), F32),
            in_vmem((new, devices * per), F32),
            in_vmem((rows, 128), F32),
        ]
        + [in_vmem(w.shape, w.dtype) for w in weights],
        [(projected[0], anywhere), (expert_ids.T, hbm), (gate_probs.T, hbm)]
        + [(w, hbm) for w in weights],
        [
            pltpu.VMEM((top, all_tokens), jnp.int32),
            pltpu.VMEM((top, all_tokens), F32),
            pltpu.VMEM((devices, tokens), F32),
            pltpu.VMEM((devices, tokens), F32),
            pltpu.VMEM((devices * per, tokens), F32),
            pltpu.SemaphoreType.DMA((2 + len(weights),)),
        ],
        limit=16,
        moved=4 * width * (q_width + w_down.shape[1]),
    )
    kv_ready = []
    if new_width != head:
        pieces = [None] * devices
        for rel in range(devices):
            left = 2 * q_width + (rel % 2) * new_width
            pieces[step(rel // 2) ^ (rel % 2)] = got[rel // 2][:, left : left + new_width]
        pieces = jnp.stack(pieces)[lax.axis_index("tensor") ^ jnp.arange(devices)]
        pieces = pieces.transpose(1, 0, 2).reshape(new, 2 * kv_heads, head)
        kv_ready = [(pieces.transpose(1, 0, 2), vmem)]
    *attended, wo = call(
        functools.partial(attend_kernel, chips, q_width, bool(kv_ready)),
        "attend",
        [in_vmem((new, 2 * q_width), BF16)] * chips + [in_vmem(wo.shape, wo.dtype)],
        [(block, vmem) for block in got]
        + kv_ready
        + [(keys, vmem), (values, vmem), (mask, vmem), (rot, vmem)]
        + [(wo, vmem)],
        [] if kv_ready else [pltpu.VMEM((devices, new, head), BF16)],
        limit=16,
        same={chips + len(kv_ready) + 4: chips},
        flops=8 * new * chips * q_width * span,
        moved=4 * span * kv_heads * head,
    )
    wo_sib = hop(wo, 1)
    heads = exchange(attended)
    picked, wg, wu = call(
        functools.partial(select_kernel, chips),
        "select",
        [in_vmem((rows, width), F32)] + [in_vmem(w.shape, w.dtype) for w in (w_gate, w_up)],
        [(block, vmem) for block in blocks]
        + [(pick, vmem), (attended[0], anywhere), (w_gate, hbm), (w_up, hbm)],
        [pltpu.SemaphoreType.DMA((2,))],
        limit=8,
        flops=2 * rows * width * tokens,
        moved=8 * width * w_gate.shape[1],
    )

    def spread(name, each, more):
        return call(
            functools.partial(spread_kernel, chips, name == "experts"),
            name,
            [in_vmem((each, width), BF16)] * chips,
            [(block, vmem) for block in heads] + [(wo, vmem), (wo_sib, vmem)] + more,
            limit=16,
            flops=4 * chips * each * width * q_width,
            moved=4 * q_width * width,
        )

    partial = spread("experts", rows, [(pick, vmem), (wg, anywhere)])
    for_experts = exchange(partial)
    partial = spread("slots", new, [(partial[0], anywhere)])
    for_slots = exchange(partial)

    own, other = call(
        functools.partial(rows_kernel, chips),
        "rows",
        [in_vmem((rows // 2, width), BF16)] * 2,
        [(block, vmem) for block in for_experts]
        + [(picked, vmem), (ffn, vmem), (partial[0], anywhere)],
        limit=8,
        moved=2 * chips * rows * width,
    )
    own_out, other_out = call(
        expert_kernel,
        "expert",
        [in_vmem((rows // 2, width), F32), in_vmem((rows // 2, width), BF16)],
        [(own, vmem), (hop(other, 1), vmem), (wg, vmem), (wu, vmem), (wd, vmem)],
        limit=16,
        flops=6 * rows * width * w_gate.shape[1],
        moved=6 * width * w_gate.shape[1],
    )
    results = call(
        functools.partial(pack_kernel, chips, per),
        "pack",
        [in_vmem((2 * per, width), BF16)] * chips,
        [(own_out, vmem), (hop(other_out, 1), vmem), (weight, vmem)],
        limit=8,
        moved=4 * rows * width,
    )
    returned = exchange(results)
    hidden = call(
        functools.partial(hidden_kernel, chips),
        "hidden",
        [in_vmem((new, width), F32)],
        [(block, vmem) for block in for_slots] + [(residual_in, vmem)],
        limit=8,
        moved=2 * chips * new * width,
    )[0]
    return call(
        functools.partial(combine_kernel, chips),
        "combine",
        [jax.ShapeDtypeStruct((new, width), BF16)],
        [(hidden, vmem), (combine, vmem)] + [(block, vmem) for block in returned],
        limit=8,
        moved=6 * new * width,
    )[0]


def solution(mesh):
    in_specs = (
        P(("group", "tensor"), None),
        P(),
        P(None, "tensor"),
        P("tensor", None),
        P(),
        P(),
        P("tensor", None),
        P(),
        P("tensor", None, None),
        P("tensor", None, None),
        P("tensor", None, None),
        P(("group", "tensor"), None, None),
        P(("group", "tensor"), None, None),
        P(("group", "tensor")),
        P(("group", "tensor")),
        P(("group", "tensor"), None),
        P(("group", "tensor"), None),
        P(("group", "tensor")),
        P("group", None),
        P("group", None),
    )
    out_specs = P(("group", "tensor"), None)
    return jax.shard_map(body, mesh=mesh, in_specs=in_specs, out_specs=out_specs, check_vma=False)
```

```python
import functools
import math

import jax
import jax.numpy as jnp
import numpy as np
from jax import lax
from jax.experimental import pallas as pl
from jax.experimental.pallas import tpu as pltpu
from jax.sharding import PartitionSpec as P

EXPERTS = 128
SINK = 4
WIN = 512

EPSILON = 1e-06
NEG_FILL = -1e30
ROPE_BASE = 1000000.0
LOG2E = math.log2(math.e)
F32 = jnp.float32
BF16 = jnp.bfloat16
MIB = 1 << 20


def step(j):
    return 2 * j + (j >> 1) % 2


def iota(shape, dim):
    return lax.broadcasted_iota(jnp.int32, shape, dim)


def dot(left, right):
    return jnp.dot(left, right, preferred_element_type=F32)


def dot_last(left, right):
    return lax.dot_general(left, right, (((1,), (1,)), ((), ())), preferred_element_type=F32)


def dot_first(left, right):
    return lax.dot_general(left, right, (((0,), (0,)), ((), ())), preferred_element_type=F32)


def norm_rows(values):
    return values * lax.rsqrt(jnp.mean(values * values, axis=-1, keepdims=True) + EPSILON)


def in_vmem(shape, dtype):
    return pltpu.VMEM(shape, dtype)


def call(kernel, name, outs, args, scratch=(), limit=16, flops=0, moved=0, same=None):
    arrays = []
    specs = []
    for array, space in args:
        if space is pltpu.HBM or space is pltpu.VMEM:
            array = pltpu.with_memory_space_constraint(array, space)
        arrays.append(array)
        specs.append(pl.BlockSpec(memory_space=space))
    return pl.pallas_call(
        kernel,
        out_shape=outs,
        in_specs=specs,
        out_specs=[pl.BlockSpec(memory_space=pltpu.VMEM) for _ in outs],
        scratch_shapes=list(scratch),
        input_output_aliases=same or {},
        compiler_params=pltpu.CompilerParams(vmem_limit_bytes=limit * MIB),
        cost_estimate=pl.CostEstimate(flops=flops, bytes_accessed=moved, transcendentals=0),
        name=name,
    )(*arrays)


def hop(value, step):
    devices = lax.axis_size("tensor")
    return lax.ppermute(value, "tensor", [(i, i ^ step) for i in range(devices)])


def exchange(blocks):
    return [blocks[0]] + [hop(blocks[j], step(j)) for j in range(1, len(blocks))]


def window_rows(path_len):
    return -(-(WIN + 2 * (path_len - 1) + 16) // 16) * 16


def prep_kernel(path_len, n_weights, *refs):
    key_cache, value_cache, prefix_ref, accepted_ref, kind_ref = refs[:5]
    small_in = refs[5:10]
    sources = refs[10 : 10 + n_weights]
    refs = refs[10 + n_weights :]
    keys_ref, values_ref, mask_ref, rot_ref = refs[:4]
    targets = refs[4 : 4 + n_weights]
    refs = refs[4 + n_weights :]
    path_ref, parents_ref, freq_ref, q_gain_ref, k_gain_ref = refs[:5]
    small_sems, cache_sems, weight_sems = refs[5:]

    new = mask_ref.shape[0]
    kv_heads, span, head = keys_ref.shape
    cache_len = key_cache.shape[1]
    wide = window_rows(path_len)
    sink_at, win_at = new, new + 16
    end = win_at + wide

    small = [
        pltpu.make_async_copy(source, target, small_sems.at[which])
        for which, (source, target) in enumerate(zip(small_in, refs[:5]))
    ]
    for copy in small:
        copy.start()
    copies = [
        pltpu.make_async_copy(source, target, weight_sems.at[which])
        for which, (source, target) in enumerate(zip(sources, targets))
    ]
    prefix = prefix_ref[0]
    accepted = accepted_ref[0]
    total = prefix + accepted
    low = jnp.maximum(total - WIN, 0)
    start = pl.multiple_of(jnp.minimum((low // 16) * 16, cache_len - wide), 16)
    for which, (cache, buf) in enumerate(((key_cache, keys_ref), (value_cache, values_ref))):
        for kv in range(kv_heads):
            cols = pl.ds(kv * head, head)
            copies.append(
                pltpu.make_async_copy(
                    cache.at[0, pl.ds(start, wide), cols],
                    buf.at[kv, pl.ds(win_at, wide)],
                    cache_sems.at[which, kv, 0],
                )
            )
            copies.append(
                pltpu.make_async_copy(
                    cache.at[0, pl.ds(0, 16), cols],
                    buf.at[kv, pl.ds(sink_at, 16)],
                    cache_sems.at[which, kv, 1],
                )
            )
    for copy in copies:
        copy.start()

    for buf in (keys_ref, values_ref):
        buf[:, 0:new, :] = jnp.zeros((kv_heads, new, head), BF16)
        buf[:, end:span, :] = jnp.zeros((kv_heads, span - end, head), BF16)

    for copy in small:
        copy.wait()
    column = iota((1, span), 1)
    row = jnp.where(column < win_at, column - sink_at, start + column - win_at)
    taken = jnp.zeros((1, span), jnp.bool_)
    for step in range(path_len):
        at = prefix + path_ref[0, step]
        taken = taken | ((row == at) & (step < accepted))
    old = (row < prefix) & ((row < SINK) | (row >= total - WIN))
    in_window = (column >= win_at) & (column < end) & (old | taken)
    in_sink = (column >= sink_at) & (column < win_at) & (row < SINK) & (row < prefix) & (start > 0)
    seen = jnp.where(in_window | in_sink, 0.0, NEG_FILL)
    mask_ref[...] = jnp.broadcast_to(seen, mask_ref.shape)

    down, across = iota((new, new), 0), iota((new, new), 1)
    eye = (down == across).astype(F32)
    back = eye + (down == parents_ref[...]).astype(F32)
    for _ in range((new - 1).bit_length()):
        half = back.astype(BF16)
        back = jnp.minimum(dot(half, half), 1.0)
    reach = dot_first(back.astype(BF16), eye.astype(BF16))
    tree = (kind_ref[0] == 1).astype(F32)
    causal = (across <= down).astype(F32)
    allowed = tree * reach + (1.0 - tree) * causal
    mask_ref[:, 0:new] = jnp.where(allowed > 0.5, 0.0, NEG_FILL)
    depth = tree * (jnp.sum(reach, axis=1, keepdims=True) - 1.0)
    depth = depth + (1.0 - tree) * iota((new, 1), 0).astype(F32)
    angle = (total.astype(F32) + depth) * freq_ref[...]
    lane = iota(angle.shape, 1)
    cosine, sine = jnp.cos(angle), jnp.sin(angle)
    sine = jnp.where(lane < head // 2, -sine, sine)
    for which, gain_ref in enumerate((q_gain_ref, k_gain_ref)):
        gain = jnp.broadcast_to(gain_ref[...], angle.shape)
        rot_ref[2 * which] = cosine * gain
        rot_ref[2 * which + 1] = sine * pltpu.roll(gain, head // 2, 1)
    for copy in copies:
        copy.wait()


def route_kernel(per, new, n_weights, *refs):
    small_in = refs[1:3]
    sources = refs[3 : 3 + n_weights]
    refs = refs[3 + n_weights :]
    pick_ref, combine_ref, weight_ref = refs[:3]
    targets = refs[3 : 3 + n_weights]
    ids_ref, gates_ref, hit_ref, rank_ref, own_ref, sems = refs[3 + n_weights :]
    sources, targets = (*small_in, *sources), (ids_ref, gates_ref, *targets)
    copies = [
        pltpu.make_async_copy(source, target, sems.at[which])
        for which, (source, target) in enumerate(zip(sources, targets))
    ]
    for copy in copies:
        copy.start()
    for copy in copies[:2]:
        copy.wait()

    me = lax.axis_index("tensor")
    all_tokens = ids_ref.shape[1]
    devices = hit_ref.shape[0]
    chips = devices // 2
    tokens = chips * new
    slot = iota((all_tokens, tokens), 1) // new
    source = (me ^ (2 * slot + ((slot >> 1) & 1))) * new + iota((all_tokens, tokens), 1) % new
    order = (iota((all_tokens, tokens), 0) == source).astype(F32)
    ids = dot(ids_ref[...].astype(F32).astype(BF16), order.astype(BF16))
    gates = lax.dot_general(
        gates_ref[...],
        order,
        (((1,), (0,)), ((), ())),
        precision=lax.Precision.HIGHEST,
        preferred_element_type=F32,
    )
    for rel in range(devices):
        expert = (me ^ step(rel // 2) ^ (rel % 2)).astype(F32)
        named = (ids == expert).astype(F32)
        hit_ref[rel : rel + 1, :] = jnp.max(named, axis=0, keepdims=True)
    before, later = iota((tokens, tokens), 0), iota((tokens, tokens), 1)
    earlier = (before < later) & (before // new == later // new)
    rank_ref[...] = dot(hit_ref[...].astype(BF16), earlier.astype(F32).astype(BF16))
    rows = chips * per
    slot_of = iota((rows, tokens), 1) // new
    row_slot = iota((rows, tokens), 0) // per
    row_rank = (iota((rows, tokens), 0) % per).astype(F32)
    in_first = iota((1, tokens), 1) < new
    for rel in range(devices):
        hit = hit_ref[rel : rel + 1, :] > 0.5
        rank = rank_ref[rel : rel + 1, :]
        chosen = (slot_of == (row_slot ^ (rel // 2))) & hit & (rank == row_rank)
        pick_ref[rel * rows : (rel + 1) * rows, :] = chosen.astype(F32)
        if rel < 2:
            named = ids == (me ^ rel).astype(F32)
            weight = jnp.sum(jnp.where(named, gates, 0.0), axis=0, keepdims=True)
            weight = jnp.sum(jnp.where(chosen, weight, 0.0), axis=1, keepdims=True)
            weight_ref[rel * rows : (rel + 1) * rows, :] = jnp.broadcast_to(
                weight, (rows, weight_ref.shape[1])
            )
        for place in range(per):
            at = rel * per + place
            own_ref[at : at + 1, :] = (in_first & hit & (rank == float(place))).astype(F32)
    first = (iota((tokens, new), 0) == iota((tokens, new), 1)).astype(F32)
    combine_ref[...] = lax.dot_general(
        first.astype(BF16),
        own_ref[...].astype(BF16),
        (((0,), (1,)), ((), ())),
        preferred_element_type=F32,
    )
    for copy in copies[2:]:
        copy.wait()


def project_kernel(count, *refs):
    blocks = refs[:count]
    gain_ref, wq_ref, wkv_ref, wq_sib, wkv_sib = refs[count : count + 5]
    outs = refs[count + 5 :]
    rows = blocks[0].shape[0]
    gain = gain_ref[...]
    values = [(norm_rows(block[...].astype(F32)) * gain).astype(BF16) for block in blocks]
    values = jnp.concatenate(values, axis=0)

    def put(result, at):
        result = result.astype(BF16)
        for j in range(count):
            outs[j][:, at : at + result.shape[1]] = result[j * rows : (j + 1) * rows]

    wide, narrow = wq_ref.shape[1], wkv_ref.shape[0]
    put(dot(values, wq_ref[...]), 0)
    put(dot(values, wq_sib[...]), wide)
    put(dot_last(values, wkv_ref[...]), 2 * wide)
    put(dot_last(values, wkv_sib[...]), 2 * wide + narrow)


def attend_kernel(chips, q_width, kv_ready, *refs):
    got = refs[:chips]
    at = chips + 1 if kv_ready else chips
    keys_ref, values_ref, mask_ref, rot_ref = refs[at : at + 4]
    outs = refs[at + 5 : at + 5 + chips]
    fresh_ref = refs[chips] if kv_ready else refs[-1]
    me = lax.axis_index("tensor")
    chip = me // 2
    new = got[0].shape[0]
    kv_heads, span, head = keys_ref.shape
    per_chip = 2 * q_width // head
    group = chips * per_chip // kv_heads

    if not kv_ready:
        for rel in range(2 * chips):
            left = 2 * q_width + (rel % 2) * head
            fresh_ref[step(rel // 2) ^ (rel % 2)] = got[rel // 2][:, left : left + head]

    def rope(values, which):
        values = norm_rows(values.astype(F32))
        turned = pltpu.roll(values, head // 2, 1)
        return (values * rot_ref[2 * which] + turned * rot_ref[2 * which + 1]).astype(BF16)

    scale = head ** (-0.5) * LOG2E
    for j in range(chips):
        kv = (chip ^ j) * per_chip // group
        key_at, value_at = kv, kv + kv_heads
        if not kv_ready:
            key_at, value_at = me ^ key_at, me ^ value_at
        keys = jnp.concatenate([rope(fresh_ref[key_at], 1), keys_ref[kv, new:span]], axis=0)
        values = jnp.concatenate([fresh_ref[value_at], values_ref[kv, new:span]], axis=0)
        query = jnp.concatenate(
            [rope(got[j][:, h * head : (h + 1) * head], 0) for h in range(per_chip)], axis=0
        )
        score = dot_last(query, keys) * scale
        score = score.reshape(per_chip, new, span) + mask_ref[...][None]
        expo = jnp.exp2(score - jnp.max(score, axis=-1, keepdims=True))
        denom = jnp.sum(expo, axis=-1, keepdims=True).reshape(per_chip * new, 1)
        expo = expo.astype(BF16).reshape(per_chip * new, span)
        result = (dot(expo, values) / denom).astype(BF16)
        for h in range(per_chip):
            outs[j][:, h * head : (h + 1) * head] = result[h * new : (h + 1) * new]


def spread_kernel(chips, picks, *refs):
    got = refs[:chips]
    w_ref, w_sib = refs[chips : chips + 2]
    outs = refs[-chips:]
    depth, width = w_ref.shape
    left = jnp.concatenate([got[j][...] for j in range(chips)], axis=0)
    if picks:
        left = dot(refs[chips + 2][...].astype(BF16), left).astype(BF16)
    each = left.shape[0] // chips
    tile = min(512, width)
    for at in range(0, width, tile):
        part = dot(left[:, :depth], w_ref[:, at : at + tile])
        part = (part + dot(left[:, depth:], w_sib[:, at : at + tile])).astype(BF16)
        for j in range(chips):
            outs[j][:, at : at + tile] = part[j * each : (j + 1) * each]


def select_kernel(chips, *refs):
    blocks = refs[:chips]
    pick_ref, _ = refs[chips : chips + 2]
    sources = refs[chips + 2 : chips + 4]
    picked_ref = refs[chips + 4]
    targets = refs[chips + 5 : chips + 7]
    sems = refs[-1]
    copies = [
        pltpu.make_async_copy(source, target, sems.at[which])
        for which, (source, target) in enumerate(zip(sources, targets))
    ]
    for copy in copies:
        copy.start()
    values = jnp.concatenate([block[...] for block in blocks], axis=0)
    pick = pick_ref[0 : picked_ref.shape[0], :].astype(BF16)
    picked_ref[...] = dot(pick, values)
    for copy in copies:
        copy.wait()


def hidden_kernel(*refs):
    *got, own_ref, out_ref = refs
    total = own_ref[...].astype(F32)
    for block in got:
        total = total + block[...].astype(F32)
    out_ref[...] = total


def rows_kernel(chips, *refs):
    got = refs[:chips]
    picked_ref, gain_ref, _, own_ref, other_ref = refs[chips:]
    hidden = picked_ref[...]
    for j in range(chips):
        hidden = hidden + got[j][...].astype(F32)
    normed = (norm_rows(hidden) * gain_ref[...]).astype(BF16)
    half = own_ref.shape[0]
    own_ref[...] = normed[:half]
    other_ref[...] = normed[half:]


def expert_kernel(own_ref, other_ref, gate_ref, up_ref, down_ref, own_out, other_out):
    left = jnp.concatenate([own_ref[...].astype(F32), other_ref[...].astype(F32)], axis=0)
    left = left.astype(BF16)
    gate = dot_last(left, gate_ref[0])
    up = dot_last(left, up_ref[0])
    inner = (gate / (1.0 + jnp.exp(-gate)) * up).astype(BF16)
    result = dot(inner, down_ref[0])
    half = own_ref.shape[0]
    own_out[...] = result[:half]
    other_out[...] = result[half:].astype(BF16)


def pack_kernel(chips, per, own_ref, other_ref, weight_ref, slot_ref, *outs):
    half = own_ref.shape[0]
    own = own_ref[...] * weight_ref[:half, 0:1]
    other = other_ref[...].astype(F32) * weight_ref[half:, 0:1]
    for j in range(chips):
        at = slice(j * per, (j + 1) * per)
        rows = jnp.concatenate([own[at], other[at]], axis=0).astype(BF16)
        if j == 1:
            outs[j][: slot_ref.shape[0], :] = slot_ref[...]
            outs[j][slot_ref.shape[0] :, :] = rows
        else:
            outs[j][...] = rows


def combine_kernel(chips, *refs):
    hidden_ref, combine_ref = refs[:2]
    got = refs[2 : 2 + chips]
    out_ref = refs[2 + chips]
    new = out_ref.shape[0]
    rows = [block[new:, :] if j == 1 else block[...] for j, block in enumerate(got)]
    rows = jnp.concatenate([block.astype(F32) for block in rows], axis=0)
    moe = got[1][:new, :].astype(F32) + dot(combine_ref[...].astype(BF16), rows.astype(BF16))
    out_ref[...] = (hidden_ref[...] + moe).astype(BF16)


def body(
    residual_in,
    attn_gain,
    w_query,
    w_keyval,
    query_gain,
    key_gain,
    w_out,
    ffn_gain,
    w_gate,
    w_up,
    w_down,
    key_cache,
    value_cache,
    prefix_lens,
    accepted,
    accept_path,
    parents,
    slot_kinds,
    expert_ids,
    gate_probs,
):
    devices = lax.axis_size("tensor")
    chips = devices // 2
    new, width = residual_in.shape
    head = query_gain.shape[0]
    kv_heads = key_cache.shape[2] // head
    q_width = w_query.shape[1]
    new_width = w_keyval.shape[0]
    all_tokens, top = expert_ids.shape
    tokens = chips * new
    per = new * top // EXPERTS
    path_len = accept_path.shape[1]
    rows = 2 * chips * per
    assert key_cache.shape[0] == 1 and w_gate.shape[0] == 1
    assert devices & (devices - 1) == 0
    vmem, smem, hbm, anywhere = pltpu.VMEM, pltpu.SMEM, pltpu.HBM, pl.ANY

    blocks = exchange([residual_in] * chips)
    wq_sib = hop(w_query, 1)
    wkv_sib = hop(w_keyval, 1)

    freq = ROPE_BASE ** (-2.0 * np.arange(head // 2) / head)
    freq = jnp.asarray(np.concatenate([freq, freq])[None, :], F32)
    span = -(-(new + 16 + window_rows(path_len)) // 128) * 128
    weights = [attn_gain[None, :], w_query, w_keyval]
    keys, values, mask, rot, gain, wq, wkv = call(
        functools.partial(prep_kernel, path_len, len(weights)),
        "prep",
        [
            in_vmem((kv_heads, span, head), BF16),
            in_vmem((kv_heads, span, head), BF16),
            in_vmem((new, span), F32),
            in_vmem((4, new, head), F32),
        ]
        + [in_vmem(w.shape, w.dtype) for w in weights],
        [
            (key_cache, hbm),
            (value_cache, hbm),
            (prefix_lens, smem),
            (accepted, smem),
            (slot_kinds, smem),
            (accept_path, hbm),
            (parents, hbm),
            (freq, hbm),
            (query_gain[None, :], hbm),
            (key_gain[None, :], hbm),
        ]
        + [(w, hbm) for w in weights],
        [
            pltpu.SMEM((1, path_len), jnp.int32),
            pltpu.VMEM((1, new), jnp.int32),
            pltpu.VMEM((1, head), F32),
            pltpu.VMEM((1, head), F32),
            pltpu.VMEM((1, head), F32),
            pltpu.SemaphoreType.DMA((5,)),
            pltpu.SemaphoreType.DMA((2, kv_heads, 2)),
            pltpu.SemaphoreType.DMA((len(weights),)),
        ],
        limit=16,
        moved=4 * span * kv_heads * head * 2,
    )

    projected = call(
        functools.partial(project_kernel, chips),
        "project",
        [in_vmem((new, 2 * (q_width + new_width)), BF16)] * chips,
        [(block, vmem) for block in blocks]
        + [(w, vmem) for w in (gain, wq, wkv, wq_sib, wkv_sib)],
        limit=16,
        flops=4 * tokens * width * (q_width + new_width),
        moved=4 * width * (q_width + new_width),
    )
    got = exchange(projected)

    weights = [ffn_gain[None, :], w_out, w_down]
    pick, combine, weight, ffn, wo, wd = call(
        functools.partial(route_kernel, per, new, len(weights)),
        "route",
        [
            in_vmem((chips * rows, tokens), F32),
            in_vmem((new, devices * per), F32),
            in_vmem((rows, 128), F32),
        ]
        + [in_vmem(w.shape, w.dtype) for w in weights],
        [(projected[0], anywhere), (expert_ids.T, hbm), (gate_probs.T, hbm)]
        + [(w, hbm) for w in weights],
        [
            pltpu.VMEM((top, all_tokens), jnp.int32),
            pltpu.VMEM((top, all_tokens), F32),
            pltpu.VMEM((devices, tokens), F32),
            pltpu.VMEM((devices, tokens), F32),
            pltpu.VMEM((devices * per, tokens), F32),
            pltpu.SemaphoreType.DMA((2 + len(weights),)),
        ],
        limit=16,
        moved=4 * width * (q_width + w_down.shape[1]),
    )
    kv_ready = []
    if new_width != head:
        pieces = [None] * devices
        for rel in range(devices):
            left = 2 * q_width + (rel % 2) * new_width
            pieces[step(rel // 2) ^ (rel % 2)] = got[rel // 2][:, left : left + new_width]
        pieces = jnp.stack(pieces)[lax.axis_index("tensor") ^ jnp.arange(devices)]
        pieces = pieces.transpose(1, 0, 2).reshape(new, 2 * kv_heads, head)
        kv_ready = [(pieces.transpose(1, 0, 2), vmem)]
    *attended, wo = call(
        functools.partial(attend_kernel, chips, q_width, bool(kv_ready)),
        "attend",
        [in_vmem((new, 2 * q_width), BF16)] * chips + [in_vmem(wo.shape, wo.dtype)],
        [(block, vmem) for block in got]
        + kv_ready
        + [(keys, vmem), (values, vmem), (mask, vmem), (rot, vmem)]
        + [(wo, vmem)],
        [] if kv_ready else [pltpu.VMEM((devices, new, head), BF16)],
        limit=16,
        same={chips + len(kv_ready) + 4: chips},
        flops=8 * new * chips * q_width * span,
        moved=4 * span * kv_heads * head,
    )
    wo_sib = hop(wo, 1)
    heads = exchange(attended)
    picked, wg, wu = call(
        functools.partial(select_kernel, chips),
        "select",
        [in_vmem((rows, width), F32)] + [in_vmem(w.shape, w.dtype) for w in (w_gate, w_up)],
        [(block, vmem) for block in blocks]
        + [(pick, vmem), (attended[0], anywhere), (w_gate, hbm), (w_up, hbm)],
        [pltpu.SemaphoreType.DMA((2,))],
        limit=8,
        flops=2 * rows * width * tokens,
        moved=8 * width * w_gate.shape[1],
    )

    def spread(name, each, more):
        return call(
            functools.partial(spread_kernel, chips, name == "experts"),
            name,
            [in_vmem((each, width), BF16)] * chips,
            [(block, vmem) for block in heads] + [(wo, vmem), (wo_sib, vmem)] + more,
            limit=16,
            flops=4 * chips * each * width * q_width,
            moved=4 * q_width * width,
        )

    partial = spread("experts", rows, [(pick, vmem), (wg, anywhere)])
    for_experts = exchange(partial)
    partial = spread("slots", new, [(partial[0], anywhere)])
    for_slots = [partial[0]] + [hop(partial[j], step(j)) for j in range(2, chips)]

    own, other = call(
        functools.partial(rows_kernel, chips),
        "rows",
        [in_vmem((rows // 2, width), BF16)] * 2,
        [(block, vmem) for block in for_experts]
        + [(picked, vmem), (ffn, vmem), (partial[0], anywhere)],
        limit=8,
        moved=2 * chips * rows * width,
    )
    own_out, other_out = call(
        expert_kernel,
        "expert",
        [in_vmem((rows // 2, width), F32), in_vmem((rows // 2, width), BF16)],
        [(own, vmem), (hop(other, 1), vmem), (wg, vmem), (wu, vmem), (wd, vmem)],
        limit=16,
        flops=6 * rows * width * w_gate.shape[1],
        moved=6 * width * w_gate.shape[1],
    )
    results = call(
        functools.partial(pack_kernel, chips, per),
        "pack",
        [in_vmem((2 * per + (new if j == 1 else 0), width), BF16) for j in range(chips)],
        [(own_out, vmem), (hop(other_out, 1), vmem), (weight, vmem), (partial[1], vmem)],
        limit=8,
        moved=4 * rows * width,
    )
    returned = exchange(results)
    hidden = call(
        hidden_kernel,
        "hidden",
        [in_vmem((new, width), F32)],
        [(block, vmem) for block in for_slots] + [(residual_in, vmem)],
        limit=8,
        moved=2 * chips * new * width,
    )[0]
    return call(
        functools.partial(combine_kernel, chips),
        "combine",
        [jax.ShapeDtypeStruct((new, width), BF16)],
        [(hidden, vmem), (combine, vmem)] + [(block, vmem) for block in returned],
        limit=8,
        moved=6 * new * width,
    )[0]


def solution(mesh):
    in_specs = (
        P(("group", "tensor"), None),
        P(),
        P(None, "tensor"),
        P("tensor", None),
        P(),
        P(),
        P("tensor", None),
        P(),
        P("tensor", None, None),
        P("tensor", None, None),
        P("tensor", None, None),
        P(("group", "tensor"), None, None),
        P(("group", "tensor"), None, None),
        P(("group", "tensor")),
        P(("group", "tensor")),
        P(("group", "tensor"), None),
        P(("group", "tensor"), None),
        P(("group", "tensor")),
        P("group", None),
        P("group", None),
    )
    out_specs = P(("group", "tensor"), None)
    return jax.shard_map(body, mesh=mesh, in_specs=in_specs, out_specs=out_specs, check_vma=False)
```
